32 devices in a mesh: dp: 8 (over z, y), tensor: 4 (over x, core).
Axes of the slice: x: 2, y: 2, z: 4, core: 2. Of those that a mesh axis runs over, the one named last changes fastest.
Arguments:
- tokens: bfloat16 [12288, 1024], P(('dp', 'tensor')), may hold values from -6 to 6
- gain_attn: bfloat16 [1024], replicated, may hold values from 0.099609375 to 1.8984375
- w_query: bfloat16 [1024, 1024], P(None, 'tensor'), may hold values from -0.1875 to 0.1875
- w_key: bfloat16 [1024, 1024], P(None, 'tensor'), may hold values from -0.1875 to 0.1875
- w_value: bfloat16 [1024, 1024], P(None, 'tensor'), may hold values from -0.1875 to 0.1875
- w_out: bfloat16 [1024, 1024], P('tensor'), may hold values from -1 to 1
- gain_mlp: bfloat16 [1024], replicated, may hold values from 0.099609375 to 1.8984375
- w_gate: bfloat16 [1024, 2816], P(None, 'tensor'), may hold values from -0.1875 to 0.1875
- w_up: bfloat16 [1024, 2816], P(None, 'tensor'), may hold values from -0.1875 to 0.1875
- w_down: bfloat16 [2816, 1024], P('tensor'), may hold values from -0.109375 to 0.109375
- doc_lens: int32 [8, 2], P('dp'), may hold values from 0 to 1536, as said below
- pad_mask: int32 [12288], P(('dp', 'tensor')), may hold values 0 or 1
- cotangent: bfloat16 [12288, 1024], P(('dp', 'tensor')), may hold values from -6 to 6
Outputs:
- output: bfloat16 [12288, 1024], P(('dp', 'tensor'))
- grad_tokens: bfloat16 [12288, 1024], P(('dp', 'tensor'))
- grad_gain_attn: float32 [1024], replicated
- grad_query: float32 [1024, 1024], P(None, 'tensor')
- grad_key: float32 [1024, 1024], P(None, 'tensor')
- grad_value: float32 [1024, 1024], P(None, 'tensor')
- grad_out: float32 [1024, 1024], P('tensor')
- grad_gain_mlp: float32 [1024], replicated
- grad_gate: float32 [1024, 2816], P(None, 'tensor')
- grad_up: float32 [1024, 2816], P(None, 'tensor')
- grad_down: float32 [2816, 1024], P('tensor')
The draws below stay inside these ranges and needn't reach their ends.
Inputs may be any that keep to these rules, and one draw needn't show every extreme that they name: `doc_lens`: each row holds the length of one sequence, of 1344 to 1536 patches, and then the length of the padding tail that fills the group's 1536 patches.
All inputs are finite; a program needn't handle non-finite values. No bound on the sum of `pad_mask` on one device may be relied on, other than what follows from the above.
Results may differ from the reference program's by a relative error of at most 0.02.
Values may be sent and summed in bfloat16 or wider, within the bound.
No kernel may reach another device: no remote copies, remote signals or barrier semaphores. Data moves between devices by JAX's collectives and lax.ppermute only.
A program may use at most 128 MiB of HBM per device.

```python
import math
import jax
import jax.numpy as jnp
from jax import lax

D = 1024
HEADS = 16
HEAD_DIM = 64
FF = 2816
TOK_DEV = 384
GROUP_TOK = 1536
TOKENS = 12288
N_DP = 8


def draw_doc_lens(key, part):
    key = jax.random.fold_in(key, 11)
    key_len, key_row = jax.random.split(key)
    shortest = GROUP_TOK - TOK_DEV // 2
    first = jax.random.randint(key_len, (N_DP,), shortest, GROUP_TOK + 1, dtype=jnp.int32)
    full_row = jax.random.randint(key_row, (), 0, N_DP, dtype=jnp.int32)
    rows = lax.iota(jnp.int32, N_DP)
    first = jnp.where(rows == full_row, jnp.int32(GROUP_TOK), first)
    tail = jnp.int32(GROUP_TOK) - first
    return jnp.stack([first, tail], axis=1).astype(jnp.int32)


def touch_ends(array, key, low, largest):
    index_at = [jax.random.randint(jax.random.fold_in(key, axis), (), 0, length) for axis, length in enumerate(array.shape)]
    longest = array.shape.index(max(array.shape))
    neighbour = index_at[:longest] + [(index_at[longest] + 1) % array.shape[longest]] + index_at[longest + 1:]
    return array.at[tuple(index_at)].set(low).at[tuple(neighbour)].set(largest)


def level_of(key, dims, shards, smallest, top_value):
    factor_of, own = 1.0, jax.random.fold_in(key, 6)
    for position, blocks in shards:
        draws = jnp.exp(jax.random.uniform(jax.random.fold_in(own, position), (blocks,), jnp.float32, smallest / len(shards), top_value / len(shards)))
        factor_of = factor_of * jnp.repeat(draws, dims[position] // blocks).reshape([-1 if axis == position else 1 for axis in range(len(dims))])
    return factor_of


def centred(key, dims, deviation, most, pieces=(), kind=jnp.bfloat16):
    drawn = jax.random.normal(key, dims, jnp.float32) * deviation
    if len(pieces) > 0:
        drawn = level_of(key, dims, pieces, -0.22, 0.18) * drawn
    return jnp.clip(drawn, min=-most, max=most).astype(kind)


def setup_inputs(seed: int = 0) -> dict:
    keys = jax.random.split(jax.random.key(seed), 14)
    return {
        "tokens": centred(keys[0], (TOKENS, D), 1.0, 6.0, ((0, 32),)),
        "gain_attn": jnp.clip(1.0 + 0.18 * jax.random.normal(keys[1], (D,), jnp.float32), 0.099609375, 1.8984375).astype(jnp.bfloat16),
        "w_query": centred(keys[2], (D, D), D ** -0.5, 0.1875, ((1, 4),)),
        "w_key": centred(keys[3], (D, D), D ** -0.5, 0.1875, ((1, 4),)),
        "w_value": centred(keys[4], (D, D), D ** -0.5, 0.1875, ((1, 4),)),
        "w_out": centred(keys[5], (D, D), (D // 32) ** -0.5, 1.0, ((0, 4),)),
        "gain_mlp": jnp.clip(1.0 + 0.18 * jax.random.normal(keys[6], (D,), jnp.float32), 0.099609375, 1.8984375).astype(jnp.bfloat16),
        "w_gate": centred(keys[7], (D, FF), D ** -0.5, 0.1875, ((1, 4),)),
        "w_up": centred(keys[8], (D, FF), D ** -0.5, 0.1875, ((1, 4),)),
        "w_down": centred(keys[9], (FF, D), FF ** -0.5, 0.109375, ((0, 4),)),
        "doc_lens": draw_doc_lens(jax.random.fold_in(keys[13], 71), 0),
        "pad_mask": touch_ends((jax.random.randint(keys[11], (TOKENS,), 0, 8) < 7).astype(jnp.int32), jax.random.fold_in(keys[11], 1), 0, 1),
        "cotangent": centred(keys[12], (TOKENS, D), 1.0, 6.0, ((0, 32),)),
    }


eps = 1e-05
precise = lax.Precision.HIGHEST

@jax.custom_vjp
def low(v):
    return lax.optimization_barrier(v.astype(jnp.bfloat16)).astype(jnp.float32)

@jax.custom_vjp
def low_back(v):
    return v

def low_keep(v):
    return (low(v), None)

def low_pass(kept, grad):
    return (grad,)

def back_keep(v):
    return (v, None)

def back_low(kept, grad):
    return (low(grad),)
low.defvjp(low_keep, low_pass)
low_back.defvjp(back_keep, back_low)

def doc_numbers(doc_lens, length):
    doc_ends = jnp.cumsum(doc_lens.astype(jnp.int32))
    positions = lax.iota(jnp.int32, length)
    return lax.optimization_barrier(jnp.sum((positions[:, None] >= doc_ends[None, :]).astype(jnp.int32), axis=1))

def allowed_block(offset, block_rows, doc_ids, keep_all):
    length = doc_ids.shape[0]
    key_pos = lax.iota(jnp.int32, length)
    query_pos = offset + lax.iota(jnp.int32, block_rows)
    query_doc = lax.dynamic_slice_in_dim(doc_ids, offset, block_rows, 0)
    same_doc = query_doc[:, None] == doc_ids[None, :]
    causal = key_pos[None, :] <= query_pos[:, None]
    visible = (keep_all[None, :] == 1) | (key_pos[None, :] == query_pos[:, None])
    return same_doc & causal & visible

def group_layer(inputs, gain_one, wq_f, wk_f, wv_f, wo_f, gain_two, wg_f, wu_f, wd_f, doc_lens, keep_all):
    length = inputs.shape[0]
    doc_ids = doc_numbers(doc_lens, length)
    inv_one = lax.rsqrt(lax.optimization_barrier(jnp.mean(inputs * inputs, axis=-1, keepdims=True)) + eps)
    normed = low(inputs * inv_one * gain_one)
    shaped = (length, HEADS, HEAD_DIM)
    queries = low_back(low(jnp.dot(normed, wq_f, precision=precise))).reshape(shaped)
    key_all = low_back(low(jnp.dot(normed, wk_f, precision=precise))).reshape(shaped)
    value_all = low_back(low(jnp.dot(normed, wv_f, precision=precise))).reshape(shaped)
    block_rows = min(512, length)
    factor = 1.0 / math.sqrt(HEAD_DIM)

    def one_block(offset):
        q_block = lax.dynamic_slice_in_dim(queries, offset, block_rows, 0)
        raw = low_back(jnp.einsum('qhd,khd->hqk', q_block, key_all, precision=precise))
        allowed = allowed_block(offset, block_rows, doc_ids, keep_all)
        scores = jnp.where(allowed[None], raw * factor, -1e+30)
        row_max = lax.optimization_barrier(jnp.max(scores, axis=-1, keepdims=True))
        powers = jnp.exp(scores - row_max)
        row_sum = lax.optimization_barrier(jnp.sum(powers, axis=-1, keepdims=True))
        weights = low(powers / row_sum)
        return jnp.einsum('hqk,khd->qhd', weights, value_all, precision=precise)
    offsets = lax.iota(jnp.int32, length // block_rows) * block_rows
    attended = lax.map(jax.checkpoint(one_block), offsets).reshape(length, HEADS * HEAD_DIM)
    attended = low_back(low(attended))
    hidden_sum = inputs + low_back(jnp.dot(attended, wo_f, precision=precise))
    inv_two = lax.rsqrt(lax.optimization_barrier(jnp.mean(hidden_sum * hidden_sum, axis=-1, keepdims=True)) + eps)
    normed_two = low(hidden_sum * inv_two * gain_two)
    gate_pre = low_back(jnp.dot(normed_two, wg_f, precision=precise))
    up_pre = low_back(jnp.dot(normed_two, wu_f, precision=precise))
    activ = low_back(low(jax.nn.silu(gate_pre) * up_pre))
    return hidden_sum + low_back(jnp.dot(activ, wd_f, precision=precise))

def reference(tokens, gain_attn, w_query, w_key, w_value, w_out, gain_mlp, w_gate, w_up, w_down, doc_lens, pad_mask, cotangent):
    inputs = tokens.astype(jnp.float32).reshape(N_DP, GROUP_TOK, D)
    keeps = pad_mask.reshape(N_DP, GROUP_TOK)
    pulls = cotangent.astype(jnp.float32).reshape(N_DP, GROUP_TOK, D)
    params = (gain_attn, w_query, w_key, w_value, w_out, gain_mlp, w_gate, w_up, w_down)
    params = tuple((item_w.astype(jnp.float32) for item_w in params))
    layer_saved = jax.checkpoint(group_layer)

    def whole(inputs_all, gain_one, wq_f, wk_f, wv_f, wo_f, gain_two, wg_f, wu_f, wd_f):

        def step(running, packet):
            group_in, group_lens, group_keep = packet
            result = layer_saved(group_in, gain_one, wq_f, wk_f, wv_f, wo_f, gain_two, wg_f, wu_f, wd_f, group_lens, group_keep)
            return (running, result)
        unused, outputs = lax.scan(step, jnp.zeros((), jnp.float32), (inputs_all, doc_lens, keeps))
        return outputs
    outputs, pull_back = jax.vjp(whole, inputs, *params)
    grads = pull_back(pulls)
    output = outputs.reshape(TOKENS, D).astype(jnp.bfloat16)
    grad_tokens = grads[0].reshape(TOKENS, D).astype(jnp.bfloat16)
    return (output, grad_tokens, grads[1], grads[2], grads[3], grads[4], grads[5], grads[6], grads[7], grads[8], grads[9])
```

```python
import functools

import jax
import jax.numpy as jnp
from jax import lax
from jax.experimental import pallas as pl
from jax.experimental.pallas import tpu as pltpu
from jax.sharding import PartitionSpec as P

HEAD_DIM = 64
EPS = 1e-05
NEG = -1e30
BLOCK = 256
INNER = 8
bf16 = jnp.bfloat16
f32 = jnp.float32
MIB = 2**20


def dot(a, b, ca=1, cb=0):
    return lax.dot_general(a, b, (((ca,), (cb,)), ((), ())), preferred_element_type=f32)


def params(limit_mib):
    return pltpu.CompilerParams(vmem_limit_bytes=limit_mib * MIB)


def cost(gflop, mbytes):
    return pl.CostEstimate(
        flops=int(gflop * 1e9), bytes_accessed=int(mbytes * 1e6), transcendentals=0
    )


def sds(shape, dtype):
    return jax.ShapeDtypeStruct(shape, dtype)


SMEM = pl.BlockSpec(memory_space=pltpu.SMEM)
VMEM = pl.BlockSpec(memory_space=pltpu.VMEM)
ANY = pl.BlockSpec(memory_space=pl.ANY)

def region(shape):
    return lax.broadcasted_iota(jnp.int32, shape, 1) // HEAD_DIM


def lanes(shape):
    return lax.broadcasted_iota(jnp.int32, shape, 1)


def attn_fwd_kernel(q_ref, k_ref, v_ref, aq_ref, ak_ref, cols_ref, rows_ref, o_ref, l_ref, qm, km, *, length):
    zero = jnp.zeros((), bf16)
    reg = region((length, 256))
    for h in range(4):
        following = (h + 1) % 4
        qm[h] = jnp.where(reg == h, q_ref[...], jnp.where(reg == following, aq_ref[...], zero))
        km[h] = jnp.where(reg == h, k_ref[...], ak_ref[...])
    reg_b = region((BLOCK, 256))
    ri = lax.broadcasted_iota(jnp.int32, (BLOCK, BLOCK), 0)
    ci = lax.broadcasted_iota(jnp.int32, (BLOCK, BLOCK), 1)
    ln = lanes((BLOCK, 128))
    for i in range(length // BLOCK):
        r0 = i * BLOCK
        here = slice(r0, r0 + BLOCK)
        same = cols_ref[here, 0:1] == rows_ref[1:2, here]
        seen = (ri == ci) | ((ci < ri) & (rows_ref[0:1, here] > 0.5) & same)
        bias = jnp.where(seen, 0.0, NEG).astype(f32)
        o_acc = jnp.zeros((BLOCK, 256), f32)
        l_acc = jnp.zeros((BLOCK, 128), f32)
        for h in range(4):
            qh = qm[h, here, :]
            plain = jnp.where(reg_b == h, qh, zero)
            s_diag = dot(plain, k_ref[here, :], 1, 1) + bias
            top = jnp.max(s_diag, axis=1, keepdims=True)
            if i > 0:
                s_left = dot(qh, km[h, 0:r0, :], 1, 1)
                top = jnp.maximum(top, jnp.max(s_left, axis=1, keepdims=True))
            p_diag = jnp.exp(s_diag - top)
            total = jnp.sum(p_diag, axis=1, keepdims=True)
            acc = dot(p_diag.astype(bf16), v_ref[here, :])
            if i > 0:
                p_left = jnp.exp(s_left - top)
                total = total + jnp.sum(p_left, axis=1, keepdims=True)
                acc = acc + dot(p_left.astype(bf16), v_ref[0:r0, :])
            o_acc = jnp.where(reg_b == h, acc * (1.0 / total), o_acc)
            l_acc = jnp.where(ln == h, top + jnp.log(total), l_acc)
        o_ref[here, :] = o_acc.astype(bf16)
        l_ref[here, :] = l_acc


def attend(q, k, v, masks):
    length = q.shape[0]
    return pl.pallas_call(
        functools.partial(attn_fwd_kernel, length=length),
        out_shape=(sds((length, 256), bf16), sds((length, 128), f32)),
        scratch_shapes=[pltpu.VMEM((4, length, 256), bf16)] * 2,
        compiler_params=params(56),
        cost_estimate=cost(12, 6),
        name="attend",
    )(q, k, v, *masks)


def split3(value):
    high = value.astype(bf16)
    rest = value - high.astype(f32)
    middle = rest.astype(bf16)
    return high, middle, (rest - middle.astype(f32)).astype(bf16)


def attn_bwd_kernel(
    t_ref, q_ref, k_ref, v_ref, d0, d1, d2, d3, o_ref, l_ref, aq_ref, ak_ref, cols_ref, rows_ref,
    dq_ref, dk_ref, dv_ref, qm, km, dm, vm, do_ref, dq_acc, *, length,
):
    zero = jnp.zeros((), bf16)
    minus = -jnp.ones((), bf16)
    part = length // 4
    for k, piece in enumerate((d0, d1, d2, d3)):
        do_ref[pl.ds(pl.multiple_of((t_ref[0] ^ k) * part, part), part), :] = piece[...]
    reg = region((length, 256))
    ln = lanes((length, 256))
    both = do_ref[...].astype(f32) * o_ref[...].astype(f32)
    for h in range(4):
        following = (h + 1) % 4
        a = following * HEAD_DIM
        high, middle, low = split3(l_ref[:, h : h + 1])
        extra = jnp.where(reg == following, aq_ref[...], zero)
        extra = jnp.where(ln == a + 3, high, jnp.where(ln == a + 4, middle, jnp.where(ln == a + 5, low, extra)))
        qm[h] = jnp.where(reg == h, q_ref[...], extra)
        km[h] = jnp.where(reg == h, k_ref[...], ak_ref[...])
        high, middle, low = split3(jnp.sum(jnp.where(reg == h, both, 0.0), axis=1, keepdims=True))
        extra = jnp.where(ln == a, high, jnp.where(ln == a + 1, middle, jnp.where(ln == a + 2, low, zero)))
        dm[h] = jnp.where(reg == h, do_ref[...], extra)
        vm[h] = jnp.where(reg == h, v_ref[...], jnp.where((ln >= a) & (ln < a + 3), minus, zero))
    reg_b = region((BLOCK, 256))
    ln_b = lanes((BLOCK, 256))
    ri = lax.broadcasted_iota(jnp.int32, (BLOCK, BLOCK), 0)
    ci = lax.broadcasted_iota(jnp.int32, (BLOCK, BLOCK), 1)
    dq_acc[...] = jnp.zeros((length, 256), f32)
    for j in range(length // BLOCK):
        c0 = j * BLOCK
        here = slice(c0, c0 + BLOCK)
        below = slice(c0 + BLOCK, length)
        same = cols_ref[here, 0:1] == rows_ref[1:2, here]
        seen = (ri == ci) | ((ri < ci) & (cols_ref[here, 1:2] > 0.5) & same)
        bias = jnp.where(seen, 0.0, NEG).astype(f32)
        dk = jnp.zeros((BLOCK, 256), f32)
        dv = jnp.zeros((BLOCK, 256), f32)
        for h in range(4):
            a = ((h + 1) % 4) * HEAD_DIM
            plain = jnp.where(
                reg_b == h, k_ref[here, :], jnp.where((ln_b >= a + 3) & (ln_b < a + 6), minus, zero)
            )
            p = jnp.exp(dot(plain, qm[h, here, :], 1, 1) + bias)
            ds = (p * dot(vm[h, here, :], dm[h, here, :], 1, 1)).astype(bf16)
            dk_h = dot(ds, q_ref[here, :])
            dv_h = dot(p.astype(bf16), do_ref[here, :])
            dq_acc[here, :] += jnp.where(reg_b == h, dot(ds, k_ref[here, :], 0, 0), 0.0)
            if c0 + BLOCK < length:
                p = jnp.exp(dot(km[h, here, :], qm[h, below, :], 1, 1))
                ds = (p * dot(vm[h, here, :], dm[h, below, :], 1, 1)).astype(bf16)
                dk_h = dk_h + dot(ds, q_ref[below, :])
                dv_h = dv_h + dot(p.astype(bf16), do_ref[below, :])
                pulled = dot(ds, k_ref[here, :], 0, 0)
                dq_acc[below, :] += jnp.where(region(pulled.shape) == h, pulled, 0.0)
            dk = jnp.where(reg_b == h, dk_h, dk)
            dv = jnp.where(reg_b == h, dv_h, dv)
        dk_ref[here, :] = dk.astype(bf16)
        dv_ref[here, :] = dv.astype(bf16)
    dq_ref[...] = (dq_acc[...] * 0.125).astype(bf16)


def attend_back(t, q, k, v, do_parts, o, log_norm, masks):
    length = q.shape[0]
    return pl.pallas_call(
        functools.partial(attn_bwd_kernel, length=length),
        out_shape=(sds((length, 256), bf16),) * 3,
        in_specs=[SMEM] + [VMEM] * 13,
        scratch_shapes=[pltpu.VMEM((4, length, 256), bf16)] * 4
        + [pltpu.VMEM((length, 256), bf16), pltpu.VMEM((length, 256), f32)],
        compiler_params=params(60),
        cost_estimate=cost(25, 6),
        name="attend_back",
    )(t, q, k, v, *do_parts, o, log_norm, *masks)

def rms_rows(values):
    return lax.rsqrt(jnp.mean(values * values, axis=-1, keepdims=True) + EPS)


def project_kernel(t_ref, x0, x1, x2, x3, gain_ref, wq, wk, wv, xn_ref, q_ref, k_ref, v_ref):
    part = x0.shape[0]
    for k, piece in enumerate((x0, x1, x2, x3)):
        rows = pl.ds(pl.multiple_of((t_ref[0] ^ k) * part, part), part)
        x = piece[...].astype(f32)
        xn = (x * rms_rows(x) * gain_ref[...]).astype(bf16)
        xn_ref[rows, :] = xn
        q_ref[rows, :] = (dot(xn, wq[...]).astype(bf16).astype(f32) * 0.125).astype(bf16)
        k_ref[rows, :] = dot(xn, wk[...]).astype(bf16)
        v_ref[rows, :] = dot(xn, wv[...]).astype(bf16)


def project(t, x_parts, gain, wq, wk, wv):
    part, width = x_parts[0].shape
    length, cols = 4 * part, wq.shape[1]
    return pl.pallas_call(
        project_kernel,
        out_shape=(sds((length, width), bf16),) + (sds((length, cols), bf16),) * 3,
        in_specs=[SMEM] + [VMEM] * 8,
        compiler_params=params(40),
        cost_estimate=cost(4, 12),
        name="project",
    )(t, *x_parts, gain, wq, wk, wv)


def mlp_kernel(
    t_ref, o0, o1, o2, o3, w0, w1, w2, w3, xa, xb, ya, yb, gain_ref, wg, wu, wd,
    hn_ref, act_ref, dgate_ref, dup_ref, fa, fb, ba, bb, gsum_ref, *own, ks,
):
    part = xa.shape[0]
    gsum = jnp.zeros(gsum_ref.shape, f32)
    for i, (k, x, dy, ffn, dhn) in enumerate(zip(ks, (xa, xb), (ya, yb), (fa, fb), (ba, bb))):
        rows = pl.ds(pl.multiple_of((t_ref[0] ^ k) * part, part), part)
        here = slice(i * part, (i + 1) * part)
        hidden = x[...].astype(f32)
        for o, w in ((o0, w0), (o1, w1), (o2, w2), (o3, w3)):
            hidden = hidden + dot(o[rows, :], w[...])
        if k == 0:
            own[0][...] = hidden
        hn = (hidden * rms_rows(hidden) * gain_ref[...]).astype(bf16)
        hn_ref[here, :] = hn
        gate = dot(hn, wg[...])
        up = dot(hn, wu[...])
        sig = 1.0 / (1.0 + jnp.exp(-gate))
        silu = gate * sig
        act = (silu * up).astype(bf16)
        act_ref[here, :] = act
        dact = dot(dy[...], wd[...], 1, 1).astype(bf16).astype(f32)
        dgate = (dact * up * sig * (1.0 + gate * (1.0 - sig))).astype(bf16)
        dup = (dact * silu).astype(bf16)
        dgate_ref[here, :] = dgate
        dup_ref[here, :] = dup
        back = dot(dgate, wg[...], 1, 1) + dot(dup, wu[...], 1, 1)
        dhn[...] = back.astype(bf16)
        gsum = gsum + jnp.sum(back * hn.astype(f32), axis=0, keepdims=True)
        ffn[...] = dot(act, wd[...]).astype(bf16)
    gsum_ref[...] = gsum


def mlp(t, o_parts, w_parts, x_pair, dy_pair, gain, wg, wu, wd, ks):
    part, width = x_pair[0].shape
    hidden = wg.shape[1]
    out = (
        [sds((2 * part, width), bf16)]
        + [sds((2 * part, hidden), bf16)] * 3
        + [sds((part, width), bf16)] * 4
        + [sds((1, width), f32)]
    )
    if 0 in ks:
        out.append(sds((part, width), f32))
    return pl.pallas_call(
        functools.partial(mlp_kernel, ks=ks),
        out_shape=tuple(out),
        in_specs=[SMEM] + [VMEM] * 16,
        compiler_params=params(56),
        cost_estimate=cost(10, 20),
        name="mlp",
    )(t, *o_parts, *w_parts, *x_pair, *dy_pair, gain, wg, wu, wd)


def mlp_grads_kernel(hn_a, hn_b, act_a, act_b, dg_a, dg_b, du_a, du_b, y0, y1, y2, y3, out_ref, left, dy_a, dy_b):
    width = hn_a.shape[1]
    hidden = act_a.shape[1]
    half = hidden // 2
    last = hidden // 128 * 128
    part = y0.shape[0]
    for ref, first, second in ((dy_a, y0, y1), (dy_b, y2, y3)):
        ref[:part, :] = first[...]
        ref[part:, :] = second[...]
    rows_up = 64 * (2 * hidden // 128)

    def store(base, block, value):
        for i in range(value.shape[0] // 128):
            for way in range(2):
                at = 128 * i + 64 * way
                out_ref[base + i, way, 64 * block : 64 * block + 64, :] = value[at : at + 64, :].astype(bf16)

    for base in range(0, width // 128, 4):
        cols = slice(128 * base, 128 * base + 512)
        left[0] = hn_a[:, cols].T
        left[1] = hn_b[:, cols].T
        tails = []
        for which, (one, two) in enumerate(((dg_a, dg_b), (du_a, du_b))):
            for c in range(0, last, 256):
                got = slice(c, min(c + 256, hidden))
                grad = dot(left[0], one[:, got]) + dot(left[1], two[:, got])
                for b in range(min(c + 256, last) // 128 - c // 128):
                    store(base, which * (last // 128) + c // 128 + b, grad[:, 128 * b : 128 * b + 128])
                if c + 256 > last:
                    tails.append(grad[:, last - c :])
        store(base, 2 * (last // 128), jnp.concatenate(tails, axis=1))
    for c in range(0, width, 256):
        grad = dot(act_a[...], dy_a[:, c : c + 256], 0, 0) + dot(act_b[...], dy_b[:, c : c + 256], 0, 0)
        for b in range(2):
            for way in range(2):
                out_ref[c // 128 + b, way, rows_up:, :] = grad[
                    half * way : half * way + half, 128 * b : 128 * b + 128
                ].astype(bf16)


def mlp_grads(hn, act, dgate, dup, dy_parts):
    width, hidden = hn[0].shape[1], act[0].shape[1]
    length = 2 * hn[0].shape[0]
    rows = 64 * (2 * hidden // 128) + hidden // 2
    return pl.pallas_call(
        mlp_grads_kernel,
        out_shape=sds((INNER, 2, rows, 128), bf16),
        scratch_shapes=[
            pltpu.VMEM((2, 512, length // 2), bf16),
            pltpu.VMEM((length // 2, width), bf16),
            pltpu.VMEM((length // 2, width), bf16),
        ],
        compiler_params=params(56),
        cost_estimate=cost(10, 18),
        name="mlp_grads",
    )(*hn, *act, *dgate, *dup, *dy_parts)


def mlp_unpack_kernel(idx, *refs):
    pieces, (gate_ref, up_ref, down_ref), (stage_g, stage_u, stage_d, sems) = refs[:16], refs[16:19], refs[19:]
    hidden = gate_ref.shape[1]
    last, half = hidden // 128 * 128, hidden // 2
    n = last // 128
    copies = []
    for way in range(2):
        for j in range(INNER):
            p, s = pieces[way * INNER + j], way * INNER + j
            for b in range(n):
                stage_g[s, :, 128 * b : 128 * b + 128] = p[64 * b : 64 * b + 64, :].astype(f32)
                stage_u[s, :, 128 * b : 128 * b + 128] = p[64 * (n + b) : 64 * (n + b) + 64, :].astype(f32)
            tail = p[64 * 2 * n : 64 * 2 * n + 64, :].astype(f32)
            stage_g[s, :, last:] = tail[:, : hidden - last]
            stage_u[s, :, last:] = tail[:, hidden - last :]
            stage_d[s] = p[64 * (2 * n + 1) :, :].astype(f32)
            at = idx[s] * 128
            rows = pl.ds(pl.multiple_of(at + 64 * way, 64), 64)
            for c, (src, dst) in enumerate(
                (
                    (stage_g.at[s], gate_ref.at[rows, :]),
                    (stage_u.at[s], up_ref.at[rows, :]),
                    (stage_d.at[s], down_ref.at[pl.ds(half * way, half), pl.ds(pl.multiple_of(at, 128), 128)]),
                )
            ):
                copies.append(pltpu.make_async_copy(src, dst, sems.at[s, c]))
                copies[-1].start()
    for copy in copies:
        copy.wait()


def mlp_unpack(idx, pieces, width, hidden):
    return pl.pallas_call(
        mlp_unpack_kernel,
        out_shape=(sds((width, hidden), f32), sds((width, hidden), f32), sds((hidden, width), f32)),
        in_specs=[SMEM] + [VMEM] * 16,
        out_specs=[ANY] * 3,
        scratch_shapes=[
            pltpu.VMEM((16, 64, hidden), f32),
            pltpu.VMEM((16, 64, hidden), f32),
            pltpu.VMEM((16, hidden // 2, 128), f32),
            pltpu.SemaphoreType.DMA((16, 3)),
        ],
        compiler_params=params(40),
        cost_estimate=cost(0.1, 14),
        name="mlp_unpack",
    )(idx, *pieces)


def hidden_back_kernel(b0, b1, b2, h_ref, dy_ref, gain_ref, w0, w1, w2, w3, dh_ref, da_ref, d0, d1, d2, d3):
    dhn = b0[...].astype(f32) + b1[...].astype(f32) + b2[...].astype(f32)
    hidden = h_ref[...]
    inv = rms_rows(hidden)
    weighted = dhn * gain_ref[...]
    inner = jnp.mean(weighted * hidden, axis=-1, keepdims=True)
    dh = dy_ref[...].astype(f32) + inv * weighted - hidden * (inv * inv * inv) * inner
    dh_ref[...] = dh
    da = dh.astype(bf16)
    da_ref[...] = da
    for w, d in ((w1, d1), (w2, d2), (w3, d3), (w0, d0)):
        d[...] = dot(da, w[...], 1, 1).astype(bf16)


def hidden_back(sums, h_own, dy_own, gain, w_parts):
    part, width = h_own.shape
    return pl.pallas_call(
        hidden_back_kernel,
        out_shape=(sds((part, width), f32), sds((part, width), bf16))
        + (sds((part, w_parts[0].shape[0]), bf16),) * 4,
        compiler_params=params(40),
        cost_estimate=cost(2, 10),
        name="hidden_back",
    )(*sums, h_own, dy_own, gain, *w_parts)


def tokens_back_kernel(t_ref, dq, dk, dv, wq, wk, wv, xn, b0, b1, b2, b3, gsum_ref):
    part = b0.shape[0]
    gsum = jnp.zeros(gsum_ref.shape, f32)
    for k, out in ((3, b3), (2, b2), (1, b1), (0, b0)):
        rows = pl.ds(pl.multiple_of((t_ref[0] ^ k) * part, part), part)
        dxn = dot(dq[rows, :], wq[...], 1, 1) + dot(dk[rows, :], wk[...], 1, 1) + dot(dv[rows, :], wv[...], 1, 1)
        out[...] = dxn.astype(bf16)
        gsum = gsum + jnp.sum(dxn * xn[rows, :].astype(f32), axis=0, keepdims=True)
    gsum_ref[...] = gsum


def tokens_back(t, dq, dk, dv, wq, wk, wv, xn):
    length, width = xn.shape
    return pl.pallas_call(
        tokens_back_kernel,
        out_shape=(sds((length // 4, width), bf16),) * 4 + (sds((1, width), f32),),
        in_specs=[SMEM] + [VMEM] * 7,
        compiler_params=params(40),
        cost_estimate=cost(4, 12),
        name="tokens_back",
    )(t, dq, dk, dv, wq, wk, wv, xn)


def head_grads_kernel(t_ref, xn, dq, dk, dv, o, a0, a1, a2, a3, gains, out_ref, left, left_o):
    length, width = xn.shape
    part = a0.shape[0]
    for base in range(0, width // 128, 4):
        left[...] = xn[:, 128 * base : 128 * base + 512].T
        for m, d in enumerate((dq, dk, dv)):
            grad = dot(left[...], d[...])
            for i in range(4):
                for way in range(2):
                    at = 128 * i + 64 * way
                    for b in range(2):
                        row = 64 * (2 * m + b)
                        out_ref[base + i, way, row : row + 64, :] = grad[
                            at : at + 64, 128 * b : 128 * b + 128
                        ].astype(bf16)
    for k in range(4):
        rows = pl.ds(pl.multiple_of((t_ref[0] ^ k) * part, part), part)
        left_o[k] = o[rows, :].T
    for c in range(0, width, 256):
        cols = slice(c, c + 256)
        grad = sum(dot(left_o[k], a[:, cols]) for k, a in enumerate((a0, a1, a2, a3)))
        for b in range(2):
            for way in range(2):
                out_ref[c // 128 + b, way, 384:512, :] = grad[
                    128 * way : 128 * way + 128, 128 * b : 128 * b + 128
                ].astype(bf16)
    for i in range(width // 128):
        out_ref[i, 0, 512:, :] = gains[:, 128 * i : 128 * i + 128].astype(bf16)
        out_ref[i, 1, 512:, :] = jnp.zeros((16, 128), bf16)


def head_grads(t, xn, dq, dk, dv, o, da_parts, gains):
    length, width = xn.shape
    return pl.pallas_call(
        head_grads_kernel,
        out_shape=sds((INNER, 2, 528, 128), bf16),
        in_specs=[SMEM] + [VMEM] * 10,
        scratch_shapes=[pltpu.VMEM((512, length), bf16), pltpu.VMEM((4, 256, length // 4), bf16)],
        compiler_params=params(48),
        cost_estimate=cost(5, 12),
        name="head_grads",
    )(t, xn, dq, dk, dv, o, *da_parts, gains)


def head_unpack_kernel(idx, *refs):
    pieces, (q_ref, k_ref, v_ref, o_ref, gain_ref), (stage, stage_o, sems) = refs[:16], refs[16:21], refs[21:]
    copies = []
    for way in range(2):
        for j in range(INNER):
            s = way * INNER + j
            p = pieces[s]
            at = idx[s] * 128
            for m in range(3):
                for b in range(2):
                    row = 64 * (2 * m + b)
                    stage[s, m, :, 128 * b : 128 * b + 128] = p[row : row + 64, :].astype(f32)
            stage_o[s] = p[384:512, :].astype(f32)
            lane_at = pl.ds(pl.multiple_of(at, 128), 128)
            if way == 0:
                gain_ref[:, lane_at] = p[512:528, :].astype(f32)
            rows = pl.ds(pl.multiple_of(at + 64 * way, 64), 64)
            for c, (src, dst) in enumerate(
                (
                    (stage.at[s, 0], q_ref.at[rows, :]),
                    (stage.at[s, 1], k_ref.at[rows, :]),
                    (stage.at[s, 2], v_ref.at[rows, :]),
                    (stage_o.at[s], o_ref.at[pl.ds(128 * way, 128), lane_at]),
                )
            ):
                copies.append(pltpu.make_async_copy(src, dst, sems.at[s, c]))
                copies[-1].start()
    for copy in copies:
        copy.wait()


def head_unpack(idx, pieces, width, cols):
    return pl.pallas_call(
        head_unpack_kernel,
        out_shape=(sds((width, cols), f32),) * 3 + (sds((cols, width), f32), sds((16, width), f32)),
        in_specs=[SMEM] + [VMEM] * 16,
        out_specs=[ANY] * 4 + [VMEM],
        scratch_shapes=[
            pltpu.VMEM((16, 3, 64, cols), f32),
            pltpu.VMEM((16, 128, 128), f32),
            pltpu.SemaphoreType.DMA((16, 4)),
        ],
        compiler_params=params(40),
        cost_estimate=cost(0.1, 6),
        name="head_unpack",
    )(idx, *pieces)


def mask_arrays(doc_lens, keep, length):
    positions = lax.iota(jnp.int32, length)
    ends = jnp.cumsum(doc_lens)
    second = (positions >= ends[0]).astype(f32)
    first = 1.0 - second
    keep = (keep == 1).astype(f32)
    lane = lax.iota(jnp.int32, 256)[None, :] % HEAD_DIM
    first_c, second_c, keep_c = first[:, None], second[:, None], keep[:, None]
    add_q = jnp.where(lane == 0, first_c, jnp.where(lane == 1, second_c, jnp.where(lane == 2, 1.0, 0.0)))
    add_k = jnp.where(
        lane == 0,
        second_c * NEG,
        jnp.where(
            lane == 1,
            first_c * NEG,
            jnp.where(lane == 2, (1.0 - keep_c) * NEG, jnp.where(lane < 6, -1.0, 0.0)),
        ),
    )
    return (
        add_q.astype(bf16),
        add_k.astype(bf16),
        jnp.stack([second, keep], axis=1),
        jnp.stack([keep, second], axis=0),
    )


def swap(value, k):
    return lax.ppermute(value, "tensor", [(i, i ^ k) for i in range(4)])


def spread(own):
    far = swap(own, 2)
    return own, swap(own, 1), far, swap(far, 1)


def collect(parts):
    passed = (parts[2].astype(f32) + swap(parts[3], 1).astype(f32)).astype(bf16)
    return parts[0], swap(parts[1], 1), swap(passed, 2)


class Ring:
    order = (0, 2, 4, 6, 7, 5, 3, 1)

    def __init__(self, dp):
        self.dp = dp
        place = [0] * INNER
        for p, d in enumerate(self.order):
            place[d] = p
        self.place = jnp.array(place, jnp.int32)[lax.axis_index("dp") % INNER]

    def send(self, value, way):
        step = 1 if way == 0 else -1
        pairs = [
            (g + self.order[p], g + self.order[(p + step) % INNER])
            for g in range(0, self.dp, INNER)
            for p in range(INNER)
        ]
        return lax.ppermute(value, "dp", pairs)

    def piece(self, packed, step, way):
        number = (self.place - step if way == 0 else self.place + step) % INNER
        return lax.dynamic_index_in_dim(packed, number, 0, keepdims=False)[way], number

    def total(self, packed):
        moving = [self.piece(packed, 0, way)[0] for way in range(2)]
        for step in range(1, INNER):
            moving = [self.send(moving[way], way) for way in range(2)]
            moving = [
                (moving[way].astype(f32) + self.piece(packed, step, way)[0].astype(f32)).astype(bf16)
                for way in range(2)
            ]
        if self.dp > INNER:
            groups = [[g + d for g in range(0, self.dp, INNER)] for d in range(INNER)]
            moving = [lax.psum(m, "dp", axis_index_groups=groups) for m in moving]
        pieces, numbers = [[], []], [[], []]
        for step in range(INNER):
            for way in range(2):
                pieces[way].append(moving[way])
                shift = INNER - 1 - (INNER - step) % INNER
                number = self.place - (INNER - 1 + step) if way == 0 else self.place + (INNER - 1 + step)
                numbers[way].append(number % INNER)
            if step < INNER - 1:
                moving = [self.send(moving[way], way) for way in range(2)]
        return jnp.stack(numbers[0] + numbers[1]).astype(jnp.int32), pieces[0] + pieces[1]


def per_device(
    dp, tokens, gain_attn, w_query, w_key, w_value, w_out, gain_mlp, w_gate, w_up, w_down, doc_lens, pad_mask, cotangent
):
    t = lax.axis_index("tensor").astype(jnp.int32).reshape(1)
    width, hidden = w_gate.shape
    length = 4 * tokens.shape[0]
    gain_one = gain_attn.astype(f32).reshape(1, width)
    gain_two = gain_mlp.astype(f32).reshape(1, width)

    x_parts = spread(tokens)
    keep_parts = jnp.stack([swap(pad_mask, k) if k else pad_mask for k in range(4)])
    keep = jnp.stack([keep_parts[t[0] ^ k] for k in range(4)]).reshape(length)
    masks = mask_arrays(doc_lens[0], keep, length)
    w_parts = spread(w_out)
    dy_parts = spread(cotangent)

    xn, q, k, v = project(t, x_parts, gain_one, w_query, w_key, w_value)
    o, log_norm = attend(q, k, v, masks)
    o_parts = spread(o)

    far = mlp(
        t, o_parts, w_parts, (x_parts[3], x_parts[2]), (dy_parts[3], dy_parts[2]), gain_two, w_gate, w_up, w_down, (3, 2)
    )
    near = mlp(
        t, o_parts, w_parts, (x_parts[1], x_parts[0]), (dy_parts[1], dy_parts[0]), gain_two, w_gate, w_up, w_down, (1, 0)
    )
    h_own = near[9]
    sums = collect((near[7], near[6], far[7], far[6]))
    packed = mlp_grads(
        (near[0], far[0]), (near[1], far[1]), (near[2], far[2]), (near[3], far[3]),
        (dy_parts[1], dy_parts[0], dy_parts[3], dy_parts[2]),
    )
    ring = Ring(dp)
    mlp_idx, mlp_pieces = ring.total(packed)
    dh, da, *do_parts = hidden_back(sums, h_own, cotangent, gain_two, w_parts)
    do_parts = [do_parts[0]] + [swap(do_parts[i], i) for i in range(1, 4)]
    dq, dk, dv = attend_back(t, q, k, v, do_parts, o, log_norm, masks)
    *dx_parts, gsum_one = tokens_back(t, dq, dk, dv, w_query, w_key, w_value, xn)
    gains = jnp.concatenate([gsum_one / gain_one, (near[8] + far[8]) / gain_two], axis=0)
    gains = gains + swap(gains, 1)
    gains = gains + swap(gains, 2)
    gains = jnp.concatenate([gains, jnp.zeros((14, width), f32)], axis=0)
    da_parts = spread(da)
    head_packed = head_grads(t, xn, dq, dk, dv, o, da_parts, gains)
    head_idx, head_pieces = ring.total(head_packed)

    terms = collect((near[5], near[4], far[5], far[4]))
    output = (h_own + sum(term.astype(f32) for term in terms)).astype(bf16)

    dxn = sum(term.astype(f32) for term in collect(dx_parts))
    x = tokens.astype(f32)
    inv = rms_rows(x)
    weighted = dxn * gain_one
    inner = jnp.mean(weighted * x, axis=-1, keepdims=True)
    grad_tokens = (dh + inv * weighted - x * (inv * inv * inv) * inner).astype(bf16)

    grad_gate, grad_up, grad_down = mlp_unpack(mlp_idx, mlp_pieces, width, hidden)
    grad_query, grad_key, grad_value, grad_out, grad_gains = head_unpack(head_idx, head_pieces, width, w_query.shape[1])
    return (
        output, grad_tokens, grad_gains[0], grad_query, grad_key, grad_value, grad_out, grad_gains[1],
        grad_gate, grad_up, grad_down,
    )


def solution(mesh):
    rows = P(("dp", "tensor"), None)
    columns = P(None, "tensor")
    shares = P("tensor", None)
    return jax.shard_map(
        functools.partial(per_device, mesh.shape["dp"]),
        mesh=mesh,
        in_specs=(
            rows, P(), columns, columns, columns, shares, P(), columns, columns, shares,
            P("dp", None), P(("dp", "tensor")), rows,
        ),
        out_specs=(rows, rows, P(), columns, columns, columns, shares, P(), columns, columns, shares),
        check_vma=False,
    )
```

```python
import functools

import jax
import jax.numpy as jnp
from jax import lax
from jax.experimental import pallas as pl
from jax.experimental.pallas import tpu as pltpu
from jax.sharding import PartitionSpec as P

HEAD_DIM = 64
EPS = 1e-05
NEG = -1e30
BLOCK = 256
INNER = 8
bf16 = jnp.bfloat16
f32 = jnp.float32
MIB = 2**20


def dot(a, b, ca=1, cb=0):
    return lax.dot_general(a, b, (((ca,), (cb,)), ((), ())), preferred_element_type=f32)


def params(limit_mib):
    return pltpu.CompilerParams(vmem_limit_bytes=limit_mib * MIB)


def cost(gflop, mbytes):
    return pl.CostEstimate(
        flops=int(gflop * 1e9), bytes_accessed=int(mbytes * 1e6), transcendentals=0
    )


def sds(shape, dtype):
    return jax.ShapeDtypeStruct(shape, dtype)


SMEM = pl.BlockSpec(memory_space=pltpu.SMEM)
VMEM = pl.BlockSpec(memory_space=pltpu.VMEM)
ANY = pl.BlockSpec(memory_space=pl.ANY)

def region(shape):
    return lax.broadcasted_iota(jnp.int32, shape, 1) // HEAD_DIM


def lanes(shape):
    return lax.broadcasted_iota(jnp.int32, shape, 1)


def part_rows(t_ref, k, part):
    return pl.ds(pl.multiple_of((t_ref[0] ^ k) * part, part), part)


def mask_terms(t_ref, lens_ref, keep_refs, keep_row, width=256):
    length = keep_row.shape[1]
    part = length // 4
    keep_row[...] = jnp.zeros(keep_row.shape, f32)
    for k, piece in enumerate(keep_refs):
        keep_row[0:1, part_rows(t_ref, k, part)] = jnp.where(piece[...] == 1, 1.0, 0.0)
    keep_col = keep_row[...].T[:, 0:1]
    end = lens_ref[0, 0]
    doc_col = jnp.where(lax.broadcasted_iota(jnp.int32, (length, 1), 0) >= end, 1.0, 0.0)
    doc_row = jnp.where(lax.broadcasted_iota(jnp.int32, (1, length), 1) >= end, 1.0, 0.0)
    lane = lanes((length, width)) % HEAD_DIM
    add_q = jnp.where(lane == 0, 1.0 - doc_col, jnp.where(lane == 1, doc_col, jnp.where(lane == 2, 1.0, 0.0)))
    hide = jnp.where(lane == 0, doc_col, jnp.where(lane == 1, 1.0 - doc_col, 1.0 - keep_col))
    add_k = jnp.where(lane < 3, hide * NEG, jnp.where(lane < 6, -1.0, 0.0))
    return add_q.astype(bf16), add_k.astype(bf16), keep_col, doc_col, keep_row[0:1, :], doc_row


def rms_rows(values):
    return lax.rsqrt(jnp.mean(values * values, axis=-1, keepdims=True) + EPS)


class Copies:
    def __init__(self, sems):
        self.sems = sems
        self.count = 0
        self.flying = {}

    def start(self, source, target):
        copy = pltpu.make_async_copy(source, target, self.sems.at[self.count])
        copy.start()
        self.flying[id(copy)] = copy
        self.count += 1
        return copy

    def wait(self, *copies):
        for copy in copies or tuple(self.flying.values()):
            self.flying.pop(id(copy)).wait()


def attend_kernel(
    t_ref, lens_ref, gain_ref, p0, p1, p2, p3, x0, x1, x2, x3, wq, wk, wv,
    xn_ref, q_ref, k_ref, v_ref, o_ref, l_ref,
    x_s, w_s, xn_s, q_s, k_s, v_s, qm, km, o_s, l_s, keep_s, in_sems, out_sems,
):
    length = q_s.shape[0]
    part = length // 4
    zero = jnp.zeros((), bf16)
    inward, outward = Copies(in_sems), Copies(out_sems)
    gain = gain_ref[...].astype(f32)
    arrived = [inward.start(x0, x_s.at[0])]
    arrived += [inward.start(w, w_s.at[m]) for m, w in enumerate((wq, wk, wv))]
    arrived += [inward.start(x, x_s.at[1 + i]) for i, x in enumerate((x1, x2, x3))]
    add_q, add_k, _, doc_col, keep_row, doc_row = mask_terms(t_ref, lens_ref, (p0, p1, p2, p3), keep_s)
    inward.wait(*arrived[:4])
    for k in range(4):
        if k > 0:
            inward.wait(arrived[3 + k])
        rows = part_rows(t_ref, k, part)
        x = x_s[k].astype(f32)
        xn = (x * rms_rows(x) * gain).astype(bf16)
        xn_s[rows, :] = xn
        q_s[rows, :] = (dot(xn, w_s[0]).astype(bf16).astype(f32) * 0.125).astype(bf16)
        k_s[rows, :] = dot(xn, w_s[1]).astype(bf16)
        v_s[rows, :] = dot(xn, w_s[2]).astype(bf16)
    for source, target in ((xn_s, xn_ref), (q_s, q_ref), (k_s, k_ref), (v_s, v_ref)):
        outward.start(source, target)
    reg = region((length, 256))
    for h in range(4):
        following = (h + 1) % 4
        qm[h] = jnp.where(reg == h, q_s[...], jnp.where(reg == following, add_q, zero))
        km[h] = jnp.where(reg == h, k_s[...], add_k)
    reg_b = region((BLOCK, 256))
    ri = lax.broadcasted_iota(jnp.int32, (BLOCK, BLOCK), 0)
    ci = lax.broadcasted_iota(jnp.int32, (BLOCK, BLOCK), 1)
    ln = lanes((BLOCK, 128))
    for i in range(length // BLOCK):
        r0 = i * BLOCK
        here = slice(r0, r0 + BLOCK)
        same = doc_col[here, :] == doc_row[:, here]
        seen = (ri == ci) | ((ci < ri) & (keep_row[:, here] > 0.5) & same)
        bias = jnp.where(seen, 0.0, NEG).astype(f32)
        o_acc = jnp.zeros((BLOCK, 256), f32)
        l_acc = jnp.zeros((BLOCK, 128), f32)
        for h in range(4):
            qh = qm[h, here, :]
            plain = jnp.where(reg_b == h, qh, zero)
            s_diag = dot(plain, k_s[here, :], 1, 1) + bias
            top = jnp.max(s_diag, axis=1, keepdims=True)
            if i > 0:
                s_left = dot(qh, km[h, 0:r0, :], 1, 1)
                top = jnp.maximum(top, jnp.max(s_left, axis=1, keepdims=True))
            p_diag = jnp.exp(s_diag - top)
            total = jnp.sum(p_diag, axis=1, keepdims=True)
            acc = dot(p_diag.astype(bf16), v_s[here, :])
            if i > 0:
                p_left = jnp.exp(s_left - top)
                total = total + jnp.sum(p_left, axis=1, keepdims=True)
                acc = acc + dot(p_left.astype(bf16), v_s[0:r0, :])
            o_acc = jnp.where(reg_b == h, acc * (1.0 / total), o_acc)
            l_acc = jnp.where(ln == h, top + jnp.log(total), l_acc)
        o_s[here, :] = o_acc.astype(bf16)
        l_s[here, :] = l_acc
        outward.start(o_s.at[here, :], o_ref.at[here, :])
        outward.start(l_s.at[here, :], l_ref.at[here, :])
    outward.wait()


def attend(t, lens, gain, keep_parts, x_parts, wq, wk, wv):
    part, width = x_parts[0].shape
    length, cols = 4 * part, wq.shape[1]
    head_rows = sds((length, cols), bf16)
    scratch = [
        ((4, part, width), bf16),
        ((3, width, cols), bf16),
        ((length, width), bf16),
        *[((length, cols), bf16)] * 3,
        *[((4, length, cols), bf16)] * 2,
        ((length, cols), bf16),
        ((length, 128), f32),
        ((128, length), f32),
    ]
    return pl.pallas_call(
        attend_kernel,
        out_shape=(sds((length, width), bf16), *[head_rows] * 4, sds((length, 128), f32)),
        in_specs=[SMEM] * 2 + [VMEM] * 5 + [ANY] * 7,
        out_specs=[ANY] * 6,
        scratch_shapes=[pltpu.VMEM(*s) for s in scratch]
        + [pltpu.SemaphoreType.DMA((7,)), pltpu.SemaphoreType.DMA((4 + 2 * (length // BLOCK),))],
        compiler_params=params(60),
        cost_estimate=cost(15, 15),
        name="attend",
    )(t, lens, gain, *keep_parts, *x_parts, wq, wk, wv)


def split3(value):
    high = value.astype(bf16)
    rest = value - high.astype(f32)
    middle = rest.astype(bf16)
    return high, middle, (rest - middle.astype(f32)).astype(bf16)


def attn_bwd_kernel(
    t_ref, lens_ref, p0, p1, p2, p3, q_ref, k_ref, v_ref, d0, d1, d2, d3, o_ref, l_ref,
    dq_ref, dk_ref, dv_ref, qm, km, dm, vm, do_ref, dq_acc, keep_s, *, pair,
):
    length = q_ref.shape[0]
    blocks = length // BLOCK
    zero = jnp.zeros((), bf16)
    minus = -jnp.ones((), bf16)
    for k, piece in enumerate((d0, d1, d2, d3)):
        do_ref[part_rows(t_ref, k, length // 4), :] = piece[...]
    add_q, add_k, keep_col, doc_col, _, doc_row = mask_terms(t_ref, lens_ref, (p0, p1, p2, p3), keep_s, 128)
    half = region((length, 128))
    ln = lanes((length, 128))
    both = do_ref[...].astype(f32) * o_ref[...].astype(f32)
    for h in range(2):
        a = (1 - h) * HEAD_DIM
        own = half == h
        high, middle, low = split3(l_ref[:, 2 * pair + h : 2 * pair + h + 1])
        extra = jnp.where(ln == a + 3, high, jnp.where(ln == a + 4, middle, jnp.where(ln == a + 5, low, add_q)))
        qm[h] = jnp.where(own, q_ref[...], extra)
        km[h] = jnp.where(own, k_ref[...], add_k)
        high, middle, low = split3(jnp.sum(jnp.where(own, both, 0.0), axis=1, keepdims=True))
        extra = jnp.where(ln == a, high, jnp.where(ln == a + 1, middle, jnp.where(ln == a + 2, low, zero)))
        dm[h] = jnp.where(own, do_ref[...], extra)
        vm[h] = jnp.where(own, v_ref[...], jnp.where((ln >= a) & (ln < a + 3), minus, zero))
    half_b = region((BLOCK, 128))
    ln_b = lanes((BLOCK, 128))
    ri = lax.broadcasted_iota(jnp.int32, (BLOCK, BLOCK), 0)
    ci = lax.broadcasted_iota(jnp.int32, (BLOCK, BLOCK), 1)
    dq_acc[...] = jnp.zeros(dq_acc.shape, f32)
    turned = [k_ref[BLOCK * j : BLOCK * (j + 1), :].T for j in range(blocks)]
    biases = []
    for j in range(blocks):
        here = slice(BLOCK * j, BLOCK * (j + 1))
        same = doc_col[here, :] == doc_row[:, here]
        seen = (ri == ci) | ((ri < ci) & (keep_col[here, :] > 0.5) & same)
        biases.append(jnp.where(seen, 0.0, NEG).astype(f32))

    def products(j, h):
        here, below = slice(BLOCK * j, BLOCK * (j + 1)), slice(BLOCK * (j + 1), length)
        a = (1 - h) * HEAD_DIM
        plain = jnp.where(half_b == h, k_ref[here, :], jnp.where((ln_b >= a + 3) & (ln_b < a + 6), minus, zero))
        got = [(here, dot(plain, qm[h, here, :], 1, 1), dot(vm[h, here, :], dm[h, here, :], 1, 1))]
        if j < blocks - 1:
            got.append((below, dot(km[h, here, :], qm[h, below, :], 1, 1), dot(vm[h, here, :], dm[h, below, :], 1, 1)))
        return got

    items = [(j, h) for j in range(blocks) for h in range(2)]
    ahead = products(*items[0])
    for n, (j, h) in enumerate(items):
        now, ahead = ahead, products(*items[n + 1]) if n + 1 < len(items) else None
        dk = dv = None
        for rows, s, dp in now:
            p = jnp.exp(s + biases[j] if rows.start == BLOCK * j else s)
            ds = (p * dp).astype(bf16)
            dk_part, dv_part = dot(ds, q_ref[rows, :]), dot(p.astype(bf16), do_ref[rows, :])
            dk, dv = (dk_part, dv_part) if dk is None else (dk + dk_part, dv + dv_part)
            dq_acc[h, :, rows] += dot(turned[j], ds)
        if h == 0:
            first = dk, dv
        else:
            here = slice(BLOCK * j, BLOCK * (j + 1))
            dk_ref[here, :] = jnp.where(half_b == 0, first[0], dk).astype(bf16)
            dv_ref[here, :] = jnp.where(half_b == 0, first[1], dv).astype(bf16)
    dq_ref[...] = (jnp.where(half == 0, dq_acc[0].T, dq_acc[1].T) * 0.125).astype(bf16)


def attend_back(t, lens, keep_parts, q, k, v, do_parts, o, log_norm, pair):
    length = q.shape[0]
    mine = pl.BlockSpec((length, 128), lambda i: (0, pair))
    mine_part = pl.BlockSpec((length // 4, 128), lambda i: (0, pair))
    return pl.pallas_call(
        functools.partial(attn_bwd_kernel, pair=pair),
        grid=(1,),
        out_shape=(sds((length, 128), bf16),) * 3,
        in_specs=[SMEM] * 2 + [VMEM] * 4 + [mine] * 3 + [mine_part] * 4 + [mine, VMEM],
        scratch_shapes=[pltpu.VMEM((2, length, 128), bf16)] * 4
        + [pltpu.VMEM((length, 128), bf16), pltpu.VMEM((2, 128, length), f32), pltpu.VMEM((128, length), f32)],
        compiler_params=params(60),
        cost_estimate=cost(12, 4),
        name="attend_back",
    )(t, lens, *keep_parts, q, k, v, *do_parts, o, log_norm)

def fetch_w_out(inward, t_ref, sources, target):
    started = [inward.start(w, target.at[u]) for u, w in enumerate(sources[:2])]
    few = target.shape[1] // INNER
    for u in (2, 3):
        for block in range(INNER):
            turn = t_ref[1] ^ block
            turn = (turn % 2) * 4 + turn // 2 % 2 * 2 + turn // 4
            rows = pl.ds(pl.multiple_of(turn * few, few), few)
            started.append(inward.start(sources[u].at[rows, :], target.at[u, block * few : (block + 1) * few, :]))
    return started


def mlp_kernel(
    t_ref, gain_ref, o0, o1, o2, o3, w0, w1, w2, w3, x0, x1, x2, x3, y0, y1, y2, y3, wg, wu, wd,
    f0, f1, f2, f3, b0, b1, b2, b3, own_ref, pack_ref, sum_ref,
    o_s, w_s, x_s, y_s, wg_s, wu_s, wd_s, hn_s, act_s, dg_s, du_s, f_s, b_s, own_s, left, pack_s, in_sems, out_sems,
):
    part = x_s.shape[1]
    hidden, width = wg_s.shape
    gain = gain_ref[...].astype(f32)
    inward, outward = Copies(in_sems), Copies(out_sems)
    order = (3, 2, 1, 0)
    slot = {k: i % 2 for i, k in enumerate(order)}
    blocks = {k: slice(k * part, (k + 1) * part) for k in order}
    o_here, sent = {}, {}

    def fetch(k):
        rows = part_rows(t_ref, k, part)
        o_here[k] = [inward.start(o.at[rows, :], o_s.at[slot[k], u]) for u, o in enumerate((o0, o1, o2, o3))]
        o_here[k].append(inward.start((x0, x1, x2, x3)[k], x_s.at[slot[k]]))

    fetch(order[0])
    w_here = fetch_w_out(inward, t_ref, (w0, w1, w2, w3), w_s)
    up_here = [inward.start(wg, wg_s), inward.start(wu, wu_s)]
    fetch(order[1])
    y_here = {k: inward.start((y0, y1, y2, y3)[k], y_s.at[blocks[k], :]) for k in order}
    down_here = inward.start(wd, wd_s)
    totals, products = {}, {}

    def project_out(k):
        inward.wait(*o_here[k])
        totals[k] = x_s[slot[k]].astype(f32)
        for u in range(4):
            totals[k] = totals[k] + dot(o_s[slot[k], u], w_s[u])

    def norm(k):
        if k == 0:
            own_s[...] = totals[k]
            outward.start(own_s, own_ref)
        hn_s[blocks[k], :] = (totals[k] * rms_rows(totals[k]) * gain).astype(bf16)

    def forward(k):
        hn = hn_s[blocks[k], :]
        products[k] = (
            dot(hn, wg_s[...], 1, 1),
            dot(hn, wu_s[...], 1, 1),
            dot(y_s[blocks[k], :], wd_s[...], 1, 1).astype(bf16).astype(f32),
        )

    def activate(k):
        gate, up, dact = products[k]
        sig = 1.0 / (1.0 + jnp.exp(-gate))
        silu = gate * sig
        act_s[blocks[k], :] = (silu * up).astype(bf16)
        dg_s[blocks[k], :] = (dact * up * sig * (1.0 + gate * (1.0 - sig))).astype(bf16)
        du_s[blocks[k], :] = (dact * silu).astype(bf16)

    def backward(k):
        if slot[k] in sent:
            outward.wait(*sent[slot[k]])
        b_s[slot[k]] = (dot(dg_s[blocks[k], :], wg_s[...]) + dot(du_s[blocks[k], :], wu_s[...])).astype(bf16)
        f_s[slot[k]] = dot(act_s[blocks[k], :], wd_s[...]).astype(bf16)
        sent[slot[k]] = [
            outward.start(b_s.at[slot[k]], (b0, b1, b2, b3)[k]),
            outward.start(f_s.at[slot[k]], (f0, f1, f2, f3)[k]),
        ]

    inward.wait(*w_here)
    for pair in (order[:2], order[2:]):
        one, two = pair
        project_out(one)
        project_out(two)
        if pair == order[:2]:
            inward.wait(*up_here, down_here, *y_here.values())
            for k in order[2:]:
                fetch(k)
        norm(one)
        forward(one)
        norm(two)
        forward(two)
        activate(one)
        backward(one)
        activate(two)
        backward(two)
    for m, held, right in ((0, dg_s, hn_s), (1, du_s, hn_s), (2, act_s, y_s)):
        left[m % 2] = held[...].T
        for c in range(0, width, 256):
            cols = slice(c, c + 256)
            grad = dot(left[m % 2], right[:, cols])
            if m < 2:
                sums = jnp.sum(grad * (wg_s, wu_s)[m][:, cols].astype(f32), axis=0, keepdims=True)
                sum_ref[:, cols] = sums if m == 0 else sum_ref[:, cols] + sums
            grad = grad.astype(bf16)
            for b in range(2):
                pack_s[c // 128 + b, m * hidden : (m + 1) * hidden, :] = grad[:, 128 * b : 128 * b + 128]
            if m == 2:
                two = pl.ds(c // 128, 2)
                outward.start(pack_s.at[two], pack_ref.at[two])
    outward.wait()


def mlp(t, o_parts, w_parts, x_parts, dys, gain, wg, wu, wd):
    part, width = x_parts[0].shape
    hidden = wg.shape[0]
    block, inner = sds((part, width), bf16), (4 * part, hidden)
    pack = (width // 128, 3 * hidden, 128)
    scratch = [
        ((2, 4, part, o_parts[0].shape[1]), bf16),
        ((4,) + w_parts[0].shape, bf16),
        ((2, part, width), bf16),
        ((4 * part, width), bf16),
        *[((hidden, width), bf16)] * 3,
        ((4 * part, width), bf16),
        *[(inner, bf16)] * 3,
        ((2, part, width), bf16),
        ((2, part, width), bf16),
        ((part, width), f32),
        ((2, hidden, 4 * part), bf16),
        (pack, bf16),
    ]
    return pl.pallas_call(
        mlp_kernel,
        out_shape=(*[block] * 8, sds((part, width), f32), sds(pack, bf16), sds((1, width), f32)),
        in_specs=[SMEM, VMEM] + [ANY] * 19,
        out_specs=[ANY] * 10 + [VMEM],
        scratch_shapes=[pltpu.VMEM(*s) for s in scratch]
        + [pltpu.SemaphoreType.DMA((48,)), pltpu.SemaphoreType.DMA((16,))],
        compiler_params=params(61),
        cost_estimate=cost(35, 25),
        name="mlp",
    )(t, gain, *o_parts, *w_parts, *x_parts, *dys, wg, wu, wd)


def unpack_kernel(idx, *refs, shapes):
    n = len(shapes)
    given = len(refs) - 2 * n - 3
    pieces, outs, refs = refs[:given], refs[given : given + n], refs[given + n :]
    held, stages, inward, outward = refs[0], refs[1 : n + 1], Copies(refs[n + 1]), Copies(refs[n + 2])
    strands = len(pieces) // INNER
    high = held.shape[1] // strands
    here = [
        inward.start(piece, held.at[i // strands, high * (i % strands) : high * (i % strands + 1), :])
        for i, piece in enumerate(pieces)
    ]
    for j in range(INNER):
        inward.wait(*here[j * strands : (j + 1) * strands])
        at = pl.ds(pl.multiple_of(idx[j] * 128, 128), 128)
        top = 0
        for (rows, width), out, stage in zip(shapes, outs, stages):
            whole = width == 128 * INNER
            for b in range(1 if whole else width // 128):
                high_b = rows if whole else 128
                stage[j, :, 128 * b : 128 * b + 128] = held[j, top : top + high_b, :].astype(f32)
                top += high_b
            outward.start(stage.at[j], out.at[:, at] if whole else out.at[at, :])
    outward.wait()


def unpack(idx, pieces, shapes, name):
    stages = [(INNER, r, 128) if w == 128 * INNER else (INNER, 128, w) for r, w in shapes]
    held = (INNER, sum(s[1] * s[2] for s in stages) // 128, 128)
    count = max(len(pieces), INNER)
    return pl.pallas_call(
        functools.partial(unpack_kernel, shapes=shapes),
        out_shape=tuple(sds(s, f32) for s in shapes),
        in_specs=[SMEM] + [ANY] * len(pieces),
        out_specs=[ANY] * len(shapes),
        scratch_shapes=[pltpu.VMEM(held, bf16)]
        + [pltpu.VMEM(s, f32) for s in stages]
        + [pltpu.SemaphoreType.DMA((count,)), pltpu.SemaphoreType.DMA((INNER * len(shapes),))],
        compiler_params=params(60),
        cost_estimate=cost(0.1, 14),
        name=name,
    )(idx, *pieces)


def hidden_back_kernel(
    t_ref, gain_ref, b0, b1, b2, b3, h_ref, dy_ref, w0, w1, w2, w3, dh_ref, da_ref, d0, d1, d2, d3,
    b_s, h_s, dy_s, w_s, dh_s, da_s, d_s, in_sems, out_sems,
):
    inward, outward = Copies(in_sems), Copies(out_sems)
    part = dh_s.shape[0]
    halves = [slice(0, part // 2), slice(part // 2, part)]
    here = [inward.start(b, b_s.at[i]) for i, b in enumerate((b0, b1))]
    here += [inward.start(b, b_s.at[2, rows, :]) for b, rows in zip((b2, b3), halves)]
    here += [inward.start(h_ref, h_s), inward.start(dy_ref, dy_s)]
    w_here = fetch_w_out(inward, t_ref, (w0, w1, w2, w3), w_s)
    inward.wait(*(here + w_here))
    for rows in halves:
        dhn = b_s[0, rows, :].astype(f32) + b_s[1, rows, :].astype(f32) + b_s[2, rows, :].astype(f32)
        hidden = h_s[rows, :]
        inv = rms_rows(hidden)
        weighted = dhn * gain_ref[...].astype(f32)
        inner = jnp.mean(weighted * hidden, axis=-1, keepdims=True)
        dh = dy_s[rows, :].astype(f32) + inv * weighted - hidden * (inv * inv * inv) * inner
        dh_s[rows, :] = dh
        da_s[rows, :] = dh.astype(bf16)
        for u in (2, 3, 1, 0):
            d_s[u, rows, :] = dot(da_s[rows, :], w_s[u], 1, 1).astype(bf16)
    for u, d in ((2, d2), (3, d3), (1, d1), (0, d0)):
        outward.start(d_s.at[u], d)
    outward.start(dh_s, dh_ref)
    outward.start(da_s, da_ref)
    outward.wait()


def hidden_back(t, sums, h_own, dy_own, gain, w_parts):
    part, width = h_own.shape
    cols = w_parts[0].shape[0]
    scratch = [
        ((3, part, width), bf16), ((part, width), f32), ((part, width), bf16), ((4, cols, width), bf16),
        ((part, width), f32), ((part, width), bf16), ((4, part, cols), bf16),
    ]
    return pl.pallas_call(
        hidden_back_kernel,
        out_shape=(sds((part, width), f32), sds((part, width), bf16)) + (sds((part, cols), bf16),) * 4,
        in_specs=[SMEM, VMEM] + [ANY] * 10,
        out_specs=[ANY] * 6,
        scratch_shapes=[pltpu.VMEM(*s) for s in scratch]
        + [pltpu.SemaphoreType.DMA((6 + 2 + 2 * INNER,)), pltpu.SemaphoreType.DMA((6,))],
        compiler_params=params(60),
        cost_estimate=cost(2, 10),
        name="hidden_back",
    )(t, gain, *sums, h_own, dy_own, *w_parts)


def tokens_back_kernel(
    t_ref, dq0, dq1, dk0, dk1, dv0, dv1, wq, wk, wv, b0, b1, b2, b3, d_s, w_s, b_s, in_sems, out_sems
):
    inward, outward = Copies(in_sems), Copies(out_sems)
    part = b_s.shape[1]
    for m, pair in enumerate(((dq0, dq1), (dk0, dk1), (dv0, dv1))):
        for b, d in enumerate(pair):
            inward.start(d, d_s.at[m, :, 128 * b : 128 * b + 128])
    for m, w in enumerate((wq, wk, wv)):
        inward.start(w, w_s.at[m])
    inward.wait()
    for k, out in ((3, b3), (2, b2), (1, b1), (0, b0)):
        rows = part_rows(t_ref, k, part)
        b_s[k] = sum(dot(d_s[m, rows, :], w_s[m], 1, 1) for m in range(3)).astype(bf16)
        outward.start(b_s.at[k], out)
    outward.wait()


def tokens_back(t, head_parts, wq, wk, wv):
    length, (width, cols) = head_parts[0].shape[0], wq.shape
    scratch = [(3, length, cols), (3, width, cols), (4, length // 4, width)]
    return pl.pallas_call(
        tokens_back_kernel,
        out_shape=(sds((length // 4, width), bf16),) * 4,
        in_specs=[SMEM] + [ANY] * 9,
        out_specs=[ANY] * 4,
        scratch_shapes=[pltpu.VMEM(s, bf16) for s in scratch]
        + [pltpu.SemaphoreType.DMA((9,)), pltpu.SemaphoreType.DMA((4,))],
        compiler_params=params(60),
        cost_estimate=cost(4, 8),
        name="tokens_back",
    )(t, *head_parts, wq, wk, wv)


def head_grads_kernel(
    t_ref, xn_ref, o_ref, a0, a1, a2, a3, dq0, dq1, dk0, dk1, dv0, dv1, wq, wk, wv, out_ref, gain_ref,
    xn_s, o_s, a_s, d_s, w_s, left, left_o, pack_s, in_sems, out_sems,
):
    length, width = xn_s.shape
    part = length // 4
    cols = o_s.shape[1]
    inward, outward = Copies(in_sems), Copies(out_sems)
    halves = [slice(0, width // 2), slice(width // 2, width)]
    xn_here = [inward.start(xn_ref.at[:, halves[0]], xn_s.at[:, halves[0]])]
    here = [
        inward.start(d, d_s.at[m, :, 128 * b : 128 * b + 128])
        for m, pair in enumerate(((dq0, dq1), (dk0, dk1), (dv0, dv1)))
        for b, d in enumerate(pair)
    ]
    here += [inward.start(w, w_s.at[m]) for m, w in enumerate((wq, wk, wv))]
    xn_here.append(inward.start(xn_ref.at[:, halves[1]], xn_s.at[:, halves[1]]))
    o_here = [inward.start(o_ref, o_s)]
    o_here += [inward.start(a, a_s.at[part_rows(t_ref, k, part), :]) for k, a in enumerate((a0, a1, a2, a3))]
    for i, rows in enumerate(halves):
        inward.wait(xn_here[i])
        left[rows, :] = xn_s[:, rows].T
        if i == 0:
            inward.wait(*here)
        by_row = jnp.zeros((width // 2, cols), f32)
        for m in range(3):
            grad = dot(left[rows, :], d_s[m])
            by_row = by_row + grad * w_s[m, rows, :].astype(f32)
            for piece in range(width // 256):
                for b in range(cols // 128):
                    at = m * cols + 128 * b
                    pack_s[rows.start // 128 + piece, at : at + 128, :] = grad[
                        128 * piece : 128 * piece + 128, 128 * b : 128 * b + 128
                    ].astype(bf16)
        gain_ref[rows, :] = jnp.sum(by_row, axis=1, keepdims=True)
    inward.wait(*o_here)
    left_o[...] = o_s[...].T
    for c in range(0, width, 256):
        grad = dot(left_o[...], a_s[:, c : c + 256]).astype(bf16)
        for b in range(2):
            pack_s[c // 128 + b, 3 * cols :, :] = grad[:, 128 * b : 128 * b + 128]
        two = pl.ds(c // 128, 2)
        outward.start(pack_s.at[two], out_ref.at[two])
    outward.wait()


def head_grads(t, xn, o, da_parts, head_parts, wq, wk, wv):
    length, width = xn.shape
    cols = o.shape[1]
    scratch = [
        (length, width), (length, cols), (length, width), (3, length, cols), (3, width, cols),
        (width, length), (cols, length), (width // 128, 4 * cols, 128),
    ]
    return pl.pallas_call(
        head_grads_kernel,
        out_shape=(sds((width // 128, 4 * cols, 128), bf16), sds((width, 1), f32)),
        in_specs=[SMEM] + [ANY] * 15,
        out_specs=[ANY, VMEM],
        scratch_shapes=[pltpu.VMEM(s, bf16) for s in scratch]
        + [pltpu.SemaphoreType.DMA((16,)), pltpu.SemaphoreType.DMA((4,))],
        compiler_params=params(60),
        cost_estimate=cost(5, 12),
        name="head_grads",
    )(t, xn, o, *da_parts, *head_parts, wq, wk, wv)


def swap(value, k):
    return lax.ppermute(value, "tensor", [(i, i ^ k) for i in range(4)])


def spread(own):
    far = swap(own, 2)
    return own, swap(own, 1), far, swap(far, 1)


def double(value, bit, dp):
    return jnp.concatenate([value, lax.ppermute(value, "dp", [(i, i ^ bit) for i in range(dp)])], axis=0)


class Ring:
    order = (0, 2, 4, 6, 7, 5, 3, 1)

    def __init__(self, dp):
        self.dp = dp
        place = [0] * INNER
        for p, d in enumerate(self.order):
            place[d] = p
        self.place = jnp.array(place, jnp.int32)[lax.axis_index("dp") % INNER]
        self.step = 1 - 2 * (lax.axis_index("tensor") % 2)
        self.pairs = [
            (4 * (g + self.order[p]) + t, 4 * (g + self.order[(p + 1 - 2 * (t % 2)) % INNER]) + t)
            for g in range(0, dp, INNER)
            for p in range(INNER)
            for t in range(4)
        ]

    def send(self, value):
        return lax.ppermute(value, ("dp", "tensor"), self.pairs)

    def number(self, step):
        return (self.place - step * self.step) % INNER

    def piece(self, packed, step):
        return lax.dynamic_index_in_dim(packed, self.number(step), 0, keepdims=False)

    def numbers(self):
        return jnp.stack([self.number(INNER - 1 + s) for s in range(INNER)]).astype(jnp.int32)


class Sum:
    def __init__(self, ring, packed, strands):
        self.ring, self.packed, self.step = ring, packed, 0
        self.on_way = [ring.send(ring.piece(packed, 0))]
        self.pieces = [[] for _ in range(strands)]

    def advance(self, *before):
        ring, strands = self.ring, len(self.pieces)
        self.step += 1
        arrived = pin(self.on_way.pop(0), *before)
        if self.step < INNER:
            arrived = (arrived.astype(f32) + ring.piece(self.packed, self.step).astype(f32)).astype(bf16)
        if self.step < INNER - 1:
            self.on_way = [ring.send(arrived)]
        elif self.step == INNER - 1:
            if ring.dp > INNER:
                groups = [[g + d for g in range(0, ring.dp, INNER)] for d in range(INNER)]
                arrived = lax.psum(arrived, "dp", axis_index_groups=groups)
            rows = arrived.shape[0] // strands
            for s, held in enumerate(self.pieces):
                held.append(arrived[s * rows : (s + 1) * rows])
                self.on_way.append(ring.send(held[0]))
        else:
            held = self.pieces[(self.step - INNER) % strands]
            held.append(arrived)
            if len(held) < INNER:
                self.on_way.append(ring.send(arrived))
        return arrived

    @property
    def done(self):
        return not self.on_way

    def result(self):
        return [piece for arrived in zip(*self.pieces) for piece in arrived]


def pin(value, *before):
    return lax.optimization_barrier((value, *before))[0]


def per_device(
    dp, tokens, gain_attn, w_query, w_key, w_value, w_out, gain_mlp, w_gate, w_up, w_down, doc_lens, pad_mask, cotangent
):
    t = jnp.stack([lax.axis_index("tensor"), lax.axis_index("dp") % INNER]).astype(jnp.int32)
    width, hidden = w_gate.shape
    cols = w_query.shape[1]
    gain_one = gain_attn.reshape(1, width)
    gain_two = gain_mlp.reshape(1, width)
    gate_t, up_t = w_gate.T, w_up.T
    ring = Ring(dp)

    keep_parts = spread(pad_mask.reshape(1, -1))
    few = w_out.shape[0] // INNER
    w_far = swap(lax.dynamic_slice_in_dim(w_out, t[1] * few, few, 0), 2)
    w_first = w_far
    for bit in (4, 2, 1):
        w_far = double(w_far, bit, dp)
        if bit == 4:
            x_own = pin(tokens, w_far)
    x_far = pin(swap(tokens, 2), keep_parts[2])
    x_parts = x_own, swap(tokens, 1), x_far, swap(x_far, 1)
    dy_parts = spread(cotangent)
    w_parts = w_out, swap(w_out, 1), w_far, swap(w_far, 1)

    xn, q, k, v, o, log_norm = attend(t, doc_lens, gain_one, keep_parts, x_parts, w_query, w_key, w_value)
    dy_parts = spread(cotangent)
    o_parts = spread(pin(o, dy_parts[2], w_first))

    *shares, h_own, packed, gain_two_sum = mlp(
        t, o_parts, w_parts, x_parts, dy_parts, gain_two, gate_t, up_t, w_down
    )
    ffn, dhn = shares[:4], shares[4:]
    sum_mlp = Sum(ring, packed, 2)
    passed = (dhn[2].astype(f32) + swap(dhn[3], 1).astype(f32)).astype(bf16)
    half = passed.shape[0] // 2
    passed = [swap(passed[:half], 2), swap(passed[half:], 2)]
    step = sum_mlp.advance(packed)
    step = sum_mlp.advance(passed[0])
    sums = (pin(dhn[0], step), swap(dhn[1], 1), *passed)
    dh, da, *do_parts = hidden_back(t, sums, h_own, cotangent, gain_two, w_parts)
    do_parts = [do_parts[0]] + [swap(do_parts[i], i) for i in range(1, 4)]
    step = sum_mlp.advance(dh)
    da_far = swap(pin(da, do_parts[2], do_parts[3], step), 2)
    step = sum_mlp.advance(do_parts[2], do_parts[3])
    ffn_passed = (ffn[2].astype(f32) + swap(ffn[3], 1).astype(f32)).astype(bf16)
    pairs = []
    for pair in range(2):
        pairs.append(attend_back(t, doc_lens, keep_parts, pin(q, step), k, v, do_parts, o, log_norm, pair))
        step = sum_mlp.advance(pairs[-1][0])
    da_far = pin(da_far, pairs[0][0])
    da_parts = da, swap(da, 1), da_far, swap(da_far, 1)
    head_parts = [pairs[p][m] for m in range(3) for p in range(2)]
    ffn_terms = ffn[0], swap(ffn[1], 1), swap(pin(ffn_passed, da_far), 2)
    head_packed, gain_one_sum = head_grads(t, pin(xn, step), o, da_parts, head_parts, w_query, w_key, w_value)
    sum_head = Sum(ring, head_packed, 1)
    step = sum_mlp.advance(head_packed)

    def back(step):
        out["dx"] = tokens_back(t, [pin(head_parts[0], step), *head_parts[1:]], w_query, w_key, w_value)
        out["across"] = swap(out["dx"][3], 1)
        return out["dx"][0]

    def pass_on(step):
        dx = out["dx"]
        passed = (pin(dx[2], step).astype(f32) + out["across"].astype(f32)).astype(bf16)
        out["dxn"] = dx[0], swap(dx[1], 1), swap(passed, 2)
        return passed

    def finish_output(step):
        out["y"] = (h_own + sum(pin(term, step).astype(f32) for term in ffn_terms)).astype(bf16)
        return out["y"]

    def finish_tokens(step):
        dxn = sum(pin(term, step).astype(f32) for term in out["dxn"])
        x = tokens.astype(f32)
        inv = rms_rows(x)
        weighted = dxn * gain_one.astype(f32)
        inner = jnp.mean(weighted * x, axis=-1, keepdims=True)
        out["dx"] = (dh + inv * weighted - x * (inv * inv * inv) * inner).astype(bf16)
        return out["dx"]

    def add_gains(axis, k):
        def run(step):
            size = 4 if axis == "tensor" else dp
            if "arriving" in out:
                out["gain"] = out["gain"] + pin(out["arriving"], step)
            if k:
                out["arriving"] = lax.ppermute(pin(out["gain"], step), axis, [(i, i ^ k) for i in range(size)])
            return out["gain"]

        return run

    def unpack_mlp(step):
        first, *others = sum_mlp.result()
        pieces = [pin(first, step), *others]
        out["mlp"] = unpack(ring.numbers(), pieces, ((hidden, width),) * 3, "mlp_unpack")
        return out["mlp"][0]

    out = {"gain": jnp.concatenate([gain_one_sum.reshape(1, width), gain_two_sum], axis=0)}
    hops = [("tensor", 1), ("tensor", 2)] + [("dp", 1 << b) for b in range(dp.bit_length() - 1)]
    hops = [add_gains(*hop) for hop in (*hops, (None, 0))]
    tasks = [hops[0], back, hops[1], pass_on, hops[2], finish_output, *hops[3:], finish_tokens]
    while not (sum_mlp.done and sum_head.done):
        for running in (sum_head, sum_mlp):
            if not running.done:
                step = running.advance(step)
                if running.done and running is sum_mlp:
                    tasks.insert(0, unpack_mlp)
        if tasks:
            step = tasks.pop(0)(step)
    for task in tasks:
        step = task(step)
    grad_gate, grad_up, grad_down = out["mlp"]
    grad_query, grad_key, grad_value, grad_out = unpack(
        ring.numbers(), sum_head.result(), ((width, cols),) * 3 + ((cols, width),), "head_unpack"
    )
    output, grad_tokens = out["y"], out["dx"]
    grad_gain_attn, grad_gain_mlp = out["gain"][0] / gain_attn.astype(f32), out["gain"][1] / gain_mlp.astype(f32)
    return (
        output, grad_tokens, grad_gain_attn, grad_query, grad_key, grad_value, grad_out, grad_gain_mlp,
        grad_gate.T, grad_up.T, grad_down,
    )


def solution(mesh):
    rows = P(("dp", "tensor"), None)
    columns = P(None, "tensor")
    shares = P("tensor", None)
    return jax.shard_map(
        functools.partial(per_device, mesh.shape["dp"]),
        mesh=mesh,
        in_specs=(
            rows, P(), columns, columns, columns, shares, P(), columns, columns, shares,
            P("dp", None), P(("dp", "tensor")), rows,
        ),
        out_specs=(rows, rows, P(), columns, columns, columns, shares, P(), columns, columns, shares),
        check_vma=False,
    )
```

```python
import functools

import jax
import jax.numpy as jnp
from jax import lax
from jax.experimental import pallas as pl
from jax.experimental.pallas import tpu as pltpu
from jax.sharding import PartitionSpec as P

HEAD_DIM = 64
EPS = 1e-05
NEG = -1e30
BLOCK = 256
INNER = 8
bf16 = jnp.bfloat16
f32 = jnp.float32
MIB = 2**20


def dot(a, b, ca=1, cb=0):
    return lax.dot_general(a, b, (((ca,), (cb,)), ((), ())), preferred_element_type=f32)


def params(limit_mib):
    return pltpu.CompilerParams(vmem_limit_bytes=limit_mib * MIB)


def cost(gflop, mbytes):
    return pl.CostEstimate(
        flops=int(gflop * 1e9), bytes_accessed=int(mbytes * 1e6), transcendentals=0
    )


def sds(shape, dtype):
    return jax.ShapeDtypeStruct(shape, dtype)


SMEM = pl.BlockSpec(memory_space=pltpu.SMEM)
VMEM = pl.BlockSpec(memory_space=pltpu.VMEM)
ANY = pl.BlockSpec(memory_space=pl.ANY)

def region(shape):
    return lax.broadcasted_iota(jnp.int32, shape, 1) // HEAD_DIM


def lanes(shape):
    return lax.broadcasted_iota(jnp.int32, shape, 1)


def part_rows(t_ref, k, part):
    return pl.ds(pl.multiple_of((t_ref[0] ^ k) * part, part), part)


def mask_terms(t_ref, lens_ref, keep_refs, keep_row, width=256):
    length = keep_row.shape[1]
    part = length // 4
    keep_row[...] = jnp.zeros(keep_row.shape, f32)
    for k, piece in enumerate(keep_refs):
        keep_row[0:1, part_rows(t_ref, k, part)] = jnp.where(piece[...] == 1, 1.0, 0.0)
    keep_col = keep_row[...].T[:, 0:1]
    end = lens_ref[0, 0]
    doc_col = jnp.where(lax.broadcasted_iota(jnp.int32, (length, 1), 0) >= end, 1.0, 0.0)
    doc_row = jnp.where(lax.broadcasted_iota(jnp.int32, (1, length), 1) >= end, 1.0, 0.0)
    lane = lanes((length, width)) % HEAD_DIM
    add_q = jnp.where(lane == 0, 1.0 - doc_col, jnp.where(lane == 1, doc_col, jnp.where(lane == 2, 1.0, 0.0)))
    hide = jnp.where(lane == 0, doc_col, jnp.where(lane == 1, 1.0 - doc_col, 1.0 - keep_col))
    add_k = jnp.where(lane < 3, hide * NEG, jnp.where(lane < 6, -1.0, 0.0))
    return add_q.astype(bf16), add_k.astype(bf16), keep_col, doc_col, keep_row[0:1, :], doc_row


def rms_rows(values):
    return lax.rsqrt(jnp.mean(values * values, axis=-1, keepdims=True) + EPS)


class Copies:
    def __init__(self, sems):
        self.sems = sems
        self.count = 0
        self.flying = {}

    def describe(self, source, target):
        return pltpu.make_async_copy(source, target, self.sems.at[self.count])

    def add(self, copy):
        self.flying[id(copy)] = copy
        self.count += 1
        return copy

    def start(self, source, target):
        copy = self.describe(source, target)
        copy.start()
        return self.add(copy)

    def wait(self, *copies):
        for copy in copies or tuple(self.flying.values()):
            self.flying.pop(id(copy)).wait()


def attend_kernel(
    t_ref, lens_ref, gain_ref, p0, p1, p2, p3, x0, x1, x2, x3, wq, wk, wv,
    xn_ref, q_ref, k_ref, v_ref, o_ref, l_ref,
    x_s, w_s, xn_s, q_s, k_s, v_s, qm, km, o_s, l_s, keep_s, in_sems, out_sems,
):
    length = q_s.shape[0]
    part = length // 4
    zero = jnp.zeros((), bf16)
    inward, outward = Copies(in_sems), Copies(out_sems)
    gain = gain_ref[...].astype(f32)
    arrived = [inward.start(x0, x_s.at[0])]
    arrived += [inward.start(w, w_s.at[m]) for m, w in enumerate((wq, wk, wv))]
    arrived += [inward.start(x, x_s.at[1 + i]) for i, x in enumerate((x1, x2, x3))]
    add_q, add_k, _, doc_col, keep_row, doc_row = mask_terms(t_ref, lens_ref, (p0, p1, p2, p3), keep_s)
    inward.wait(*arrived[:4])
    for k in range(4):
        if k > 0:
            inward.wait(arrived[3 + k])
        rows = part_rows(t_ref, k, part)
        x = x_s[k].astype(f32)
        xn = (x * rms_rows(x) * gain).astype(bf16)
        xn_s[rows, :] = xn
        q_s[rows, :] = (dot(xn, w_s[0]).astype(bf16).astype(f32) * 0.125).astype(bf16)
        k_s[rows, :] = dot(xn, w_s[1]).astype(bf16)
        v_s[rows, :] = dot(xn, w_s[2]).astype(bf16)
    for source, target in ((xn_s, xn_ref), (q_s, q_ref), (k_s, k_ref), (v_s, v_ref)):
        outward.start(source, target)
    reg = region((length, 256))
    for h in range(4):
        following = (h + 1) % 4
        qm[h] = jnp.where(reg == h, q_s[...], jnp.where(reg == following, add_q, zero))
        km[h] = jnp.where(reg == h, k_s[...], add_k)
    reg_b = region((BLOCK, 256))
    ri = lax.broadcasted_iota(jnp.int32, (BLOCK, BLOCK), 0)
    ci = lax.broadcasted_iota(jnp.int32, (BLOCK, BLOCK), 1)
    ln = lanes((BLOCK, 128))
    for i in range(length // BLOCK):
        r0 = i * BLOCK
        here = slice(r0, r0 + BLOCK)
        same = doc_col[here, :] == doc_row[:, here]
        seen = (ri == ci) | ((ci < ri) & (keep_row[:, here] > 0.5) & same)
        bias = jnp.where(seen, 0.0, NEG).astype(f32)
        o_acc = jnp.zeros((BLOCK, 256), f32)
        l_acc = jnp.zeros((BLOCK, 128), f32)
        for h in range(4):
            qh = qm[h, here, :]
            plain = jnp.where(reg_b == h, qh, zero)
            s_diag = dot(plain, k_s[here, :], 1, 1) + bias
            top = jnp.max(s_diag, axis=1, keepdims=True)
            if i > 0:
                s_left = dot(qh, km[h, 0:r0, :], 1, 1)
                top = jnp.maximum(top, jnp.max(s_left, axis=1, keepdims=True))
            p_diag = jnp.exp(s_diag - top)
            total = jnp.sum(p_diag, axis=1, keepdims=True)
            acc = dot(p_diag.astype(bf16), v_s[here, :])
            if i > 0:
                p_left = jnp.exp(s_left - top)
                total = total + jnp.sum(p_left, axis=1, keepdims=True)
                acc = acc + dot(p_left.astype(bf16), v_s[0:r0, :])
            o_acc = jnp.where(reg_b == h, acc * (1.0 / total), o_acc)
            l_acc = jnp.where(ln == h, top + jnp.log(total), l_acc)
        o_s[here, :] = o_acc.astype(bf16)
        l_s[here, :] = l_acc
        outward.start(o_s.at[here, :], o_ref.at[here, :])
        outward.start(l_s.at[here, :], l_ref.at[here, :])
    outward.wait()


def attend(t, lens, gain, keep_parts, x_parts, wq, wk, wv):
    part, width = x_parts[0].shape
    length, cols = 4 * part, wq.shape[1]
    head_rows = sds((length, cols), bf16)
    scratch = [
        ((4, part, width), bf16),
        ((3, width, cols), bf16),
        ((length, width), bf16),
        *[((length, cols), bf16)] * 3,
        *[((4, length, cols), bf16)] * 2,
        ((length, cols), bf16),
        ((length, 128), f32),
        ((128, length), f32),
    ]
    return pl.pallas_call(
        attend_kernel,
        out_shape=(sds((length, width), bf16), *[head_rows] * 4, sds((length, 128), f32)),
        in_specs=[SMEM] * 2 + [VMEM] * 5 + [ANY] * 7,
        out_specs=[ANY] * 6,
        scratch_shapes=[pltpu.VMEM(*s) for s in scratch]
        + [pltpu.SemaphoreType.DMA((7,)), pltpu.SemaphoreType.DMA((4 + 2 * (length // BLOCK),))],
        compiler_params=params(60),
        cost_estimate=cost(15, 15),
        name="attend",
    )(t, lens, gain, *keep_parts, *x_parts, wq, wk, wv)


def split3(value):
    high = value.astype(bf16)
    rest = value - high.astype(f32)
    middle = rest.astype(bf16)
    return high, middle, (rest - middle.astype(f32)).astype(bf16)


def attn_bwd_kernel(
    t_ref, lens_ref, p0, p1, p2, p3, q_ref, k_ref, v_ref, d0, d1, d2, d3, o_ref, l_ref,
    dq_ref, dk_ref, dv_ref, qm, km, dm, vm, do_ref, dq_acc, keep_s, *, pair,
):
    length = q_ref.shape[0]
    blocks = length // BLOCK
    zero = jnp.zeros((), bf16)
    minus = -jnp.ones((), bf16)
    for k, piece in enumerate((d0, d1, d2, d3)):
        do_ref[part_rows(t_ref, k, length // 4), :] = piece[...]
    add_q, add_k, keep_col, doc_col, _, doc_row = mask_terms(t_ref, lens_ref, (p0, p1, p2, p3), keep_s, 128)
    half = region((length, 128))
    ln = lanes((length, 128))
    both = do_ref[...].astype(f32) * o_ref[...].astype(f32)
    for h in range(2):
        a = (1 - h) * HEAD_DIM
        own = half == h
        high, middle, low = split3(l_ref[:, 2 * pair + h : 2 * pair + h + 1])
        extra = jnp.where(ln == a + 3, high, jnp.where(ln == a + 4, middle, jnp.where(ln == a + 5, low, add_q)))
        qm[h] = jnp.where(own, q_ref[...], extra)
        km[h] = jnp.where(own, k_ref[...], add_k)
        high, middle, low = split3(jnp.sum(jnp.where(own, both, 0.0), axis=1, keepdims=True))
        extra = jnp.where(ln == a, high, jnp.where(ln == a + 1, middle, jnp.where(ln == a + 2, low, zero)))
        dm[h] = jnp.where(own, do_ref[...], extra)
        vm[h] = jnp.where(own, v_ref[...], jnp.where((ln >= a) & (ln < a + 3), minus, zero))
    half_b = region((BLOCK, 128))
    ln_b = lanes((BLOCK, 128))
    ri = lax.broadcasted_iota(jnp.int32, (BLOCK, BLOCK), 0)
    ci = lax.broadcasted_iota(jnp.int32, (BLOCK, BLOCK), 1)
    dq_acc[...] = jnp.zeros(dq_acc.shape, f32)
    turned = [k_ref[BLOCK * j : BLOCK * (j + 1), :].T for j in range(blocks)]
    biases = []
    for j in range(blocks):
        here = slice(BLOCK * j, BLOCK * (j + 1))
        same = doc_col[here, :] == doc_row[:, here]
        seen = (ri == ci) | ((ri < ci) & (keep_col[here, :] > 0.5) & same)
        biases.append(jnp.where(seen, 0.0, NEG).astype(f32))

    def products(j, h):
        here, below = slice(BLOCK * j, BLOCK * (j + 1)), slice(BLOCK * (j + 1), length)
        a = (1 - h) * HEAD_DIM
        plain = jnp.where(half_b == h, k_ref[here, :], jnp.where((ln_b >= a + 3) & (ln_b < a + 6), minus, zero))
        got = [(here, dot(plain, qm[h, here, :], 1, 1), dot(vm[h, here, :], dm[h, here, :], 1, 1))]
        if j < blocks - 1:
            got.append((below, dot(km[h, here, :], qm[h, below, :], 1, 1), dot(vm[h, here, :], dm[h, below, :], 1, 1)))
        return got

    items = [(j, h) for j in range(blocks) for h in range(2)]
    ahead = products(*items[0])
    for n, (j, h) in enumerate(items):
        now, ahead = ahead, products(*items[n + 1]) if n + 1 < len(items) else None
        dk = dv = None
        for rows, s, dp in now:
            p = jnp.exp(s + biases[j] if rows.start == BLOCK * j else s)
            ds = (p * dp).astype(bf16)
            dk_part, dv_part = dot(ds, q_ref[rows, :]), dot(p.astype(bf16), do_ref[rows, :])
            dk, dv = (dk_part, dv_part) if dk is None else (dk + dk_part, dv + dv_part)
            dq_acc[h, :, rows] += dot(turned[j], ds)
        if h == 0:
            first = dk, dv
        else:
            here = slice(BLOCK * j, BLOCK * (j + 1))
            dk_ref[here, :] = jnp.where(half_b == 0, first[0], dk).astype(bf16)
            dv_ref[here, :] = jnp.where(half_b == 0, first[1], dv).astype(bf16)
    dq_ref[...] = (jnp.where(half == 0, dq_acc[0].T, dq_acc[1].T) * 0.125).astype(bf16)


def attend_back(t, lens, keep_parts, q, k, v, do_parts, o, log_norm, pair):
    length = q.shape[0]
    mine = pl.BlockSpec((length, 128), lambda i: (0, pair))
    mine_part = pl.BlockSpec((length // 4, 128), lambda i: (0, pair))
    return pl.pallas_call(
        functools.partial(attn_bwd_kernel, pair=pair),
        grid=(1,),
        out_shape=(sds((length, 128), bf16),) * 3,
        in_specs=[SMEM] * 2 + [VMEM] * 4 + [mine] * 3 + [mine_part] * 4 + [mine, VMEM],
        scratch_shapes=[pltpu.VMEM((2, length, 128), bf16)] * 4
        + [pltpu.VMEM((length, 128), bf16), pltpu.VMEM((2, 128, length), f32), pltpu.VMEM((128, length), f32)],
        compiler_params=params(60),
        cost_estimate=cost(0.1, 0.1),
        name="attend_back",
    )(t, lens, *keep_parts, q, k, v, *do_parts, o, log_norm)

def fetch_w_out(inward, t_ref, sources, target):
    started = [inward.start(w, target.at[u]) for u, w in enumerate(sources[:2])]
    few = target.shape[1] // INNER
    for u in (2, 3):
        for block in range(INNER):
            turn = t_ref[1] ^ block
            turn = (turn % 2) * 4 + turn // 2 % 2 * 2 + turn // 4
            rows = pl.ds(pl.multiple_of(turn * few, few), few)
            started.append(inward.start(sources[u].at[rows, :], target.at[u, block * few : (block + 1) * few, :]))
    return started


def send_pieces(outward, t_ref, pack, first, kept, given):
    half = pack.shape[0] // 2
    source, at = pack.at[pl.ds(first, 2)], pl.ds(first % half, 2)
    keep = t_ref[2] == first // half
    copies = outward.describe(source, kept.at[at]), outward.describe(source, given.at[at])
    pl.when(keep)(copies[0].start)
    pl.when(jnp.logical_not(keep))(copies[1].start)
    outward.add(copies[0])


def mlp_kernel(t_ref, gain_ref, o0, o1, o2, o3, w0, w1, w2, w3, *refs, order, last):
    (xa, xb), refs = refs[:2], refs[2:]
    dys, refs = refs[: 4 if last else 2], refs[4 if last else 2 :]
    (wg, wu, wd), refs = refs[:3], refs[3:]
    far, refs = refs[: 4 * last], refs[4 * last :]
    (fa, fb, ba, bb), refs = refs[:4], refs[4:]
    if last:
        b_low, refs = refs[0], refs[1:]
    outs, refs = refs[:4], refs[4:]
    (o_s, w_s, x_s, y_s, wg_s, wu_s, wd_s, hn_s, act_s, dg_s, du_s, f_s, b_s), refs = refs[:13], refs[13:]
    (own_s, left, pack_s), refs = (refs[:3], refs[3:]) if last else ((None,) * 3, refs)
    inward, outward = Copies(refs[0]), Copies(refs[1])
    part = x_s.shape[1]
    hidden, width = wg_s.shape
    gain = gain_ref[...].astype(f32)
    slot = {k: i for i, k in enumerate(order)}
    blocks = {k: slice((k - min(order)) * part, (k - min(order) + 1) * part) for k in range(min(order), 4)}
    o_here = {}
    for k in order:
        rows = part_rows(t_ref, k, part)
        o_here[k] = [inward.start(o.at[rows, :], o_s.at[slot[k], u]) for u, o in enumerate((o0, o1, o2, o3))]
        o_here[k].append(inward.start((xa, xb)[slot[k]], x_s.at[slot[k]]))
        if slot[k] == 0:
            w_here = fetch_w_out(inward, t_ref, (w0, w1, w2, w3), w_s)
            rest = [inward.start(wg, wg_s), inward.start(wu, wu_s)]
    rest += [inward.start(dys[slot[k]], y_s.at[blocks[k], :]) for k in order]
    rest.append(inward.start(wd, wd_s))
    late = [inward.start(source, target.at[2 * part :, :]) for source, target in zip(far, (hn_s, act_s, dg_s, du_s))]
    late += [inward.start(dy, y_s.at[blocks[k], :]) for dy, k in zip(dys[2:], (3, 2))]
    totals, products = {}, {}

    def project_out(k):
        inward.wait(*o_here[k])
        totals[k] = x_s[slot[k]].astype(f32)
        for u in range(4):
            totals[k] = totals[k] + dot(o_s[slot[k], u], w_s[u])

    def norm(k):
        if k == 0:
            own_s[...] = totals[k]
            outward.start(own_s, outs[0])
        hn_s[blocks[k], :] = (totals[k] * rms_rows(totals[k]) * gain).astype(bf16)

    def forward(k):
        hn = hn_s[blocks[k], :]
        products[k] = (
            dot(hn, wg_s[...], 1, 1),
            dot(hn, wu_s[...], 1, 1),
            dot(y_s[blocks[k], :], wd_s[...], 1, 1).astype(bf16).astype(f32),
        )

    def activate(k):
        gate, up, dact = products[k]
        sig = 1.0 / (1.0 + jnp.exp(-gate))
        silu = gate * sig
        act_s[blocks[k], :] = (silu * up).astype(bf16)
        dg_s[blocks[k], :] = (dact * up * sig * (1.0 + gate * (1.0 - sig))).astype(bf16)
        du_s[blocks[k], :] = (dact * silu).astype(bf16)

    def backward(k):
        i = slot[k]
        b_s[i] = (dot(dg_s[blocks[k], :], wg_s[...]) + dot(du_s[blocks[k], :], wu_s[...])).astype(bf16)
        if k == 1:
            outward.start(b_s.at[i, : part // 2, :], ba)
            outward.start(b_s.at[i, part // 2 :, :], b_low)
        else:
            outward.start(b_s.at[i], (ba, bb)[i])
        f_s[i] = dot(act_s[blocks[k], :], wd_s[...]).astype(bf16)
        outward.start(f_s.at[i], (fa, fb)[i])
        if not last:
            for source, target in zip((hn_s, act_s, dg_s, du_s), outs):
                outward.start(source.at[blocks[k], :], target.at[blocks[k], :])

    one, two = order
    inward.wait(*w_here)
    project_out(one)
    project_out(two)
    inward.wait(*rest)
    norm(one)
    forward(one)
    norm(two)
    forward(two)
    activate(one)
    backward(one)
    activate(two)
    backward(two)
    if last:
        inward.wait(*late)
        for m, held, right in ((0, dg_s, hn_s), (1, du_s, hn_s), (2, act_s, y_s)):
            left[m % 2] = held[...].T
            for c in range(0, width, 256):
                cols = slice(c, c + 256)
                grad = dot(left[m % 2], right[:, cols])
                if m < 2:
                    sums = jnp.sum(grad * (wg_s, wu_s)[m][:, cols].astype(f32), axis=0, keepdims=True)
                    outs[3][:, cols] = sums if m == 0 else outs[3][:, cols] + sums
                grad = grad.astype(bf16)
                for b in range(2):
                    pack_s[c // 128 + b, m * hidden : (m + 1) * hidden, :] = grad[:, 128 * b : 128 * b + 128]
                if m == 2:
                    send_pieces(outward, t_ref, pack_s, c // 128, outs[1], outs[2])
    outward.wait()


def mlp(t, o_parts, w_parts, x_pair, dys, gain, wg, wu, wd, order, far=()):
    part, width = x_pair[0].shape
    hidden = wg.shape[0]
    last = bool(far)
    held = (4 if last else 2) * part
    block, inner = sds((part, width), bf16), sds((2 * part, hidden), bf16)
    pack = (width // 128, 3 * hidden, 128)
    scratch = [
        ((2, 4, part, o_parts[0].shape[1]), bf16),
        ((4,) + w_parts[0].shape, bf16),
        ((2, part, width), bf16),
        ((held, width), bf16),
        *[((hidden, width), bf16)] * 3,
        ((held, width), bf16),
        *[((held, hidden), bf16)] * 3,
        ((2, part, width), bf16),
        ((2, part, width), bf16),
    ]
    if last:
        scratch += [((part, width), f32), ((2, hidden, held), bf16), (pack, bf16)]
        half = sds((pack[0] // 2,) + pack[1:], bf16)
        half_block = sds((part // 2, width), bf16)
        shares = [block, block, half_block, block, half_block]
        out = [sds((part, width), f32), half, half, sds((1, width), f32)]
    else:
        shares = [block] * 4
        out = [sds((2 * part, width), bf16), inner, inner, inner]
    return pl.pallas_call(
        functools.partial(mlp_kernel, order=order, last=last),
        out_shape=(*shares, *out),
        in_specs=[SMEM, VMEM] + [ANY] * (13 + len(dys) + len(far)),
        out_specs=[ANY] * (len(shares) + 3) + [VMEM if last else ANY],
        scratch_shapes=[pltpu.VMEM(*s) for s in scratch]
        + [pltpu.SemaphoreType.DMA((48,)), pltpu.SemaphoreType.DMA((16,))],
        compiler_params=params(61),
        cost_estimate=cost(25 if last else 14, 25),
        name="mlp",
    )(t, gain, *o_parts, *w_parts, *x_pair, *dys, wg, wu, wd, *far)


def unpack_kernel(idx, *refs, shapes, more, strands):
    n = len(shapes)
    given = INNER * strands
    pieces, outs, refs = refs[:given], refs[given : given + n], refs[given + n :]
    if more:
        more_ref, refs = refs[0], refs[1:]
    held, stages, inward, outward = refs[0], refs[1 : n + 1], Copies(refs[n + 1]), Copies(refs[n + 2])
    high = held.shape[1] // strands
    here = [
        inward.start(piece, held.at[i // strands, high * (i % strands) : high * (i % strands + 1), :])
        for i, piece in enumerate(pieces)
    ]
    for j in range(INNER):
        inward.wait(*here[j * strands : (j + 1) * strands])
        at = pl.ds(pl.multiple_of(idx[j] * 128, 128), 128)
        top = 0
        for (rows, width), out, stage in zip(shapes, outs, stages):
            whole = width == 128 * INNER
            for b in range(1 if whole else width // 128):
                high_b = rows if whole else 128
                stage[j, :, 128 * b : 128 * b + 128] = held[j, top : top + high_b, :].astype(f32)
                top += high_b
            outward.start(stage.at[j], out.at[:, at] if whole else out.at[at, :])
        if more:
            more_ref[:, at] = held[j, top:, :].astype(f32)
    outward.wait()


def unpack(idx, pieces, shapes, name, more=0):
    stages = [(INNER, r, 128) if w == 128 * INNER else (INNER, 128, w) for r, w in shapes]
    held = (INNER, sum(s[1] * s[2] for s in stages) // 128 + more, 128)
    return pl.pallas_call(
        functools.partial(unpack_kernel, shapes=shapes, more=more, strands=len(pieces) // INNER),
        out_shape=tuple(sds(s, f32) for s in shapes) + (sds((more, 128 * INNER), f32),) * bool(more),
        in_specs=[SMEM] + [ANY] * len(pieces),
        out_specs=[ANY] * len(shapes) + [VMEM] * bool(more),
        scratch_shapes=[pltpu.VMEM(held, bf16)]
        + [pltpu.VMEM(s, f32) for s in stages]
        + [pltpu.SemaphoreType.DMA((len(pieces),)), pltpu.SemaphoreType.DMA((INNER * len(shapes),))],
        compiler_params=params(60),
        cost_estimate=cost(0.1, 0.1),
        name=name,
    )(idx, *pieces)


def hidden_back_kernel(
    t_ref, gain_ref, b0, b1, b2, b3, h_ref, dy_ref, w0, w1, w2, w3, dh_ref, da_ref, d0, d1, d2, d3,
    b_s, h_s, dy_s, w_s, dh_s, da_s, d_s, in_sems, out_sems,
):
    inward, outward = Copies(in_sems), Copies(out_sems)
    part = dh_s.shape[0]
    halves = [slice(0, part // 2), slice(part // 2, part)]
    here = [inward.start(b, b_s.at[i]) for i, b in ((0, b0), (2, b3))]
    here += [inward.start(b, b_s.at[1, rows, :]) for b, rows in zip((b1, b2), halves)]
    here += [inward.start(h_ref, h_s), inward.start(dy_ref, dy_s)]
    w_here = fetch_w_out(inward, t_ref, (w0, w1, w2, w3), w_s)
    inward.wait(*(here + w_here))
    for rows in halves:
        dhn = b_s[0, rows, :].astype(f32) + b_s[1, rows, :].astype(f32) + b_s[2, rows, :].astype(f32)
        hidden = h_s[rows, :]
        inv = rms_rows(hidden)
        weighted = dhn * gain_ref[...].astype(f32)
        inner = jnp.mean(weighted * hidden, axis=-1, keepdims=True)
        dh = dy_s[rows, :].astype(f32) + inv * weighted - hidden * (inv * inv * inv) * inner
        dh_s[rows, :] = dh
        da_s[rows, :] = dh.astype(bf16)
        for u in (2, 3, 1, 0):
            d_s[u, rows, :] = dot(da_s[rows, :], w_s[u], 1, 1).astype(bf16)
    for u, d in ((2, d2), (3, d3), (1, d1), (0, d0)):
        outward.start(d_s.at[u], d)
    outward.start(dh_s, dh_ref)
    outward.start(da_s, da_ref)
    outward.wait()


def hidden_back(t, sums, h_own, dy_own, gain, w_parts):
    part, width = h_own.shape
    cols = w_parts[0].shape[0]
    scratch = [
        ((3, part, width), bf16), ((part, width), f32), ((part, width), bf16), ((4, cols, width), bf16),
        ((part, width), f32), ((part, width), bf16), ((4, part, cols), bf16),
    ]
    return pl.pallas_call(
        hidden_back_kernel,
        out_shape=(sds((part, width), f32), sds((part, width), bf16)) + (sds((part, cols), bf16),) * 4,
        in_specs=[SMEM, VMEM] + [ANY] * 10,
        out_specs=[ANY] * 6,
        scratch_shapes=[pltpu.VMEM(*s) for s in scratch]
        + [pltpu.SemaphoreType.DMA((6 + 2 + 2 * INNER,)), pltpu.SemaphoreType.DMA((6,))],
        compiler_params=params(60),
        cost_estimate=cost(60, 10),
        name="hidden_back",
    )(t, gain, *sums, h_own, dy_own, *w_parts)


def tokens_back_kernel(
    t_ref, dq0, dq1, dk0, dk1, dv0, dv1, wq, wk, wv, b0, b1, b2, b3, d_s, w_s, b_s, in_sems, out_sems
):
    inward, outward = Copies(in_sems), Copies(out_sems)
    part = b_s.shape[1]
    for m, pair in enumerate(((dq0, dq1), (dk0, dk1), (dv0, dv1))):
        for b, d in enumerate(pair):
            inward.start(d, d_s.at[m, :, 128 * b : 128 * b + 128])
    for m, w in enumerate((wq, wk, wv)):
        inward.start(w, w_s.at[m])
    inward.wait()
    for k, out in ((3, b3), (2, b2), (1, b1), (0, b0)):
        rows = part_rows(t_ref, k, part)
        b_s[k] = sum(dot(d_s[m, rows, :], w_s[m], 1, 1) for m in range(3)).astype(bf16)
        outward.start(b_s.at[k], out)
    outward.wait()


def tokens_back(t, head_parts, wq, wk, wv):
    length, (width, cols) = head_parts[0].shape[0], wq.shape
    scratch = [(3, length, cols), (3, width, cols), (4, length // 4, width)]
    return pl.pallas_call(
        tokens_back_kernel,
        out_shape=(sds((length // 4, width), bf16),) * 4,
        in_specs=[SMEM] + [ANY] * 9,
        out_specs=[ANY] * 4,
        scratch_shapes=[pltpu.VMEM(s, bf16) for s in scratch]
        + [pltpu.SemaphoreType.DMA((9,)), pltpu.SemaphoreType.DMA((4,))],
        compiler_params=params(60),
        cost_estimate=cost(0.1, 0.1),
        name="tokens_back",
    )(t, *head_parts, wq, wk, wv)


def head_grads_kernel(
    t_ref, other_ref, xn_ref, o_ref, a0, a1, a2, a3, dq0, dq1, dk0, dk1, dv0, dv1, wq, wk, wv, out_ref,
    xn_s, o_s, a_s, d_s, w_s, left, left_o, pack_s, in_sems, out_sems,
):
    length, width = xn_s.shape
    part = length // 4
    cols = o_s.shape[1]
    inward, outward = Copies(in_sems), Copies(out_sems)
    halves = [slice(0, width // 2), slice(width // 2, width)]
    xn_here = [inward.start(xn_ref.at[:, halves[0]], xn_s.at[:, halves[0]])]
    here = [
        inward.start(d, d_s.at[m, :, 128 * b : 128 * b + 128])
        for m, pair in enumerate(((dq0, dq1), (dk0, dk1), (dv0, dv1)))
        for b, d in enumerate(pair)
    ]
    here += [inward.start(w, w_s.at[m]) for m, w in enumerate((wq, wk, wv))]
    xn_here.append(inward.start(xn_ref.at[:, halves[1]], xn_s.at[:, halves[1]]))
    o_here = [inward.start(o_ref, o_s)]
    o_here += [inward.start(a, a_s.at[part_rows(t_ref, k, part), :]) for k, a in enumerate((a0, a1, a2, a3))]
    for i, rows in enumerate(halves):
        inward.wait(xn_here[i])
        left[rows, :] = xn_s[:, rows].T
        if i == 0:
            inward.wait(*here)
        by_row = jnp.zeros((width // 2, cols), f32)
        for m in range(3):
            grad = dot(left[rows, :], d_s[m])
            by_row = by_row + grad * w_s[m, rows, :].astype(f32)
            for piece in range(width // 256):
                for b in range(cols // 128):
                    at = m * cols + 128 * b
                    pack_s[rows.start // 128 + piece, at : at + 128, :] = grad[
                        128 * piece : 128 * piece + 128, 128 * b : 128 * b + 128
                    ].astype(bf16)
        sums = lax.dot_general(
            jnp.ones((8, cols), f32), by_row, (((1,), (1,)), ((), ())),
            precision=lax.Precision.HIGHEST, preferred_element_type=f32,
        )
        for piece in range(width // 256):
            at = rows.start // 128 + piece
            others = jnp.broadcast_to(other_ref[:, 128 * at : 128 * at + 128], (8, 128))
            both = jnp.concatenate([sums[:, 128 * piece : 128 * piece + 128], others], axis=0)
            pack_s[at, 4 * cols :, :] = both.astype(bf16)
    inward.wait(*o_here)
    left_o[...] = o_s[...].T
    for c in range(0, width, 256):
        grad = dot(left_o[...], a_s[:, c : c + 256]).astype(bf16)
        for b in range(2):
            pack_s[c // 128 + b, 3 * cols : 4 * cols, :] = grad[:, 128 * b : 128 * b + 128]
        two = pl.ds(c // 128, 2)
        outward.start(pack_s.at[two], out_ref.at[two])
    outward.wait()


def head_grads(t, other_gain, xn, o, da_parts, head_parts, wq, wk, wv):
    length, width = xn.shape
    cols = o.shape[1]
    scratch = [
        (length, width), (length, cols), (length, width), (3, length, cols), (3, width, cols),
        (width, length), (cols, length), (width // 128, 4 * cols + 16, 128),
    ]
    return pl.pallas_call(
        head_grads_kernel,
        out_shape=sds((width // 128, 4 * cols + 16, 128), bf16),
        in_specs=[SMEM, VMEM] + [ANY] * 15,
        out_specs=ANY,
        scratch_shapes=[pltpu.VMEM(s, bf16) for s in scratch]
        + [pltpu.SemaphoreType.DMA((16,)), pltpu.SemaphoreType.DMA((4,))],
        compiler_params=params(60),
        cost_estimate=cost(0.1, 0.1),
        name="head_grads",
    )(t, other_gain, xn, o, *da_parts, *head_parts, wq, wk, wv)


def add_kernel(*refs, count):
    terms, out_ref, held, out_s, sems = refs[:count], refs[count], refs[count + 1 : -2], refs[-2], refs[-1]
    copies = Copies(sems)
    for term, target in zip(terms, held):
        copies.start(term, target)
    copies.wait()
    out_s[...] = sum(target[...].astype(f32) for target in held).astype(bf16)
    copies.start(out_s, out_ref)
    copies.wait()


def add(*terms):
    shape = terms[0].shape
    return pl.pallas_call(
        functools.partial(add_kernel, count=len(terms)),
        out_shape=sds(shape, bf16),
        in_specs=[ANY] * len(terms),
        out_specs=ANY,
        scratch_shapes=[pltpu.VMEM(shape, term.dtype) for term in terms]
        + [pltpu.VMEM(shape, bf16), pltpu.SemaphoreType.DMA((len(terms) + 1,))],
        compiler_params=params(60),
        cost_estimate=cost(0.1, 0.1),
        name="add",
    )(*terms)


def tokens_end_kernel(gain_ref, d0, d1, d2, dh_ref, x_ref, out_ref, d_s, dh_s, x_s, out_s, sems):
    copies = Copies(sems)
    for i, d in enumerate((d0, d1, d2)):
        copies.start(d, d_s.at[i])
    copies.start(dh_ref, dh_s)
    copies.start(x_ref, x_s)
    copies.wait()
    x = x_s[...].astype(f32)
    inv = rms_rows(x)
    weighted = (d_s[0].astype(f32) + d_s[1].astype(f32) + d_s[2].astype(f32)) * gain_ref[...].astype(f32)
    inner = jnp.mean(weighted * x, axis=-1, keepdims=True)
    out_s[...] = (dh_s[...] + inv * weighted - x * (inv * inv * inv) * inner).astype(bf16)
    copies.start(out_s, out_ref)
    copies.wait()


def tokens_end(gain, terms, dh, x):
    shape = x.shape
    return pl.pallas_call(
        tokens_end_kernel,
        out_shape=sds(shape, bf16),
        in_specs=[VMEM] + [ANY] * 5,
        out_specs=ANY,
        scratch_shapes=[
            pltpu.VMEM((3, *shape), bf16), pltpu.VMEM(shape, f32), pltpu.VMEM(shape, bf16), pltpu.VMEM(shape, bf16),
            pltpu.SemaphoreType.DMA((6,)),
        ],
        compiler_params=params(60),
        cost_estimate=cost(0.1, 0.1),
        name="tokens_end",
    )(gain, *terms, dh, x)


def swap(value, k):
    return lax.ppermute(value, "tensor", [(i, i ^ k) for i in range(4)])


def spread(own):
    far = swap(own, 2)
    return own, swap(own, 1), far, swap(far, 1)


def double(value, bit, dp):
    return jnp.concatenate([value, lax.ppermute(value, "dp", [(i, i ^ bit) for i in range(dp)])], axis=0)


class Ring:
    order = (0, 2, 4, 6, 7, 5, 3, 1)

    def __init__(self, dp):
        self.dp = dp
        self.member, self.core = lax.axis_index("dp") % INNER, lax.axis_index("tensor") % 2
        self.way = 1 - 2 * self.core
        self.place = jnp.where(self.member % 2 == 0, self.member // 2, INNER - 1 - self.member // 2)

    def side(self, step):
        return self.member >> ((step + self.core) % 3) & 1

    def send(self, value, target):
        pairs = [
            (4 * (g + d) + t, 4 * (g + target(d, t % 2)) + t)
            for g in range(0, self.dp, INNER)
            for d in range(INNER)
            for t in range(4)
        ]
        return lax.ppermute(value, ("dp", "tensor"), pairs)

    def pass_on(self, value):
        return self.send(value, lambda d, c: self.order[(self.order.index(d) + 1 - 2 * c) % INNER])


class Sum:
    def __init__(self, ring, strands):
        self.ring, self.step = ring, 0
        self.pieces = [[] for _ in range(strands)]

    def advance(self, *before):
        ring, strands = self.ring, len(self.pieces)
        self.step += 1
        arrived = pin(self.on_way.pop(0), *before)
        if self.step <= self.adds:
            arrived = (arrived.astype(f32) + self.mine.astype(f32)).astype(bf16)
        if self.step < self.adds:
            self.next_add(arrived)
        elif self.step == self.adds:
            arrived = arrived.reshape(arrived.shape[-2:])
            if ring.dp > INNER:
                groups = [[g + d for g in range(0, ring.dp, INNER)] for d in range(INNER)]
                arrived = lax.psum(arrived, "dp", axis_index_groups=groups)
            rows = arrived.shape[0] // strands
            for s, held in enumerate(self.pieces):
                held.append(arrived[s * rows : (s + 1) * rows])
                self.on_way.append(ring.pass_on(held[0]))
        else:
            held = self.pieces[(self.step - self.adds - 1) % strands]
            held.append(arrived)
            if len(held) < INNER:
                self.on_way.append(ring.pass_on(arrived))
        return arrived

    @property
    def done(self):
        return not self.on_way

    def result(self):
        return [piece for arrived in zip(*self.pieces) for piece in arrived]


class RingSum(Sum):
    adds = INNER - 1

    def __init__(self, ring, packed, strands):
        super().__init__(ring, strands)
        self.packed = packed
        self.on_way = [ring.pass_on(self.piece(0))]
        self.mine = self.piece(1)

    def piece(self, step):
        number = (self.ring.place - step * self.ring.way) % INNER
        return lax.dynamic_index_in_dim(self.packed, number, 0, keepdims=False)

    def next_add(self, arrived):
        self.on_way = [self.ring.pass_on(arrived)]
        self.mine = self.piece(self.step + 1)

    def numbers(self):
        steps = lax.iota(jnp.int32, INNER) + INNER - 1
        return (self.ring.place - steps * self.ring.way) % INNER


class HalvingSum(Sum):
    adds = 3

    def __init__(self, ring, kept, given, strands):
        super().__init__(ring, strands)
        self.mine, self.on_way = kept, [self.give(given)]

    def give(self, value):
        step = self.step
        return self.ring.send(value, lambda d, c: d ^ 1 << (step + c) % 3)

    def next_add(self, arrived):
        side = self.ring.side(self.step)
        halves = arrived.reshape(2, -1, *arrived.shape[-2:])
        self.mine = lax.dynamic_index_in_dim(halves, side, 0, keepdims=False)
        self.on_way = [self.give(lax.dynamic_index_in_dim(halves, 1 - side, 0, keepdims=False))]

    def numbers(self):
        ring = self.ring
        places = (ring.place - lax.iota(jnp.int32, INNER) * ring.way) % INNER
        members = jnp.where(places < INNER // 2, 2 * places, 2 * INNER - 1 - 2 * places)
        return sum((members >> ((step + ring.core) % 3) & 1) << (2 - step) for step in range(3))


def pin(value, *before):
    return lax.optimization_barrier((value, *before))[0]


def per_device(
    dp, tokens, gain_attn, w_query, w_key, w_value, w_out, gain_mlp, w_gate, w_up, w_down, doc_lens, pad_mask, cotangent
):
    ring = Ring(dp)
    t = jnp.stack([lax.axis_index("tensor"), ring.member, ring.side(0)]).astype(jnp.int32)
    width, hidden = w_gate.shape
    cols = w_query.shape[1]
    gain_one = gain_attn.reshape(1, width)
    gain_two = gain_mlp.reshape(1, width)
    gate_t, up_t = w_gate.T, w_up.T

    keep_parts = spread(pin(pad_mask.reshape(1, -1), gain_one, gain_two))
    few = w_out.shape[0] // INNER
    w_far = swap(lax.dynamic_slice_in_dim(w_out, t[1] * few, few, 0), 2)
    w_first = w_far
    for bit in (4, 2, 1):
        w_far = double(w_far, bit, dp)
    x_far = pin(swap(tokens, 2), keep_parts[2])
    x_parts = tokens, swap(tokens, 1), x_far, swap(x_far, 1)
    dy_parts = spread(cotangent)
    w_parts = w_out, swap(w_out, 1), w_far, swap(w_far, 1)

    xn, q, k, v, o, log_norm = attend(t, doc_lens, gain_one, keep_parts, x_parts, w_query, w_key, w_value)
    dy_parts = spread(cotangent)
    o_parts = spread(pin(o, dy_parts[2], w_first))

    weights = gain_two, gate_t, up_t, w_down
    f3, f2, b3, b2, *far = mlp(t, o_parts, w_parts, (x_parts[3], x_parts[2]), (dy_parts[3], dy_parts[2]), *weights, (3, 2))
    passed = (b2.astype(f32) + swap(b3, 1).astype(f32)).astype(bf16)
    f1, f0, b1_high, b0, b1_low, h_own, kept, given, gain_two_sum = mlp(
        t, o_parts, w_parts, (x_parts[1], pin(x_parts[0], passed)), dy_parts[1::-1] + dy_parts[:1:-1], *weights, (1, 0), far
    )
    sum_mlp = HalvingSum(ring, kept, given, 2)
    sums = (b0, swap(b1_high, 1), swap(b1_low, 1), swap(passed, 2))
    dh, da, *do_parts = hidden_back(t, sums, h_own, cotangent, gain_two, w_parts)
    do_parts = [do_parts[0]] + [swap(do_parts[i], i) for i in range(1, 4)]
    da_far = swap(pin(da, do_parts[2], do_parts[3]), 2)
    ffn_passed = add(f2, swap(f3, 1))
    pairs = [attend_back(t, doc_lens, keep_parts, q, k, v, do_parts, o, log_norm, 0)]
    step = sum_mlp.advance(pairs[0][0])
    pairs.append(attend_back(t, doc_lens, keep_parts, pin(q, step), k, v, do_parts, o, log_norm, 1))
    da_far = pin(da_far, pairs[1][0])
    da_parts = da, swap(da, 1), da_far, swap(da_far, 1)
    head_parts = [pairs[p][m] for m in range(3) for p in range(2)]
    ffn_terms = f0, swap(f1, 1), swap(pin(ffn_passed, da_far), 2)
    packed = head_grads(t, gain_two_sum, xn, o, da_parts, head_parts, w_query, w_key, w_value)
    sum_head = RingSum(ring, packed, 1)
    step = sum_mlp.advance(packed)

    def back(step):
        out["dx"] = tokens_back(t, [pin(head_parts[0], step), *head_parts[1:]], w_query, w_key, w_value)
        out["across"] = swap(out["dx"][3], 1)
        return out["dx"][0]

    def pass_on(step):
        dx = out["dx"]
        passed = add(pin(dx[2], step), out["across"])
        out["dxn"] = dx[0], swap(dx[1], 1), swap(passed, 2)
        return passed

    def finish_output(step):
        out["y"] = add(h_own, *[pin(term, step) for term in ffn_terms])
        return out["y"]

    def finish_tokens(step):
        out["dx"] = tokens_end(gain_one, [pin(term, step) for term in out["dxn"]], dh, tokens)
        return out["dx"]

    out = {}
    tasks = [back, pass_on, finish_output, *[None] * 6, finish_tokens]
    while not (sum_mlp.done and sum_head.done):
        if not sum_head.done:
            step = sum_head.advance(step)
        for _ in range(2 if sum_head.step >= 4 and sum_head.step % 2 == 0 else 1):
            if not sum_mlp.done and sum_head.step != 1:
                step = sum_mlp.advance(step)
        if tasks:
            task = tasks.pop(0)
            step = task(step) if task else step
    grad_query, grad_key, grad_value, grad_out, gains = unpack(
        sum_head.numbers(), sum_head.result(), ((width, cols),) * 3 + ((cols, width),), "head_unpack", 16
    )
    first, *others = sum_mlp.result()
    grad_gate, grad_up, grad_down = unpack(
        sum_mlp.numbers(), [pin(first, gains), *others], ((hidden, width),) * 3, "mlp_unpack"
    )
    others = [pin(swap(gains, k), grad_gate) for k in range(1, 4)]
    gains = (gains + others[0]) + (others[1] + others[2])
    output, grad_tokens = out["y"], out["dx"]
    grad_gain_attn, grad_gain_mlp = gains[0] / gain_attn.astype(f32), gains[8] / gain_mlp.astype(f32)
    return (
        output, grad_tokens, grad_gain_attn, grad_query, grad_key, grad_value, grad_out, grad_gain_mlp,
        grad_gate.T, grad_up.T, grad_down,
    )


def solution(mesh):
    rows = P(("dp", "tensor"), None)
    columns = P(None, "tensor")
    shares = P("tensor", None)
    return jax.shard_map(
        functools.partial(per_device, mesh.shape["dp"]),
        mesh=mesh,
        in_specs=(
            rows, P(), columns, columns, columns, shares, P(), columns, columns, shares,
            P("dp", None), P(("dp", "tensor")), rows,
        ),
        out_specs=(rows, rows, P(), columns, columns, columns, shares, P(), columns, columns, shares),
        check_vma=False,
    )
```

```python
import functools

import jax
import jax.numpy as jnp
from jax import lax
from jax.experimental import pallas as pl
from jax.experimental.pallas import tpu as pltpu
from jax.sharding import PartitionSpec as P

HEAD_DIM = 64
EPS = 1e-05
NEG = -1e30
BLOCK = 256
INNER = 8
bf16 = jnp.bfloat16
f32 = jnp.float32
MIB = 2**20


def dot(a, b, ca=1, cb=0):
    return lax.dot_general(a, b, (((ca,), (cb,)), ((), ())), preferred_element_type=f32)


def params(limit_mib):
    return pltpu.CompilerParams(vmem_limit_bytes=limit_mib * MIB)


def cost(gflop, mbytes):
    return pl.CostEstimate(
        flops=int(gflop * 1e9), bytes_accessed=int(mbytes * 1e6), transcendentals=0
    )


def sds(shape, dtype):
    return jax.ShapeDtypeStruct(shape, dtype)


SMEM = pl.BlockSpec(memory_space=pltpu.SMEM)
VMEM = pl.BlockSpec(memory_space=pltpu.VMEM)
ANY = pl.BlockSpec(memory_space=pl.ANY)

def region(shape):
    return lax.broadcasted_iota(jnp.int32, shape, 1) // HEAD_DIM


def lanes(shape):
    return lax.broadcasted_iota(jnp.int32, shape, 1)


def part_rows(t_ref, k, part):
    return pl.ds(pl.multiple_of((t_ref[0] ^ k) * part, part), part)


def mask_terms(t_ref, lens_ref, keep_refs, keep_row, width=256):
    length = keep_row.shape[1]
    part = length // 4
    keep_row[...] = jnp.zeros(keep_row.shape, f32)
    for k, piece in enumerate(keep_refs):
        keep_row[0:1, part_rows(t_ref, k, part)] = jnp.where(piece[...] == 1, 1.0, 0.0)
    keep_col = keep_row[...].T[:, 0:1]
    end = lens_ref[0, 0]
    doc_col = jnp.where(lax.broadcasted_iota(jnp.int32, (length, 1), 0) >= end, 1.0, 0.0)
    doc_row = jnp.where(lax.broadcasted_iota(jnp.int32, (1, length), 1) >= end, 1.0, 0.0)
    lane = lanes((length, width)) % HEAD_DIM
    add_q = jnp.where(lane == 0, 1.0 - doc_col, jnp.where(lane == 1, doc_col, jnp.where(lane == 2, 1.0, 0.0)))
    hide = jnp.where(lane == 0, doc_col, jnp.where(lane == 1, 1.0 - doc_col, 1.0 - keep_col))
    add_k = jnp.where(lane < 3, hide * NEG, jnp.where(lane < 6, -1.0, 0.0))
    return add_q.astype(bf16), add_k.astype(bf16), keep_col, doc_col, keep_row[0:1, :], doc_row


def rms_rows(values):
    return lax.rsqrt(jnp.mean(values * values, axis=-1, keepdims=True) + EPS)


class Copies:
    def __init__(self, sems):
        self.sems = sems
        self.count = 0
        self.flying = {}

    def describe(self, source, target):
        return pltpu.make_async_copy(source, target, self.sems.at[self.count])

    def add(self, copy):
        self.flying[id(copy)] = copy
        self.count += 1
        return copy

    def start(self, source, target):
        copy = self.describe(source, target)
        copy.start()
        return self.add(copy)

    def wait(self, *copies):
        for copy in copies or tuple(self.flying.values()):
            self.flying.pop(id(copy)).wait()


def attend_kernel(
    t_ref, lens_ref, gain_ref, p0, p1, p2, p3, x0, x1, x2, x3, wq, wk, wv,
    xn_ref, q_ref, k_ref, v_ref, o_ref, l_ref, near_ref, away_ref,
    x_s, w_s, xn_s, q_s, k_s, v_s, qm, km, o_s, l_s, keep_s, in_sems, out_sems,
):
    length = q_s.shape[0]
    part = length // 4
    zero = jnp.zeros((), bf16)
    inward, outward = Copies(in_sems), Copies(out_sems)
    gain = gain_ref[...].astype(f32)
    arrived = [inward.start(x0, x_s.at[0])]
    arrived += [inward.start(w, w_s.at[m]) for m, w in enumerate((wq, wk, wv))]
    arrived += [inward.start(x, x_s.at[1 + i]) for i, x in enumerate((x1, x2, x3))]
    add_q, add_k, _, doc_col, keep_row, doc_row = mask_terms(t_ref, lens_ref, (p0, p1, p2, p3), keep_s)
    inward.wait(*arrived[:4])
    for k in range(4):
        if k > 0:
            inward.wait(arrived[3 + k])
        rows = part_rows(t_ref, k, part)
        x = x_s[k].astype(f32)
        xn = (x * rms_rows(x) * gain).astype(bf16)
        xn_s[rows, :] = xn
        q_s[rows, :] = (dot(xn, w_s[0]).astype(bf16).astype(f32) * 0.125).astype(bf16)
        k_s[rows, :] = dot(xn, w_s[1]).astype(bf16)
        v_s[rows, :] = dot(xn, w_s[2]).astype(bf16)
    for source, target in ((xn_s, xn_ref), (q_s, q_ref), (k_s, k_ref), (v_s, v_ref)):
        outward.start(source, target)
    reg = region((length, 256))
    for h in range(4):
        following = (h + 1) % 4
        qm[h] = jnp.where(reg == h, q_s[...], jnp.where(reg == following, add_q, zero))
        km[h] = jnp.where(reg == h, k_s[...], add_k)
    reg_b = region((BLOCK, 256))
    ri = lax.broadcasted_iota(jnp.int32, (BLOCK, BLOCK), 0)
    ci = lax.broadcasted_iota(jnp.int32, (BLOCK, BLOCK), 1)
    ln = lanes((BLOCK, 128))
    for i in range(length // BLOCK):
        r0 = i * BLOCK
        here = slice(r0, r0 + BLOCK)
        same = doc_col[here, :] == doc_row[:, here]
        seen = (ri == ci) | ((ci < ri) & (keep_row[:, here] > 0.5) & same)
        bias = jnp.where(seen, 0.0, NEG).astype(f32)
        o_acc = jnp.zeros((BLOCK, 256), f32)
        l_acc = jnp.zeros((BLOCK, 128), f32)
        for h in range(4):
            qh = qm[h, here, :]
            plain = jnp.where(reg_b == h, qh, zero)
            s_diag = dot(plain, k_s[here, :], 1, 1) + bias
            top = jnp.max(s_diag, axis=1, keepdims=True)
            if i > 0:
                s_left = dot(qh, km[h, 0:r0, :], 1, 1)
                top = jnp.maximum(top, jnp.max(s_left, axis=1, keepdims=True))
            p_diag = jnp.exp(s_diag - top)
            total = jnp.sum(p_diag, axis=1, keepdims=True)
            acc = dot(p_diag.astype(bf16), v_s[here, :])
            if i > 0:
                p_left = jnp.exp(s_left - top)
                total = total + jnp.sum(p_left, axis=1, keepdims=True)
                acc = acc + dot(p_left.astype(bf16), v_s[0:r0, :])
            o_acc = jnp.where(reg_b == h, acc * (1.0 / total), o_acc)
            l_acc = jnp.where(ln == h, top + jnp.log(total), l_acc)
        o_s[here, :] = o_acc.astype(bf16)
        l_s[here, :] = l_acc
        outward.start(o_s.at[here, :], o_ref.at[here, :])
        outward.start(l_s.at[here, :], l_ref.at[here, :])
    for chip, target in ((t_ref[0] // 2, near_ref), (1 - t_ref[0] // 2, away_ref)):
        outward.start(o_s.at[pl.ds(pl.multiple_of(chip * (length // 2), length // 2), length // 2), :], target)
    outward.wait()


def attend(t, lens, gain, keep_parts, x_parts, wq, wk, wv):
    part, width = x_parts[0].shape
    length, cols = 4 * part, wq.shape[1]
    head_rows = sds((length, cols), bf16)
    scratch = [
        ((4, part, width), bf16),
        ((3, width, cols), bf16),
        ((length, width), bf16),
        *[((length, cols), bf16)] * 3,
        *[((4, length, cols), bf16)] * 2,
        ((length, cols), bf16),
        ((length, 128), f32),
        ((128, length), f32),
    ]
    return pl.pallas_call(
        attend_kernel,
        out_shape=(
            sds((length, width), bf16), *[head_rows] * 4, sds((length, 128), f32),
            *[sds((length // 2, cols), bf16)] * 2,
        ),
        in_specs=[SMEM] * 2 + [VMEM] * 5 + [ANY] * 7,
        out_specs=[ANY] * 8,
        scratch_shapes=[pltpu.VMEM(*s) for s in scratch]
        + [pltpu.SemaphoreType.DMA((7,)), pltpu.SemaphoreType.DMA((6 + 2 * (length // BLOCK),))],
        compiler_params=params(60),
        cost_estimate=cost(15, 15),
        name="attend",
    )(t, lens, gain, *keep_parts, *x_parts, wq, wk, wv)


def split3(value):
    high = value.astype(bf16)
    rest = value - high.astype(f32)
    middle = rest.astype(bf16)
    return high, middle, (rest - middle.astype(f32)).astype(bf16)


def attn_bwd_kernel(
    t_ref, lens_ref, p0, p1, p2, p3, q_ref, k_ref, v_ref, d0, d1, d2, d3, o_ref, l_ref,
    dq_ref, dk_ref, dv_ref, qm, km, dm, vm, do_ref, dq_acc, keep_s, *, pair,
):
    length = q_ref.shape[0]
    blocks = length // BLOCK
    zero = jnp.zeros((), bf16)
    minus = -jnp.ones((), bf16)
    for k, piece in enumerate((d0, d1, d2, d3)):
        do_ref[part_rows(t_ref, k, length // 4), :] = piece[...]
    add_q, add_k, keep_col, doc_col, _, doc_row = mask_terms(t_ref, lens_ref, (p0, p1, p2, p3), keep_s, 128)
    half = region((length, 128))
    ln = lanes((length, 128))
    both = do_ref[...].astype(f32) * o_ref[...].astype(f32)
    for h in range(2):
        a = (1 - h) * HEAD_DIM
        own = half == h
        high, middle, low = split3(l_ref[:, 2 * pair + h : 2 * pair + h + 1])
        extra = jnp.where(ln == a + 3, high, jnp.where(ln == a + 4, middle, jnp.where(ln == a + 5, low, add_q)))
        qm[h] = jnp.where(own, q_ref[...], extra)
        km[h] = jnp.where(own, k_ref[...], add_k)
        high, middle, low = split3(jnp.sum(jnp.where(own, both, 0.0), axis=1, keepdims=True))
        extra = jnp.where(ln == a, high, jnp.where(ln == a + 1, middle, jnp.where(ln == a + 2, low, zero)))
        dm[h] = jnp.where(own, do_ref[...], extra)
        vm[h] = jnp.where(own, v_ref[...], jnp.where((ln >= a) & (ln < a + 3), minus, zero))
    half_b = region((BLOCK, 128))
    ln_b = lanes((BLOCK, 128))
    ri = lax.broadcasted_iota(jnp.int32, (BLOCK, BLOCK), 0)
    ci = lax.broadcasted_iota(jnp.int32, (BLOCK, BLOCK), 1)
    dq_acc[...] = jnp.zeros(dq_acc.shape, f32)
    turned = [k_ref[BLOCK * j : BLOCK * (j + 1), :].T for j in range(blocks)]
    biases = []
    for j in range(blocks):
        here = slice(BLOCK * j, BLOCK * (j + 1))
        same = doc_col[here, :] == doc_row[:, here]
        seen = (ri == ci) | ((ri < ci) & (keep_col[here, :] > 0.5) & same)
        biases.append(jnp.where(seen, 0.0, NEG).astype(f32))

    def products(j, h):
        here, below = slice(BLOCK * j, BLOCK * (j + 1)), slice(BLOCK * (j + 1), length)
        a = (1 - h) * HEAD_DIM
        plain = jnp.where(half_b == h, k_ref[here, :], jnp.where((ln_b >= a + 3) & (ln_b < a + 6), minus, zero))
        got = [(here, dot(plain, qm[h, here, :], 1, 1), dot(vm[h, here, :], dm[h, here, :], 1, 1))]
        if j < blocks - 1:
            got.append((below, dot(km[h, here, :], qm[h, below, :], 1, 1), dot(vm[h, here, :], dm[h, below, :], 1, 1)))
        return got

    items = [(j, h) for j in range(blocks) for h in range(2)]
    ahead = products(*items[0])
    for n, (j, h) in enumerate(items):
        now, ahead = ahead, products(*items[n + 1]) if n + 1 < len(items) else None
        dk = dv = None
        for rows, s, dp in now:
            p = jnp.exp(s + biases[j] if rows.start == BLOCK * j else s)
            ds = (p * dp).astype(bf16)
            dk_part, dv_part = dot(ds, q_ref[rows, :]), dot(p.astype(bf16), do_ref[rows, :])
            dk, dv = (dk_part, dv_part) if dk is None else (dk + dk_part, dv + dv_part)
            dq_acc[h, :, rows] += dot(turned[j], ds)
        if h == 0:
            first = dk, dv
        else:
            here = slice(BLOCK * j, BLOCK * (j + 1))
            dk_ref[here, :] = jnp.where(half_b == 0, first[0], dk).astype(bf16)
            dv_ref[here, :] = jnp.where(half_b == 0, first[1], dv).astype(bf16)
    dq_ref[...] = (jnp.where(half == 0, dq_acc[0].T, dq_acc[1].T) * 0.125).astype(bf16)


def attend_back(t, lens, keep_parts, q, k, v, do_parts, o, log_norm, pair):
    length = q.shape[0]
    mine = pl.BlockSpec((length, 128), lambda i: (0, pair))
    mine_part = pl.BlockSpec((length // 4, 128), lambda i: (0, pair))
    return pl.pallas_call(
        functools.partial(attn_bwd_kernel, pair=pair),
        grid=(1,),
        out_shape=(sds((length, 128), bf16),) * 3,
        in_specs=[SMEM] * 2 + [VMEM] * 4 + [mine] * 3 + [mine_part] * 4 + [mine, VMEM],
        scratch_shapes=[pltpu.VMEM((2, length, 128), bf16)] * 4
        + [pltpu.VMEM((length, 128), bf16), pltpu.VMEM((2, 128, length), f32), pltpu.VMEM((128, length), f32)],
        compiler_params=params(60),
        cost_estimate=cost(0.1, 0.1),
        name="attend_back",
    )(t, lens, *keep_parts, q, k, v, *do_parts, o, log_norm)

def fetch_w_out(inward, t_ref, sources, target):
    started = [inward.start(w, target.at[u]) for u, w in enumerate(sources[:2])]
    half = target.shape[1] // 2
    few = half // INNER
    for u, (straight, blocks) in enumerate((sources[2:4], sources[4:6]), 2):
        started.append(inward.start(straight, target.at[u, :half, :]))
        for block in range(INNER):
            turn = t_ref[1] ^ block
            turn = (turn % 2) * 4 + turn // 2 % 2 * 2 + turn // 4
            rows = pl.ds(pl.multiple_of(turn * few, few), few)
            there = slice(half + block * few, half + (block + 1) * few)
            started.append(inward.start(blocks.at[rows, :], target.at[u, there, :]))
    return started


def send_pieces(outward, t_ref, pack, first, kept, given):
    half = pack.shape[0] // 2
    source, at = pack.at[pl.ds(first, 2)], pl.ds(first % half, 2)
    keep = t_ref[2] == first // half
    copies = outward.describe(source, kept.at[at]), outward.describe(source, given.at[at])
    pl.when(keep)(copies[0].start)
    pl.when(jnp.logical_not(keep))(copies[1].start)
    outward.add(copies[0])


def mlp_kernel(t_ref, gain_ref, o0, o1, o2, o3, w0, w1, w2, w3, w4, w5, *refs, order, last):
    (xa, xb), refs = refs[:2], refs[2:]
    dys, refs = refs[: 4 if last else 2], refs[4 if last else 2 :]
    (wg, wu, wd), refs = refs[:3], refs[3:]
    far, refs = refs[: 4 * last], refs[4 * last :]
    (fa, fb, ba, bb, b_low), refs = refs[:5], refs[5:]
    outs, refs = refs[:4], refs[4:]
    (o_s, w_s, x_s, y_s, wg_s, wu_s, wd_s, hn_s, act_s, dg_s, du_s, f_s, b_s), refs = refs[:13], refs[13:]
    (own_s, left, pack_s), refs = (refs[:3], refs[3:]) if last else ((None,) * 3, refs)
    inward, outward = Copies(refs[0]), Copies(refs[1])
    part = x_s.shape[1]
    hidden, width = wg_s.shape
    gain = gain_ref[...].astype(f32)
    slot = {k: i for i, k in enumerate(order)}
    blocks = {k: slice((k - min(order)) * part, (k - min(order) + 1) * part) for k in range(min(order), 4)}
    o_here = {}
    for k in order:
        rows = pl.ds(pl.multiple_of((t_ref[0] ^ k) % 2 * part, part), part)
        o_here[k] = [inward.start(o.at[rows, :], o_s.at[slot[k], u]) for u, o in enumerate((o0, o1, o2, o3))]
        o_here[k].append(inward.start((xa, xb)[slot[k]], x_s.at[slot[k]]))
        if slot[k] == 0:
            w_here = fetch_w_out(inward, t_ref, (w0, w1, w2, w3, w4, w5), w_s)
            rest = [inward.start(wg, wg_s), inward.start(wu, wu_s)]
    rest += [inward.start(dys[slot[k]], y_s.at[blocks[k], :]) for k in order]
    rest.append(inward.start(wd, wd_s))
    late = [inward.start(source, target.at[2 * part :, :]) for source, target in zip(far, (hn_s, act_s, dg_s, du_s))]
    late += [inward.start(dy, y_s.at[blocks[k], :]) for dy, k in zip(dys[2:], (3, 2))]
    totals, products = {}, {}

    def project_out(k):
        inward.wait(*o_here[k])
        totals[k] = x_s[slot[k]].astype(f32)
        for u in range(4):
            totals[k] = totals[k] + dot(o_s[slot[k], u], w_s[u])

    def norm(k):
        if k == 0:
            own_s[...] = totals[k]
            outward.start(own_s, outs[0])
        hn_s[blocks[k], :] = (totals[k] * rms_rows(totals[k]) * gain).astype(bf16)

    def forward(k):
        hn = hn_s[blocks[k], :]
        products[k] = (
            dot(hn, wg_s[...], 1, 1),
            dot(hn, wu_s[...], 1, 1),
            dot(y_s[blocks[k], :], wd_s[...], 1, 1).astype(bf16).astype(f32),
        )

    def activate(k):
        gate, up, dact = products[k]
        sig = 1.0 / (1.0 + jnp.exp(-gate))
        silu = gate * sig
        act_s[blocks[k], :] = (silu * up).astype(bf16)
        dg_s[blocks[k], :] = (dact * up * sig * (1.0 + gate * (1.0 - sig))).astype(bf16)
        du_s[blocks[k], :] = (dact * silu).astype(bf16)

    def backward(k):
        i = slot[k]
        b_s[i] = (dot(dg_s[blocks[k], :], wg_s[...]) + dot(du_s[blocks[k], :], wu_s[...])).astype(bf16)
        if k % 2:
            outward.start(b_s.at[i, : part // 2, :], ba)
            outward.start(b_s.at[i, part // 2 :, :], b_low)
        else:
            outward.start(b_s.at[i], (ba, bb)[i])
        f_s[i] = dot(act_s[blocks[k], :], wd_s[...]).astype(bf16)
        outward.start(f_s.at[i], (fa, fb)[i])
        if not last:
            for source, target in zip((hn_s, act_s, dg_s, du_s), outs):
                outward.start(source.at[blocks[k], :], target.at[blocks[k], :])

    one, two = order
    inward.wait(*w_here)
    project_out(one)
    project_out(two)
    inward.wait(*rest)
    norm(one)
    forward(one)
    norm(two)
    forward(two)
    activate(one)
    backward(one)
    activate(two)
    backward(two)
    if last:
        inward.wait(*late)
        for m, held, right in ((0, dg_s, hn_s), (1, du_s, hn_s), (2, act_s, y_s)):
            left[m % 2] = held[...].T
            for c in range(0, width, 256):
                cols = slice(c, c + 256)
                grad = dot(left[m % 2], right[:, cols])
                if m < 2:
                    sums = jnp.sum(grad * (wg_s, wu_s)[m][:, cols].astype(f32), axis=0, keepdims=True)
                    outs[3][:, cols] = sums if m == 0 else outs[3][:, cols] + sums
                grad = grad.astype(bf16)
                for b in range(2):
                    pack_s[c // 128 + b, m * hidden : (m + 1) * hidden, :] = grad[:, 128 * b : 128 * b + 128]
                if m == 2:
                    send_pieces(outward, t_ref, pack_s, c // 128, outs[1], outs[2])
    outward.wait()


def mlp(t, o_parts, w_parts, x_pair, dys, gain, wg, wu, wd, order, far=()):
    part, width = x_pair[0].shape
    hidden = wg.shape[0]
    last = bool(far)
    held = (4 if last else 2) * part
    block, half_block, inner = (sds(s, bf16) for s in ((part, width), (part // 2, width), (2 * part, hidden)))
    pack = (width // 128, 3 * hidden, 128)
    scratch = [
        ((2, 4, part, o_parts[0].shape[1]), bf16),
        ((4,) + w_parts[0].shape, bf16),
        ((2, part, width), bf16),
        ((held, width), bf16),
        *[((hidden, width), bf16)] * 3,
        ((held, width), bf16),
        *[((held, hidden), bf16)] * 3,
        ((2, part, width), bf16),
        ((2, part, width), bf16),
    ]
    if last:
        scratch += [((part, width), f32), ((2, hidden, held), bf16), (pack, bf16)]
        half = sds((pack[0] // 2,) + pack[1:], bf16)
        out = [sds((part, width), f32), half, half, sds((1, width), f32)]
    else:
        out = [sds((2 * part, width), bf16), inner, inner, inner]
    return pl.pallas_call(
        functools.partial(mlp_kernel, order=order, last=last),
        out_shape=(block, block, half_block, block, half_block, *out),
        in_specs=[SMEM, VMEM] + [ANY] * (15 + len(dys) + len(far)),
        out_specs=[ANY] * 8 + [VMEM if last else ANY],
        scratch_shapes=[pltpu.VMEM(*s) for s in scratch]
        + [pltpu.SemaphoreType.DMA((48,)), pltpu.SemaphoreType.DMA((16,))],
        compiler_params=params(61),
        cost_estimate=cost(25 if last else 14, 25),
        name="mlp",
    )(t, gain, *o_parts, *w_parts, *x_pair, *dys, wg, wu, wd, *far)


def unpack_kernel(idx, *refs, shapes, more, strands):
    n = len(shapes)
    given = INNER * strands
    pieces, outs, refs = refs[:given], refs[given : given + n], refs[given + n :]
    if more:
        more_ref, refs = refs[0], refs[1:]
    held, stages, inward, outward = refs[0], refs[1 : n + 1], Copies(refs[n + 1]), Copies(refs[n + 2])
    high = held.shape[1] // strands
    here = [
        inward.start(piece, held.at[i // strands, high * (i % strands) : high * (i % strands + 1), :])
        for i, piece in enumerate(pieces)
    ]
    for j in range(INNER):
        inward.wait(*here[j * strands : (j + 1) * strands])
        at = pl.ds(pl.multiple_of(idx[j] * 128, 128), 128)
        top = 0
        for (rows, width), out, stage in zip(shapes, outs, stages):
            whole = width == 128 * INNER
            for b in range(1 if whole else width // 128):
                high_b = rows if whole else 128
                stage[j, :, 128 * b : 128 * b + 128] = held[j, top : top + high_b, :].astype(f32)
                top += high_b
            outward.start(stage.at[j], out.at[:, at] if whole else out.at[at, :])
        if more:
            more_ref[:, at] = held[j, top:, :].astype(f32)
    outward.wait()


def unpack(idx, pieces, strands, shapes, name, more=0):
    stages = [(INNER, r, 128) if w == 128 * INNER else (INNER, 128, w) for r, w in shapes]
    held = (INNER, sum(s[1] * s[2] for s in stages) // 128 + more, 128)
    return pl.pallas_call(
        functools.partial(unpack_kernel, shapes=shapes, more=more, strands=strands),
        out_shape=tuple(sds(s, f32) for s in shapes) + (sds((more, 128 * INNER), f32),) * bool(more),
        in_specs=[SMEM] + [ANY] * len(pieces),
        out_specs=[ANY] * len(shapes) + [VMEM] * bool(more),
        scratch_shapes=[pltpu.VMEM(held, bf16)]
        + [pltpu.VMEM(s, f32) for s in stages]
        + [pltpu.SemaphoreType.DMA((len(pieces),)), pltpu.SemaphoreType.DMA((INNER * len(shapes),))],
        compiler_params=params(60),
        cost_estimate=cost(0.1, 0.1),
        name=name,
    )(idx, *pieces)


def hidden_back_kernel(
    t_ref, gain_ref, b0, b1, b2, b3, h_ref, dy_ref, w0, w1, w2, w3, w4, w5, dh_ref, da_ref, d0, d1, d2, d3,
    b_s, h_s, dy_s, w_s, dh_s, da_s, d_s, in_sems, out_sems,
):
    inward, outward = Copies(in_sems), Copies(out_sems)
    part = dh_s.shape[0]
    halves = [slice(0, part // 2), slice(part // 2, part)]
    here = [inward.start(b, b_s.at[i]) for i, b in ((0, b0), (2, b3))]
    here += [inward.start(b, b_s.at[1, rows, :]) for b, rows in zip((b1, b2), halves)]
    here += [inward.start(h_ref, h_s), inward.start(dy_ref, dy_s)]
    w_here = fetch_w_out(inward, t_ref, (w0, w1, w2, w3, w4, w5), w_s)
    inward.wait(*(here + w_here))
    for rows in halves:
        dhn = b_s[0, rows, :].astype(f32) + b_s[1, rows, :].astype(f32) + b_s[2, rows, :].astype(f32)
        hidden = h_s[rows, :]
        inv = rms_rows(hidden)
        weighted = dhn * gain_ref[...].astype(f32)
        inner = jnp.mean(weighted * hidden, axis=-1, keepdims=True)
        dh = dy_s[rows, :].astype(f32) + inv * weighted - hidden * (inv * inv * inv) * inner
        dh_s[rows, :] = dh
        da_s[rows, :] = dh.astype(bf16)
        for u in (2, 3, 1, 0):
            d_s[u, rows, :] = dot(da_s[rows, :], w_s[u], 1, 1).astype(bf16)
    for u, d in ((2, d2), (3, d3), (1, d1), (0, d0)):
        outward.start(d_s.at[u], d)
    outward.start(dh_s, dh_ref)
    outward.start(da_s, da_ref)
    outward.wait()


def hidden_back(t, sums, h_own, dy_own, gain, w_parts):
    part, width = h_own.shape
    cols = w_parts[0].shape[0]
    scratch = [
        ((3, part, width), bf16), ((part, width), f32), ((part, width), bf16), ((4, cols, width), bf16),
        ((part, width), f32), ((part, width), bf16), ((4, part, cols), bf16),
    ]
    return pl.pallas_call(
        hidden_back_kernel,
        out_shape=(sds((part, width), f32), sds((part, width), bf16)) + (sds((part, cols), bf16),) * 4,
        in_specs=[SMEM, VMEM] + [ANY] * 12,
        out_specs=[ANY] * 6,
        scratch_shapes=[pltpu.VMEM(*s) for s in scratch]
        + [pltpu.SemaphoreType.DMA((6 + 4 + 2 * INNER,)), pltpu.SemaphoreType.DMA((6,))],
        compiler_params=params(60),
        cost_estimate=cost(60, 10),
        name="hidden_back",
    )(t, gain, *sums, h_own, dy_own, *w_parts)


def tokens_back_kernel(
    t_ref, dq0, dq1, dk0, dk1, dv0, dv1, wq, wk, wv, b0, b1, b2, b3, d_s, w_s, b_s, in_sems, out_sems
):
    inward, outward = Copies(in_sems), Copies(out_sems)
    part = b_s.shape[1]
    for m, pair in enumerate(((dq0, dq1), (dk0, dk1), (dv0, dv1))):
        for b, d in enumerate(pair):
            inward.start(d, d_s.at[m, :, 128 * b : 128 * b + 128])
    for m, w in enumerate((wq, wk, wv)):
        inward.start(w, w_s.at[m])
    inward.wait()
    for k, out in ((3, b3), (2, b2), (1, b1), (0, b0)):
        rows = part_rows(t_ref, k, part)
        b_s[k] = sum(dot(d_s[m, rows, :], w_s[m], 1, 1) for m in range(3)).astype(bf16)
        outward.start(b_s.at[k], out)
    outward.wait()


def tokens_back(t, head_parts, wq, wk, wv):
    length, (width, cols) = head_parts[0].shape[0], wq.shape
    scratch = [(3, length, cols), (3, width, cols), (4, length // 4, width)]
    return pl.pallas_call(
        tokens_back_kernel,
        out_shape=(sds((length // 4, width), bf16),) * 4,
        in_specs=[SMEM] + [ANY] * 9,
        out_specs=[ANY] * 4,
        scratch_shapes=[pltpu.VMEM(s, bf16) for s in scratch]
        + [pltpu.SemaphoreType.DMA((9,)), pltpu.SemaphoreType.DMA((4,))],
        compiler_params=params(60),
        cost_estimate=cost(0.1, 0.1),
        name="tokens_back",
    )(t, *head_parts, wq, wk, wv)


def head_grads_kernel(
    t_ref, other_ref, xn_ref, o_ref, a0, a1, a2, a3, dq0, dq1, dk0, dk1, dv0, dv1, wq, wk, wv, out_ref,
    xn_s, o_s, a_s, d_s, w_s, left, left_o, pack_s, in_sems, out_sems,
):
    length, width = xn_s.shape
    part = length // 4
    cols = o_s.shape[1]
    inward, outward = Copies(in_sems), Copies(out_sems)
    halves = [slice(0, width // 2), slice(width // 2, width)]
    xn_here = [inward.start(xn_ref.at[:, halves[0]], xn_s.at[:, halves[0]])]
    here = [
        inward.start(d, d_s.at[m, :, 128 * b : 128 * b + 128])
        for m, pair in enumerate(((dq0, dq1), (dk0, dk1), (dv0, dv1)))
        for b, d in enumerate(pair)
    ]
    here += [inward.start(w, w_s.at[m]) for m, w in enumerate((wq, wk, wv))]
    xn_here.append(inward.start(xn_ref.at[:, halves[1]], xn_s.at[:, halves[1]]))
    o_here = [inward.start(o_ref, o_s)]
    o_here += [inward.start(a, a_s.at[part_rows(t_ref, k, part), :]) for k, a in enumerate((a0, a1, a2, a3))]
    for i, rows in enumerate(halves):
        inward.wait(xn_here[i])
        left[rows, :] = xn_s[:, rows].T
        if i == 0:
            inward.wait(*here)
        by_row = jnp.zeros((width // 2, cols), f32)
        for m in range(3):
            grad = dot(left[rows, :], d_s[m])
            by_row = by_row + grad * w_s[m, rows, :].astype(f32)
            for piece in range(width // 256):
                for b in range(cols // 128):
                    at = m * cols + 128 * b
                    pack_s[rows.start // 128 + piece, at : at + 128, :] = grad[
                        128 * piece : 128 * piece + 128, 128 * b : 128 * b + 128
                    ].astype(bf16)
        sums = lax.dot_general(
            jnp.ones((8, cols), f32), by_row, (((1,), (1,)), ((), ())),
            precision=lax.Precision.HIGHEST, preferred_element_type=f32,
        )
        for piece in range(width // 256):
            at = rows.start // 128 + piece
            others = jnp.broadcast_to(other_ref[:, 128 * at : 128 * at + 128], (8, 128))
            both = jnp.concatenate([sums[:, 128 * piece : 128 * piece + 128], others], axis=0)
            pack_s[at, 4 * cols :, :] = both.astype(bf16)
    inward.wait(*o_here)
    left_o[...] = o_s[...].T
    for c in range(0, width, 256):
        grad = dot(left_o[...], a_s[:, c : c + 256]).astype(bf16)
        for b in range(2):
            pack_s[c // 128 + b, 3 * cols : 4 * cols, :] = grad[:, 128 * b : 128 * b + 128]
        two = pl.ds(c // 128, 2)
        outward.start(pack_s.at[two], out_ref.at[two])
    outward.wait()


def head_grads(t, other_gain, xn, o, da_parts, head_parts, wq, wk, wv):
    length, width = xn.shape
    cols = o.shape[1]
    scratch = [
        (length, width), (length, cols), (length, width), (3, length, cols), (3, width, cols),
        (width, length), (cols, length), (width // 128, 4 * cols + 16, 128),
    ]
    return pl.pallas_call(
        head_grads_kernel,
        out_shape=sds((width // 128, 4 * cols + 16, 128), bf16),
        in_specs=[SMEM, VMEM] + [ANY] * 15,
        out_specs=ANY,
        scratch_shapes=[pltpu.VMEM(s, bf16) for s in scratch]
        + [pltpu.SemaphoreType.DMA((16,)), pltpu.SemaphoreType.DMA((4,))],
        compiler_params=params(60),
        cost_estimate=cost(0.1, 0.1),
        name="head_grads",
    )(t, other_gain, xn, o, *da_parts, *head_parts, wq, wk, wv)


def add_kernel(*refs, count):
    terms, out_ref, held, out_s, sems = refs[:count], refs[count], refs[count + 1 : -2], refs[-2], refs[-1]
    copies = Copies(sems)
    for term, target in zip(terms, held):
        copies.start(term, target)
    copies.wait()
    out_s[...] = sum(target[...].astype(f32) for target in held).astype(bf16)
    copies.start(out_s, out_ref)
    copies.wait()


def add(*terms):
    shape = terms[0].shape
    return pl.pallas_call(
        functools.partial(add_kernel, count=len(terms)),
        out_shape=sds(shape, bf16),
        in_specs=[ANY] * len(terms),
        out_specs=ANY,
        scratch_shapes=[pltpu.VMEM(shape, term.dtype) for term in terms]
        + [pltpu.VMEM(shape, bf16), pltpu.SemaphoreType.DMA((len(terms) + 1,))],
        compiler_params=params(60),
        cost_estimate=cost(0.1, 0.1),
        name="add",
    )(*terms)


def tokens_end_kernel(gain_ref, d0, d1, d2, dh_ref, x_ref, out_ref, d_s, dh_s, x_s, out_s, sems):
    copies = Copies(sems)
    for i, d in enumerate((d0, d1, d2)):
        copies.start(d, d_s.at[i])
    copies.start(dh_ref, dh_s)
    copies.start(x_ref, x_s)
    copies.wait()
    x = x_s[...].astype(f32)
    inv = rms_rows(x)
    weighted = (d_s[0].astype(f32) + d_s[1].astype(f32) + d_s[2].astype(f32)) * gain_ref[...].astype(f32)
    inner = jnp.mean(weighted * x, axis=-1, keepdims=True)
    out_s[...] = (dh_s[...] + inv * weighted - x * (inv * inv * inv) * inner).astype(bf16)
    copies.start(out_s, out_ref)
    copies.wait()


def tokens_end(gain, terms, dh, x):
    shape = x.shape
    return pl.pallas_call(
        tokens_end_kernel,
        out_shape=sds(shape, bf16),
        in_specs=[VMEM] + [ANY] * 5,
        out_specs=ANY,
        scratch_shapes=[
            pltpu.VMEM((3, *shape), bf16), pltpu.VMEM(shape, f32), pltpu.VMEM(shape, bf16), pltpu.VMEM(shape, bf16),
            pltpu.SemaphoreType.DMA((6,)),
        ],
        compiler_params=params(60),
        cost_estimate=cost(0.1, 0.1),
        name="tokens_end",
    )(gain, *terms, dh, x)


def swap(value, k):
    return lax.ppermute(value, "tensor", [(i, i ^ k) for i in range(4)])


def spread(own):
    far = swap(own, 2)
    return own, swap(own, 1), far, swap(far, 1)


def double(value, bit, dp):
    return jnp.concatenate([value, lax.ppermute(value, "dp", [(i, i ^ bit) for i in range(dp)])], axis=0)


class Ring:
    order = (0, 2, 4, 6, 7, 5, 3, 1)

    def __init__(self, dp):
        self.dp = dp
        self.member, self.core = lax.axis_index("dp") % INNER, lax.axis_index("tensor") % 2
        self.way = 1 - 2 * self.core
        self.place = jnp.where(self.member % 2 == 0, self.member // 2, INNER - 1 - self.member // 2)

    def side(self, step):
        return self.member >> ((step + self.core) % 3) & 1

    def send(self, value, target):
        pairs = [
            (4 * (g + d) + t, 4 * (g + target(d, t % 2)) + t)
            for g in range(0, self.dp, INNER)
            for d in range(INNER)
            for t in range(4)
        ]
        return lax.ppermute(value, ("dp", "tensor"), pairs)

    def pass_on(self, value):
        return self.send(value, lambda d, c: self.order[(self.order.index(d) + 1 - 2 * c) % INNER])


def rounded_sum(one, two):
    return (one.astype(f32) + two.astype(f32)).astype(bf16)


class Sum:
    def __init__(self, ring, strands):
        self.ring, self.step = ring, 0
        self.pieces = [[] for _ in range(strands)]

    def advance(self, *before):
        ring, strands = self.ring, len(self.pieces)
        self.step += 1
        arrived = pin(self.on_way.pop(0), *before)
        if self.step < self.adds:
            return self.next_add(arrived)
        if self.step == self.adds:
            arrived = rounded_sum(arrived, self.mine)
        if self.step == self.adds:
            arrived = arrived.reshape(arrived.shape[-2:])
            if ring.dp > INNER:
                groups = [[g + d for g in range(0, ring.dp, INNER)] for d in range(INNER)]
                arrived = lax.psum(arrived, "dp", axis_index_groups=groups)
            rows = arrived.shape[0] // strands
            for s, held in enumerate(self.pieces):
                held.append(arrived[s * rows : (s + 1) * rows])
                self.on_way.append(ring.pass_on(held[0]))
        else:
            held = self.pieces[(self.step - self.adds - 1) % strands]
            held.append(arrived)
            if len(held) < INNER:
                self.on_way.append(ring.pass_on(arrived))
        return arrived

    @property
    def done(self):
        return not self.on_way

    def result(self):
        return [piece for arrived in zip(*self.pieces) for piece in arrived]


class RingSum(Sum):
    adds = INNER - 1

    def __init__(self, ring, packed, strands):
        super().__init__(ring, strands)
        self.packed = packed
        self.on_way = [ring.pass_on(self.piece(0))]
        self.mine = self.piece(1)

    def piece(self, step):
        number = (self.ring.place - step * self.ring.way) % INNER
        return lax.dynamic_index_in_dim(self.packed, number, 0, keepdims=False)

    def next_add(self, arrived):
        arrived = rounded_sum(arrived, self.mine)
        self.on_way = [self.ring.pass_on(arrived)]
        self.mine = self.piece(self.step + 1)
        return arrived

    def numbers(self):
        steps = lax.iota(jnp.int32, INNER) + INNER - 1
        return (self.ring.place - steps * self.ring.way) % INNER


class HalvingSum(Sum):
    adds = 3

    def __init__(self, ring, kept, given, strands):
        super().__init__(ring, strands)
        self.mine, self.on_way = kept, [self.give(given)]

    def give(self, value):
        step = self.step
        return self.ring.send(value, lambda d, c: d ^ 1 << (step + c) % 3)

    def next_add(self, arrived):
        side = self.ring.side(self.step)
        given, kept = [
            rounded_sum(*[
                lax.dynamic_index_in_dim(part.reshape(2, -1, *part.shape[-2:]), half, 0, keepdims=False)
                for part in (arrived, self.mine)
            ])
            for half in (1 - side, side)
        ]
        self.mine, self.on_way = kept, [self.give(given)]
        return given

    def numbers(self):
        ring = self.ring
        places = (ring.place - lax.iota(jnp.int32, INNER) * ring.way) % INNER
        members = jnp.where(places < INNER // 2, 2 * places, 2 * INNER - 1 - 2 * places)
        return sum((members >> ((step + ring.core) % 3) & 1) << (2 - step) for step in range(3))


def pin(value, *before):
    return lax.optimization_barrier((value, *before))[0]


def per_device(
    dp, tokens, gain_attn, w_query, w_key, w_value, w_out, gain_mlp, w_gate, w_up, w_down, doc_lens, pad_mask, cotangent
):
    ring = Ring(dp)
    t = jnp.stack([lax.axis_index("tensor"), ring.member, ring.side(0)]).astype(jnp.int32)
    width, hidden = w_gate.shape
    cols = w_query.shape[1]
    gain_one = gain_attn.reshape(1, width)
    gain_two = gain_mlp.reshape(1, width)
    gate_t, up_t = w_gate.T, w_up.T

    half = w_out.shape[0] // 2
    few = half // INNER
    w_share = lax.dynamic_slice_in_dim(w_out, half + ring.member * few, few, 0)
    w_half = w_out[:half]
    keep_parts = spread(pin(pad_mask.reshape(1, -1), gain_one, gain_two, t, w_share, w_half))
    w_first, w_straight = swap(w_share, 2), swap(w_half, 2)
    x_far = pin(swap(tokens, 2), keep_parts[2])
    x_parts = tokens, swap(tokens, 1), x_far, swap(x_far, 1)
    dy_parts = spread(cotangent)

    xn, q, k, v, o, log_norm, o_near, o_away = attend(t, doc_lens, gain_one, keep_parts, x_parts, w_query, w_key, w_value)
    dy_parts = spread(cotangent)
    near, away = spread(pin(o_near, dy_parts[2], w_first, w_straight)), spread(o_away)
    w_far = pin(w_first, o_near)
    for bit in (4, 2, 1):
        w_far = double(w_far, bit, dp)
    w_parts = w_out, swap(w_out, 1), w_straight, w_far, swap(w_straight, 1), swap(w_far, 1)

    weights = gain_two, gate_t, up_t, w_down
    f3, f2, b3_high, b2, b3_low, *far = mlp(
        t, (*away[:2], *near[2:]), w_parts, (x_parts[3], x_parts[2]), (dy_parts[3], dy_parts[2]), *weights, (3, 2)
    )
    passed = rounded_sum(b2, jnp.concatenate([swap(b3_high, 1), swap(b3_low, 1)], axis=0))
    f1, f0, b1_high, b0, b1_low, h_own, kept, given, gain_two_sum = mlp(
        t, (*near[:2], *away[2:]), w_parts, (x_parts[1], pin(x_parts[0], passed)), dy_parts[1::-1] + dy_parts[:1:-1], *weights, (1, 0), far
    )
    sum_mlp = HalvingSum(ring, kept, given, 2)
    sums = (b0, swap(b1_high, 1), swap(b1_low, 1), swap(passed, 2))
    dh, da, *do_parts = hidden_back(t, sums, h_own, cotangent, gain_two, w_parts)
    do_parts = [do_parts[0]] + [swap(do_parts[i], i) for i in range(1, 4)]
    ffn_passed = add(f2, swap(f3, 1))
    da_far = swap(pin(da, do_parts[2], do_parts[3], ffn_passed), 2)
    pairs = [attend_back(t, doc_lens, keep_parts, q, k, v, do_parts, o, log_norm, 0)]
    step = sum_mlp.advance(pairs[0][0])
    pairs.append(attend_back(t, doc_lens, keep_parts, pin(q, step), k, v, do_parts, o, log_norm, 1))
    da_far = pin(da_far, pairs[1][0])
    da_parts = da, swap(da, 1), da_far, swap(da_far, 1)
    head_parts = [pairs[p][m] for m in range(3) for p in range(2)]
    ffn_terms = f0, swap(f1, 1), swap(pin(ffn_passed, da_far), 2)
    packed = head_grads(t, gain_two_sum, xn, o, da_parts, head_parts, w_query, w_key, w_value)
    sum_head = RingSum(ring, packed, 1)
    step = sum_mlp.advance(packed)

    def back(step):
        out["dx"] = tokens_back(t, [pin(head_parts[0], step), *head_parts[1:]], w_query, w_key, w_value)
        out["across"] = swap(out["dx"][3], 1)
        return out["dx"][0]

    def pass_on(step):
        dx = out["dx"]
        passed = add(pin(dx[2], step), out["across"])
        out["dxn"] = dx[0], swap(dx[1], 1), swap(passed, 2)
        return passed

    def finish_output(step):
        out["y"] = add(h_own, *[pin(term, step) for term in ffn_terms])
        return out["y"]

    def finish_tokens(step):
        out["dx"] = tokens_end(gain_one, [pin(term, step) for term in out["dxn"]], dh, tokens)
        return out["dx"]

    out = {}
    tasks = [back, pass_on, finish_output, *[None] * 4, finish_tokens]
    while not (sum_mlp.done and sum_head.done):
        if not sum_head.done:
            step = sum_head.advance(step)
        for _ in range(2 if sum_head.step >= 4 and sum_head.step % 2 == 0 else 1):
            if not sum_mlp.done and sum_head.step != 1:
                step = sum_mlp.advance(step)
        if tasks:
            task = tasks.pop(0)
            step = task(step) if task else step
    grad_query, grad_key, grad_value, grad_out, gains = unpack(
        sum_head.numbers(), sum_head.result(), 1, ((width, cols),) * 3 + ((cols, width),), "head_unpack", 16
    )
    first, *others = sum_mlp.result()
    grad_gate, grad_up, grad_down = unpack(
        sum_mlp.numbers(), [pin(first, gains), *others], 2, ((hidden, width),) * 3, "mlp_unpack"
    )
    others = [pin(swap(gains, k), grad_gate) for k in range(1, 4)]
    gains = (gains + others[0]) + (others[1] + others[2])
    output, grad_tokens = out["y"], out["dx"]
    grad_gain_attn, grad_gain_mlp = gains[0] / gain_attn.astype(f32), gains[8] / gain_mlp.astype(f32)
    return (
        output, grad_tokens, grad_gain_attn, grad_query, grad_key, grad_value, grad_out, grad_gain_mlp,
        grad_gate.T, grad_up.T, grad_down,
    )


def solution(mesh):
    rows = P(("dp", "tensor"), None)
    columns = P(None, "tensor")
    shares = P("tensor", None)
    return jax.shard_map(
        functools.partial(per_device, mesh.shape["dp"]),
        mesh=mesh,
        in_specs=(
            rows, P(), columns, columns, columns, shares, P(), columns, columns, shares,
            P("dp", None), P(("dp", "tensor")), rows,
        ),
        out_specs=(rows, rows, P(), columns, columns, columns, shares, P(), columns, columns, shares),
        check_vma=False,
    )
```

```python
import functools

import jax
import jax.numpy as jnp
from jax import lax
from jax.experimental import pallas as pl
from jax.experimental.pallas import tpu as pltpu
from jax.sharding import PartitionSpec as P

HEAD_DIM = 64
EPS = 1e-05
NEG = -1e30
BLOCK = 256
INNER = 8
bf16 = jnp.bfloat16
f32 = jnp.float32
MIB = 2**20


def dot(a, b, ca=1, cb=0):
    return lax.dot_general(a, b, (((ca,), (cb,)), ((), ())), preferred_element_type=f32)


def params(limit_mib):
    return pltpu.CompilerParams(vmem_limit_bytes=limit_mib * MIB)


def cost(gflop, mbytes):
    return pl.CostEstimate(
        flops=int(gflop * 1e9), bytes_accessed=int(mbytes * 1e6), transcendentals=0
    )


def sds(shape, dtype):
    return jax.ShapeDtypeStruct(shape, dtype)


SMEM = pl.BlockSpec(memory_space=pltpu.SMEM)
VMEM = pl.BlockSpec(memory_space=pltpu.VMEM)
ANY = pl.BlockSpec(memory_space=pl.ANY)

def region(shape):
    return lax.broadcasted_iota(jnp.int32, shape, 1) // HEAD_DIM


def lanes(shape):
    return lax.broadcasted_iota(jnp.int32, shape, 1)


def part_rows(t_ref, k, part):
    return pl.ds(pl.multiple_of((t_ref[0] ^ k) * part, part), part)


def mask_terms(t_ref, lens_ref, keep_refs, keep_row, width=256):
    length = keep_row.shape[1]
    part = length // 4
    keep_row[...] = jnp.zeros(keep_row.shape, f32)
    for k, piece in enumerate(keep_refs):
        keep_row[0:1, part_rows(t_ref, k, part)] = jnp.where(piece[...] == 1, 1.0, 0.0)
    keep_col = keep_row[...].T[:, 0:1]
    end = lens_ref[0, 0]
    doc_col = jnp.where(lax.broadcasted_iota(jnp.int32, (length, 1), 0) >= end, 1.0, 0.0)
    doc_row = jnp.where(lax.broadcasted_iota(jnp.int32, (1, length), 1) >= end, 1.0, 0.0)
    lane = lanes((length, width)) % HEAD_DIM
    add_q = jnp.where(lane == 0, 1.0 - doc_col, jnp.where(lane == 1, doc_col, jnp.where(lane == 2, 1.0, 0.0)))
    hide = jnp.where(lane == 0, doc_col, jnp.where(lane == 1, 1.0 - doc_col, 1.0 - keep_col))
    add_k = jnp.where(lane < 3, hide * NEG, jnp.where(lane < 6, -1.0, 0.0))
    return add_q.astype(bf16), add_k.astype(bf16), keep_col, doc_col, keep_row[0:1, :], doc_row


def rms_rows(values):
    return lax.rsqrt(jnp.mean(values * values, axis=-1, keepdims=True) + EPS)


class Copies:
    def __init__(self, sems):
        self.sems = sems
        self.count = 0
        self.flying = {}

    def describe(self, source, target):
        return pltpu.make_async_copy(source, target, self.sems.at[self.count])

    def add(self, copy):
        self.flying[id(copy)] = copy
        self.count += 1
        return copy

    def start(self, source, target):
        copy = self.describe(source, target)
        copy.start()
        return self.add(copy)

    def wait(self, *copies):
        for copy in copies or tuple(self.flying.values()):
            self.flying.pop(id(copy)).wait()


def attend_kernel(
    t_ref, lens_ref, gain_ref, p0, p1, p2, p3, x0, x1, x2, x3, wq, wk, wv,
    xn_ref, q_ref, k_ref, v_ref, o_ref, l_ref, near_ref, away_ref,
    x_s, w_s, xn_s, q_s, k_s, v_s, qm, km, o_s, l_s, keep_s, in_sems, out_sems,
):
    length = q_s.shape[0]
    part = length // 4
    zero = jnp.zeros((), bf16)
    inward, outward = Copies(in_sems), Copies(out_sems)
    gain = gain_ref[...].astype(f32)
    arrived = [inward.start(x0, x_s.at[0])]
    arrived += [inward.start(w, w_s.at[m]) for m, w in enumerate((wq, wk, wv))]
    arrived += [inward.start(x, x_s.at[1 + i]) for i, x in enumerate((x1, x2, x3))]
    add_q, add_k, _, doc_col, keep_row, doc_row = mask_terms(t_ref, lens_ref, (p0, p1, p2, p3), keep_s)
    inward.wait(*arrived[:4])
    for k in range(4):
        if k > 0:
            inward.wait(arrived[3 + k])
        rows = part_rows(t_ref, k, part)
        x = x_s[k].astype(f32)
        xn = (x * rms_rows(x) * gain).astype(bf16)
        xn_s[rows, :] = xn
        q_s[rows, :] = (dot(xn, w_s[0]).astype(bf16).astype(f32) * 0.125).astype(bf16)
        k_s[rows, :] = dot(xn, w_s[1]).astype(bf16)
        v_s[rows, :] = dot(xn, w_s[2]).astype(bf16)
    for source, target in ((xn_s, xn_ref), (q_s, q_ref), (k_s, k_ref), (v_s, v_ref)):
        outward.start(source, target)
    reg = region((length, 256))
    for h in range(4):
        following = (h + 1) % 4
        qm[h] = jnp.where(reg == h, q_s[...], jnp.where(reg == following, add_q, zero))
        km[h] = jnp.where(reg == h, k_s[...], add_k)
    reg_b = region((BLOCK, 256))
    ri = lax.broadcasted_iota(jnp.int32, (BLOCK, BLOCK), 0)
    ci = lax.broadcasted_iota(jnp.int32, (BLOCK, BLOCK), 1)
    ln = lanes((BLOCK, 128))
    for i in range(length // BLOCK):
        r0 = i * BLOCK
        here = slice(r0, r0 + BLOCK)
        same = doc_col[here, :] == doc_row[:, here]
        seen = (ri == ci) | ((ci < ri) & (keep_row[:, here] > 0.5) & same)
        bias = jnp.where(seen, 0.0, NEG).astype(f32)
        o_acc = jnp.zeros((BLOCK, 256), f32)
        l_acc = jnp.zeros((BLOCK, 128), f32)
        for h in range(4):
            qh = qm[h, here, :]
            plain = jnp.where(reg_b == h, qh, zero)
            s_diag = dot(plain, k_s[here, :], 1, 1) + bias
            top = jnp.max(s_diag, axis=1, keepdims=True)
            if i > 0:
                s_left = dot(qh, km[h, 0:r0, :], 1, 1)
                top = jnp.maximum(top, jnp.max(s_left, axis=1, keepdims=True))
            p_diag = jnp.exp(s_diag - top)
            total = jnp.sum(p_diag, axis=1, keepdims=True)
            acc = dot(p_diag.astype(bf16), v_s[here, :])
            if i > 0:
                p_left = jnp.exp(s_left - top)
                total = total + jnp.sum(p_left, axis=1, keepdims=True)
                acc = acc + dot(p_left.astype(bf16), v_s[0:r0, :])
            o_acc = jnp.where(reg_b == h, acc * (1.0 / total), o_acc)
            l_acc = jnp.where(ln == h, top + jnp.log(total), l_acc)
        o_s[here, :] = o_acc.astype(bf16)
        l_s[here, :] = l_acc
        outward.start(o_s.at[here, :], o_ref.at[here, :])
        outward.start(l_s.at[here, :], l_ref.at[here, :])
    for chip, target in ((t_ref[0] // 2, near_ref), (1 - t_ref[0] // 2, away_ref)):
        outward.start(o_s.at[pl.ds(pl.multiple_of(chip * (length // 2), length // 2), length // 2), :], target)
    outward.wait()


def attend(t, lens, gain, keep_parts, x_parts, wq, wk, wv):
    part, width = x_parts[0].shape
    length, cols = 4 * part, wq.shape[1]
    head_rows = sds((length, cols), bf16)
    scratch = [
        ((4, part, width), bf16),
        ((3, width, cols), bf16),
        ((length, width), bf16),
        *[((length, cols), bf16)] * 3,
        *[((4, length, cols), bf16)] * 2,
        ((length, cols), bf16),
        ((length, 128), f32),
        ((128, length), f32),
    ]
    return pl.pallas_call(
        attend_kernel,
        out_shape=(
            sds((length, width), bf16), *[head_rows] * 4, sds((length, 128), f32),
            *[sds((length // 2, cols), bf16)] * 2,
        ),
        in_specs=[SMEM] * 2 + [VMEM] * 5 + [ANY] * 7,
        out_specs=[ANY] * 8,
        scratch_shapes=[pltpu.VMEM(*s) for s in scratch]
        + [pltpu.SemaphoreType.DMA((7,)), pltpu.SemaphoreType.DMA((6 + 2 * (length // BLOCK),))],
        compiler_params=params(60),
        cost_estimate=cost(15, 15),
        name="attend",
    )(t, lens, gain, *keep_parts, *x_parts, wq, wk, wv)


def split3(value):
    high = value.astype(bf16)
    rest = value - high.astype(f32)
    middle = rest.astype(bf16)
    return high, middle, (rest - middle.astype(f32)).astype(bf16)


def attn_bwd_kernel(
    t_ref, lens_ref, p0, p1, p2, p3, q_ref, k_ref, v_ref, d0, d1, d2, d3, o_ref, l_ref,
    dq_ref, dk_ref, dv_ref, qm, km, dm, vm, do_ref, dq_acc, keep_s, *, pair,
):
    length = q_ref.shape[0]
    blocks = length // BLOCK
    zero = jnp.zeros((), bf16)
    minus = -jnp.ones((), bf16)
    for k, piece in enumerate((d0, d1, d2, d3)):
        do_ref[part_rows(t_ref, k, length // 4), :] = piece[...]
    add_q, add_k, keep_col, doc_col, _, doc_row = mask_terms(t_ref, lens_ref, (p0, p1, p2, p3), keep_s, 128)
    half = region((length, 128))
    ln = lanes((length, 128))
    both = do_ref[...].astype(f32) * o_ref[...].astype(f32)
    for h in range(2):
        a = (1 - h) * HEAD_DIM
        own = half == h
        high, middle, low = split3(l_ref[:, 2 * pair + h : 2 * pair + h + 1])
        extra = jnp.where(ln == a + 3, high, jnp.where(ln == a + 4, middle, jnp.where(ln == a + 5, low, add_q)))
        qm[h] = jnp.where(own, q_ref[...], extra)
        km[h] = jnp.where(own, k_ref[...], add_k)
        high, middle, low = split3(jnp.sum(jnp.where(own, both, 0.0), axis=1, keepdims=True))
        extra = jnp.where(ln == a, high, jnp.where(ln == a + 1, middle, jnp.where(ln == a + 2, low, zero)))
        dm[h] = jnp.where(own, do_ref[...], extra)
        vm[h] = jnp.where(own, v_ref[...], jnp.where((ln >= a) & (ln < a + 3), minus, zero))
    half_b = region((BLOCK, 128))
    ln_b = lanes((BLOCK, 128))
    ri = lax.broadcasted_iota(jnp.int32, (BLOCK, BLOCK), 0)
    ci = lax.broadcasted_iota(jnp.int32, (BLOCK, BLOCK), 1)
    dq_acc[...] = jnp.zeros(dq_acc.shape, f32)
    turned = [k_ref[BLOCK * j : BLOCK * (j + 1), :].T for j in range(blocks)]
    biases = []
    for j in range(blocks):
        here = slice(BLOCK * j, BLOCK * (j + 1))
        same = doc_col[here, :] == doc_row[:, here]
        seen = (ri == ci) | ((ri < ci) & (keep_col[here, :] > 0.5) & same)
        biases.append(jnp.where(seen, 0.0, NEG).astype(f32))

    def products(j, h):
        here, below = slice(BLOCK * j, BLOCK * (j + 1)), slice(BLOCK * (j + 1), length)
        a = (1 - h) * HEAD_DIM
        plain = jnp.where(half_b == h, k_ref[here, :], jnp.where((ln_b >= a + 3) & (ln_b < a + 6), minus, zero))
        got = [(here, dot(plain, qm[h, here, :], 1, 1), dot(vm[h, here, :], dm[h, here, :], 1, 1))]
        if j < blocks - 1:
            got.append((below, dot(km[h, here, :], qm[h, below, :], 1, 1), dot(vm[h, here, :], dm[h, below, :], 1, 1)))
        return got

    items = [(j, h) for j in range(blocks) for h in range(2)]
    ahead = products(*items[0])
    for n, (j, h) in enumerate(items):
        now, ahead = ahead, products(*items[n + 1]) if n + 1 < len(items) else None
        dk = dv = None
        for rows, s, dp in now:
            p = jnp.exp(s + biases[j] if rows.start == BLOCK * j else s)
            ds = (p * dp).astype(bf16)
            dk_part, dv_part = dot(ds, q_ref[rows, :]), dot(p.astype(bf16), do_ref[rows, :])
            dk, dv = (dk_part, dv_part) if dk is None else (dk + dk_part, dv + dv_part)
            dq_acc[h, :, rows] += dot(turned[j], ds)
        if h == 0:
            first = dk, dv
        else:
            here = slice(BLOCK * j, BLOCK * (j + 1))
            dk_ref[here, :] = jnp.where(half_b == 0, first[0], dk).astype(bf16)
            dv_ref[here, :] = jnp.where(half_b == 0, first[1], dv).astype(bf16)
    dq_ref[...] = (jnp.where(half == 0, dq_acc[0].T, dq_acc[1].T) * 0.125).astype(bf16)


def attend_back(t, lens, keep_parts, q, k, v, do_parts, o, log_norm, pair):
    length = q.shape[0]
    mine = pl.BlockSpec((length, 128), lambda i: (0, pair))
    mine_part = pl.BlockSpec((length // 4, 128), lambda i: (0, pair))
    return pl.pallas_call(
        functools.partial(attn_bwd_kernel, pair=pair),
        grid=(1,),
        out_shape=(sds((length, 128), bf16),) * 3,
        in_specs=[SMEM] * 2 + [VMEM] * 4 + [mine] * 3 + [mine_part] * 4 + [mine, VMEM],
        scratch_shapes=[pltpu.VMEM((2, length, 128), bf16)] * 4
        + [pltpu.VMEM((length, 128), bf16), pltpu.VMEM((2, 128, length), f32), pltpu.VMEM((128, length), f32)],
        compiler_params=params(60),
        cost_estimate=cost(0.1, 0.1),
        name="attend_back",
    )(t, lens, *keep_parts, q, k, v, *do_parts, o, log_norm)

def fetch_w_out(inward, t_ref, sources, target):
    started = [inward.start(w, target.at[u]) for u, w in enumerate(sources[:2])]
    half = target.shape[1] // 2
    few = half // INNER
    for u, (straight, blocks) in enumerate((sources[2:4], sources[4:6]), 2):
        started.append(inward.start(straight, target.at[u, :half, :]))
        for block in range(INNER):
            turn = t_ref[1] ^ block
            turn = (turn % 2) * 4 + turn // 2 % 2 * 2 + turn // 4
            rows = pl.ds(pl.multiple_of(turn * few, few), few)
            there = slice(half + block * few, half + (block + 1) * few)
            started.append(inward.start(blocks.at[rows, :], target.at[u, there, :]))
    return started


def send_pieces(outward, t_ref, pack, first, kept, given):
    half = pack.shape[0] // 2
    source, at = pack.at[pl.ds(first, 2)], pl.ds(first % half, 2)
    keep = t_ref[2] == first // half
    copies = outward.describe(source, kept.at[at]), outward.describe(source, given.at[at])
    pl.when(keep)(copies[0].start)
    pl.when(jnp.logical_not(keep))(copies[1].start)
    outward.add(copies[0])


def mlp_kernel(t_ref, gain_ref, o0, o1, o2, o3, w0, w1, w2, w3, w4, w5, *refs, order, last):
    (xa, xb), refs = refs[:2], refs[2:]
    dys, refs = refs[: 4 if last else 2], refs[4 if last else 2 :]
    (wg, wu, wd), refs = refs[:3], refs[3:]
    far, refs = refs[: 4 * last], refs[4 * last :]
    (fa, fb, ba, bb, b_low), refs = refs[:5], refs[5:]
    outs, refs = refs[:4], refs[4:]
    (o_s, w_s, x_s, y_s, wg_s, wu_s, wd_s, hn_s, act_s, dg_s, du_s, f_s, b_s), refs = refs[:13], refs[13:]
    (own_s, left, pack_s), refs = (refs[:3], refs[3:]) if last else ((None,) * 3, refs)
    inward, outward = Copies(refs[0]), Copies(refs[1])
    part = x_s.shape[1]
    hidden, width = wg_s.shape
    gain = gain_ref[...].astype(f32)
    slot = {k: i for i, k in enumerate(order)}
    blocks = {k: slice((k - min(order)) * part, (k - min(order) + 1) * part) for k in range(min(order), 4)}
    o_here = {}
    for k in order:
        rows = pl.ds(pl.multiple_of((t_ref[0] ^ k) % 2 * part, part), part)
        o_here[k] = [inward.start(o.at[rows, :], o_s.at[slot[k], u]) for u, o in enumerate((o0, o1, o2, o3))]
        o_here[k].append(inward.start((xa, xb)[slot[k]], x_s.at[slot[k]]))
        if slot[k] == 0:
            w_here = fetch_w_out(inward, t_ref, (w0, w1, w2, w3, w4, w5), w_s)
            rest = [inward.start(wg, wg_s), inward.start(wu, wu_s)]
    rest += [inward.start(dys[slot[k]], y_s.at[blocks[k], :]) for k in order]
    rest.append(inward.start(wd, wd_s))
    late = [inward.start(source, target.at[2 * part :, :]) for source, target in zip(far, (hn_s, act_s, dg_s, du_s))]
    late += [inward.start(dy, y_s.at[blocks[k], :]) for dy, k in zip(dys[2:], (3, 2))]
    totals, products = {}, {}

    def project_out(k):
        inward.wait(*o_here[k])
        totals[k] = x_s[slot[k]].astype(f32)
        for u in range(4):
            totals[k] = totals[k] + dot(o_s[slot[k], u], w_s[u])

    def norm(k):
        if k == 0:
            own_s[...] = totals[k]
            outward.start(own_s, outs[0])
        hn_s[blocks[k], :] = (totals[k] * rms_rows(totals[k]) * gain).astype(bf16)

    def forward(k):
        hn = hn_s[blocks[k], :]
        products[k] = (
            dot(hn, wg_s[...], 1, 1),
            dot(hn, wu_s[...], 1, 1),
            dot(y_s[blocks[k], :], wd_s[...], 1, 1).astype(bf16).astype(f32),
        )

    def activate(k):
        gate, up, dact = products[k]
        sig = 1.0 / (1.0 + jnp.exp(-gate))
        silu = gate * sig
        act_s[blocks[k], :] = (silu * up).astype(bf16)
        dg_s[blocks[k], :] = (dact * up * sig * (1.0 + gate * (1.0 - sig))).astype(bf16)
        du_s[blocks[k], :] = (dact * silu).astype(bf16)

    def backward(k):
        i = slot[k]
        b_s[i] = (dot(dg_s[blocks[k], :], wg_s[...]) + dot(du_s[blocks[k], :], wu_s[...])).astype(bf16)
        if k % 2:
            outward.start(b_s.at[i, : part // 2, :], ba)
            outward.start(b_s.at[i, part // 2 :, :], b_low)
        else:
            outward.start(b_s.at[i], (ba, bb)[i])
        f_s[i] = dot(act_s[blocks[k], :], wd_s[...]).astype(bf16)
        outward.start(f_s.at[i], (fa, fb)[i])
        if not last:
            for source, target in zip((hn_s, act_s, dg_s, du_s), outs):
                outward.start(source.at[blocks[k], :], target.at[blocks[k], :])

    one, two = order
    inward.wait(*w_here)
    project_out(one)
    project_out(two)
    inward.wait(*rest)
    norm(one)
    forward(one)
    norm(two)
    forward(two)
    activate(one)
    backward(one)
    activate(two)
    backward(two)
    if last:
        inward.wait(*late)
        for m, held, right in ((0, dg_s, hn_s), (1, du_s, hn_s), (2, act_s, y_s)):
            left[m % 2] = held[...].T
            for c in range(0, width, 256):
                cols = slice(c, c + 256)
                grad = dot(left[m % 2], right[:, cols])
                if m < 2:
                    sums = jnp.sum(grad * (wg_s, wu_s)[m][:, cols].astype(f32), axis=0, keepdims=True)
                    outs[3][:, cols] = sums if m == 0 else outs[3][:, cols] + sums
                grad = grad.astype(bf16)
                for b in range(2):
                    pack_s[c // 128 + b, m * hidden : (m + 1) * hidden, :] = grad[:, 128 * b : 128 * b + 128]
                if m == 2:
                    send_pieces(outward, t_ref, pack_s, c // 128, outs[1], outs[2])
    outward.wait()


def mlp(t, o_parts, w_parts, x_pair, dys, gain, wg, wu, wd, order, far=()):
    part, width = x_pair[0].shape
    hidden = wg.shape[0]
    last = bool(far)
    held = (4 if last else 2) * part
    block, half_block, inner = (sds(s, bf16) for s in ((part, width), (part // 2, width), (2 * part, hidden)))
    pack = (width // 128, 3 * hidden, 128)
    scratch = [
        ((2, 4, part, o_parts[0].shape[1]), bf16),
        ((4,) + w_parts[0].shape, bf16),
        ((2, part, width), bf16),
        ((held, width), bf16),
        *[((hidden, width), bf16)] * 3,
        ((held, width), bf16),
        *[((held, hidden), bf16)] * 3,
        ((2, part, width), bf16),
        ((2, part, width), bf16),
    ]
    if last:
        scratch += [((part, width), f32), ((2, hidden, held), bf16), (pack, bf16)]
        half = sds((pack[0] // 2,) + pack[1:], bf16)
        out = [sds((part, width), f32), half, half, sds((1, width), f32)]
    else:
        out = [sds((2 * part, width), bf16), inner, inner, inner]
    return pl.pallas_call(
        functools.partial(mlp_kernel, order=order, last=last),
        out_shape=(block, block, half_block, block, half_block, *out),
        in_specs=[SMEM, VMEM] + [ANY] * (15 + len(dys) + len(far)),
        out_specs=[ANY] * 8 + [VMEM if last else ANY],
        scratch_shapes=[pltpu.VMEM(*s) for s in scratch]
        + [pltpu.SemaphoreType.DMA((48,)), pltpu.SemaphoreType.DMA((16,))],
        compiler_params=params(61),
        cost_estimate=cost(25 if last else 14, 25),
        name="mlp",
    )(t, gain, *o_parts, *w_parts, *x_pair, *dys, wg, wu, wd, *far)


def unpack_kernel(head_idx, mlp_idx, *refs, head_shapes, mlp_shapes):
    heads, refs = refs[:INNER], refs[INNER:]
    strands, refs = refs[: 2 * INNER], refs[2 * INNER :]
    head_outs, refs = refs[: len(head_shapes)], refs[len(head_shapes) :]
    mlp_outs, refs = refs[: len(mlp_shapes)], refs[len(mlp_shapes) :]
    head_held, mlp_held, *stages, in_sems, out_sems = refs
    inward, outward = Copies(in_sems), Copies(out_sems)
    head_here = [[inward.start(piece, head_held.at[j])] for j, piece in enumerate(heads)]
    high = mlp_held.shape[1] // 2
    mlp_here = [
        [inward.start(strands[2 * j + s], mlp_held.at[j, high * s : high * (s + 1), :]) for s in range(2)]
        for j in range(INNER)
    ]
    for idx, held, here, shapes, outs, own in (
        (head_idx, head_held, head_here, head_shapes, head_outs, stages[: len(head_shapes)]),
        (mlp_idx, mlp_held, mlp_here, mlp_shapes, mlp_outs, stages[len(head_shapes) :]),
    ):
        for j in range(INNER):
            inward.wait(*here[j])
            at = pl.ds(pl.multiple_of(idx[j] * 128, 128), 128)
            top = 0
            for (rows, width), out, stage in zip(shapes, outs, own):
                whole = width == 128 * INNER
                for b in range(1 if whole else width // 128):
                    high_b = rows if whole else 128
                    stage[j, :, 128 * b : 128 * b + 128] = held[j, top : top + high_b, :].astype(f32)
                    top += high_b
                outward.start(stage.at[j], out.at[:, at] if whole else out.at[at, :])
    outward.wait()


def unpack(head_idx, heads, head_shapes, mlp_idx, strands, mlp_shapes):
    shapes = (*head_shapes, *mlp_shapes)
    stages = [(INNER, r, 128) if w == 128 * INNER else (INNER, 128, w) for r, w in shapes]
    return pl.pallas_call(
        functools.partial(unpack_kernel, head_shapes=head_shapes, mlp_shapes=mlp_shapes),
        out_shape=tuple(sds(s, f32) for s in shapes),
        in_specs=[SMEM] * 2 + [ANY] * (len(heads) + len(strands)),
        out_specs=[ANY] * len(shapes),
        scratch_shapes=[
            pltpu.VMEM((INNER, *heads[0].shape), bf16),
            pltpu.VMEM((INNER, 2 * strands[0].shape[0], 128), bf16),
            *[pltpu.VMEM(s, f32) for s in stages],
            pltpu.SemaphoreType.DMA((len(heads) + len(strands),)),
            pltpu.SemaphoreType.DMA((INNER * len(shapes),)),
        ],
        compiler_params=params(60),
        cost_estimate=cost(0.1, 0.1),
        name="unpack",
    )(head_idx, mlp_idx, *heads, *strands)


def gain_rows_kernel(idx, *refs):
    pieces, (out_ref, held, sems) = refs[:INNER], refs[INNER:]
    copies = Copies(sems)
    for j, piece in enumerate(pieces):
        copies.start(piece.at[piece.shape[0] - 16 :, :], held.at[j])
    copies.wait()
    for j in range(INNER):
        out_ref[:, pl.ds(pl.multiple_of(idx[j] * 128, 128), 128)] = held[j].astype(f32)


def gain_rows(idx, pieces):
    return pl.pallas_call(
        gain_rows_kernel,
        out_shape=sds((16, 128 * INNER), f32),
        in_specs=[SMEM] + [ANY] * INNER,
        out_specs=VMEM,
        scratch_shapes=[pltpu.VMEM((INNER, 16, 128), bf16), pltpu.SemaphoreType.DMA((INNER,))],
        compiler_params=params(60),
        cost_estimate=cost(0.1, 0.1),
        name="gain_rows",
    )(idx, *pieces)


def hidden_back_kernel(
    t_ref, gain_ref, b0, b1, b2, b3, h_ref, dy_ref, w0, w1, w2, w3, w4, w5, dh_ref, da_ref, d0, d1, d2, d3,
    b_s, h_s, dy_s, w_s, dh_s, da_s, d_s, in_sems, out_sems,
):
    inward, outward = Copies(in_sems), Copies(out_sems)
    part = dh_s.shape[0]
    halves = [slice(0, part // 2), slice(part // 2, part)]
    here = [inward.start(b, b_s.at[i]) for i, b in ((0, b0), (2, b3))]
    here += [inward.start(b, b_s.at[1, rows, :]) for b, rows in zip((b1, b2), halves)]
    here += [inward.start(h_ref, h_s), inward.start(dy_ref, dy_s)]
    w_here = fetch_w_out(inward, t_ref, (w0, w1, w2, w3, w4, w5), w_s)
    inward.wait(*here)
    for rows in halves:
        dhn = b_s[0, rows, :].astype(f32) + b_s[1, rows, :].astype(f32) + b_s[2, rows, :].astype(f32)
        hidden = h_s[rows, :]
        inv = rms_rows(hidden)
        weighted = dhn * gain_ref[...].astype(f32)
        inner = jnp.mean(weighted * hidden, axis=-1, keepdims=True)
        dh = dy_s[rows, :].astype(f32) + inv * weighted - hidden * (inv * inv * inv) * inner
        dh_s[rows, :] = dh
        da_s[rows, :] = dh.astype(bf16)
        if rows.start == 0:
            inward.wait(*w_here)
        for u in (2, 3, 1, 0):
            d_s[u, rows, :] = dot(da_s[rows, :], w_s[u], 1, 1).astype(bf16)
    for u, d in ((2, d2), (3, d3), (1, d1), (0, d0)):
        outward.start(d_s.at[u], d)
    outward.start(dh_s, dh_ref)
    outward.start(da_s, da_ref)
    outward.wait()


def hidden_back(t, sums, h_own, dy_own, gain, w_parts):
    part, width = h_own.shape
    cols = w_parts[0].shape[0]
    scratch = [
        ((3, part, width), bf16), ((part, width), f32), ((part, width), bf16), ((4, cols, width), bf16),
        ((part, width), f32), ((part, width), bf16), ((4, part, cols), bf16),
    ]
    return pl.pallas_call(
        hidden_back_kernel,
        out_shape=(sds((part, width), f32), sds((part, width), bf16)) + (sds((part, cols), bf16),) * 4,
        in_specs=[SMEM, VMEM] + [ANY] * 12,
        out_specs=[ANY] * 6,
        scratch_shapes=[pltpu.VMEM(*s) for s in scratch]
        + [pltpu.SemaphoreType.DMA((6 + 4 + 2 * INNER,)), pltpu.SemaphoreType.DMA((6,))],
        compiler_params=params(60),
        cost_estimate=cost(60, 10),
        name="hidden_back",
    )(t, gain, *sums, h_own, dy_own, *w_parts)


def tokens_back_kernel(
    t_ref, dq0, dq1, dk0, dk1, dv0, dv1, wq, wk, wv, b0, b1, b2, b3, d_s, w_s, b_s, in_sems, out_sems
):
    inward, outward = Copies(in_sems), Copies(out_sems)
    part = b_s.shape[1]
    for m, pair in enumerate(((dq0, dq1), (dk0, dk1), (dv0, dv1))):
        for b, d in enumerate(pair):
            inward.start(d, d_s.at[m, :, 128 * b : 128 * b + 128])
    for m, w in enumerate((wq, wk, wv)):
        inward.start(w, w_s.at[m])
    inward.wait()
    for k, out in ((3, b3), (2, b2), (1, b1), (0, b0)):
        rows = part_rows(t_ref, k, part)
        b_s[k] = sum(dot(d_s[m, rows, :], w_s[m], 1, 1) for m in range(3)).astype(bf16)
        outward.start(b_s.at[k], out)
    outward.wait()


def tokens_back(t, head_parts, wq, wk, wv):
    length, (width, cols) = head_parts[0].shape[0], wq.shape
    scratch = [(3, length, cols), (3, width, cols), (4, length // 4, width)]
    return pl.pallas_call(
        tokens_back_kernel,
        out_shape=(sds((length // 4, width), bf16),) * 4,
        in_specs=[SMEM] + [ANY] * 9,
        out_specs=[ANY] * 4,
        scratch_shapes=[pltpu.VMEM(s, bf16) for s in scratch]
        + [pltpu.SemaphoreType.DMA((9,)), pltpu.SemaphoreType.DMA((4,))],
        compiler_params=params(60),
        cost_estimate=cost(0.1, 0.1),
        name="tokens_back",
    )(t, *head_parts, wq, wk, wv)


def head_grads_kernel(
    t_ref, other_ref, xn_ref, o_ref, a0, a1, a2, a3, dq0, dq1, dk0, dk1, dv0, dv1, wq, wk, wv, out_ref,
    xn_s, o_s, a_s, d_s, w_s, left, left_o, pack_s, in_sems, out_sems,
):
    length, width = xn_s.shape
    part = length // 4
    cols = o_s.shape[1]
    inward, outward = Copies(in_sems), Copies(out_sems)
    halves = [slice(0, width // 2), slice(width // 2, width)]
    xn_here = [inward.start(xn_ref.at[:, halves[0]], xn_s.at[:, halves[0]])]
    here = [
        inward.start(d, d_s.at[m, :, 128 * b : 128 * b + 128])
        for m, pair in enumerate(((dq0, dq1), (dk0, dk1), (dv0, dv1)))
        for b, d in enumerate(pair)
    ]
    here += [inward.start(w, w_s.at[m]) for m, w in enumerate((wq, wk, wv))]
    xn_here.append(inward.start(xn_ref.at[:, halves[1]], xn_s.at[:, halves[1]]))
    o_here = [inward.start(o_ref, o_s)]
    o_here += [inward.start(a, a_s.at[part_rows(t_ref, k, part), :]) for k, a in enumerate((a0, a1, a2, a3))]
    for i, rows in enumerate(halves):
        inward.wait(xn_here[i])
        left[rows, :] = xn_s[:, rows].T
        if i == 0:
            inward.wait(*here)
        by_row = jnp.zeros((width // 2, cols), f32)
        for m in range(3):
            grad = dot(left[rows, :], d_s[m])
            by_row = by_row + grad * w_s[m, rows, :].astype(f32)
            for piece in range(width // 256):
                for b in range(cols // 128):
                    at = m * cols + 128 * b
                    pack_s[rows.start // 128 + piece, at : at + 128, :] = grad[
                        128 * piece : 128 * piece + 128, 128 * b : 128 * b + 128
                    ].astype(bf16)
        sums = lax.dot_general(
            jnp.ones((8, cols), f32), by_row, (((1,), (1,)), ((), ())),
            precision=lax.Precision.HIGHEST, preferred_element_type=f32,
        )
        for piece in range(width // 256):
            at = rows.start // 128 + piece
            others = jnp.broadcast_to(other_ref[:, 128 * at : 128 * at + 128], (8, 128))
            both = jnp.concatenate([sums[:, 128 * piece : 128 * piece + 128], others], axis=0)
            pack_s[at, 4 * cols :, :] = both.astype(bf16)
    inward.wait(*o_here)
    left_o[...] = o_s[...].T
    for c in range(0, width, 256):
        grad = dot(left_o[...], a_s[:, c : c + 256]).astype(bf16)
        for b in range(2):
            pack_s[c // 128 + b, 3 * cols : 4 * cols, :] = grad[:, 128 * b : 128 * b + 128]
        two = pl.ds(c // 128, 2)
        outward.start(pack_s.at[two], out_ref.at[two])
    outward.wait()


def head_grads(t, other_gain, xn, o, da_parts, head_parts, wq, wk, wv):
    length, width = xn.shape
    cols = o.shape[1]
    scratch = [
        (length, width), (length, cols), (length, width), (3, length, cols), (3, width, cols),
        (width, length), (cols, length), (width // 128, 4 * cols + 16, 128),
    ]
    return pl.pallas_call(
        head_grads_kernel,
        out_shape=sds((width // 128, 4 * cols + 16, 128), bf16),
        in_specs=[SMEM, VMEM] + [ANY] * 15,
        out_specs=ANY,
        scratch_shapes=[pltpu.VMEM(s, bf16) for s in scratch]
        + [pltpu.SemaphoreType.DMA((16,)), pltpu.SemaphoreType.DMA((4,))],
        compiler_params=params(60),
        cost_estimate=cost(0.1, 0.1),
        name="head_grads",
    )(t, other_gain, xn, o, *da_parts, *head_parts, wq, wk, wv)


def add_kernel(*refs, count):
    terms, out_ref, held, out_s, sems = refs[:count], refs[count], refs[count + 1 : -2], refs[-2], refs[-1]
    copies = Copies(sems)
    for term, target in zip(terms, held):
        copies.start(term, target)
    copies.wait()
    out_s[...] = sum(target[...].astype(f32) for target in held).astype(bf16)
    copies.start(out_s, out_ref)
    copies.wait()


def add(*terms):
    shape = terms[0].shape
    return pl.pallas_call(
        functools.partial(add_kernel, count=len(terms)),
        out_shape=sds(shape, bf16),
        in_specs=[ANY] * len(terms),
        out_specs=ANY,
        scratch_shapes=[pltpu.VMEM(shape, term.dtype) for term in terms]
        + [pltpu.VMEM(shape, bf16), pltpu.SemaphoreType.DMA((len(terms) + 1,))],
        compiler_params=params(60),
        cost_estimate=cost(0.1, 0.1),
        name="add",
    )(*terms)


def tokens_end_kernel(gain_ref, d0, d1, d2, dh_ref, x_ref, out_ref, d_s, dh_s, x_s, out_s, sems):
    copies = Copies(sems)
    for i, d in enumerate((d0, d1, d2)):
        copies.start(d, d_s.at[i])
    copies.start(dh_ref, dh_s)
    copies.start(x_ref, x_s)
    copies.wait()
    x = x_s[...].astype(f32)
    inv = rms_rows(x)
    weighted = (d_s[0].astype(f32) + d_s[1].astype(f32) + d_s[2].astype(f32)) * gain_ref[...].astype(f32)
    inner = jnp.mean(weighted * x, axis=-1, keepdims=True)
    out_s[...] = (dh_s[...] + inv * weighted - x * (inv * inv * inv) * inner).astype(bf16)
    copies.start(out_s, out_ref)
    copies.wait()


def tokens_end(gain, terms, dh, x):
    shape = x.shape
    return pl.pallas_call(
        tokens_end_kernel,
        out_shape=sds(shape, bf16),
        in_specs=[VMEM] + [ANY] * 5,
        out_specs=ANY,
        scratch_shapes=[
            pltpu.VMEM((3, *shape), bf16), pltpu.VMEM(shape, f32), pltpu.VMEM(shape, bf16), pltpu.VMEM(shape, bf16),
            pltpu.SemaphoreType.DMA((6,)),
        ],
        compiler_params=params(60),
        cost_estimate=cost(0.1, 0.1),
        name="tokens_end",
    )(gain, *terms, dh, x)


def swap(value, k):
    return lax.ppermute(value, "tensor", [(i, i ^ k) for i in range(4)])


def spread(own):
    far = swap(own, 2)
    return own, swap(own, 1), far, swap(far, 1)


def double(value, bit, dp):
    return jnp.concatenate([value, lax.ppermute(value, "dp", [(i, i ^ bit) for i in range(dp)])], axis=0)


class Ring:
    order = (0, 2, 4, 6, 7, 5, 3, 1)

    def __init__(self, dp):
        self.dp = dp
        self.member, self.core = lax.axis_index("dp") % INNER, lax.axis_index("tensor") % 2
        self.way = 1 - 2 * self.core
        self.place = jnp.where(self.member % 2 == 0, self.member // 2, INNER - 1 - self.member // 2)

    def side(self, step):
        return self.member >> ((step + self.core) % 3) & 1

    def send(self, value, target):
        pairs = [
            (4 * (g + d) + t, 4 * (g + target(d, t % 2)) + t)
            for g in range(0, self.dp, INNER)
            for d in range(INNER)
            for t in range(4)
        ]
        return lax.ppermute(value, ("dp", "tensor"), pairs)

    def pass_on(self, value):
        return self.send(value, lambda d, c: self.order[(self.order.index(d) + 1 - 2 * c) % INNER])


def rounded_sum(one, two):
    return (one.astype(f32) + two.astype(f32)).astype(bf16)


class Sum:
    def __init__(self, ring, strands):
        self.ring, self.step = ring, 0
        self.pieces = [[] for _ in range(strands)]

    def advance(self, *before):
        ring, strands = self.ring, len(self.pieces)
        self.step += 1
        arrived = pin(self.on_way.pop(0), *before)
        if self.step < self.adds:
            return self.next_add(arrived)
        if self.step == self.adds:
            arrived = rounded_sum(arrived, self.mine)
        if self.step == self.adds:
            arrived = arrived.reshape(arrived.shape[-2:])
            if ring.dp > INNER:
                groups = [[g + d for g in range(0, ring.dp, INNER)] for d in range(INNER)]
                arrived = lax.psum(arrived, "dp", axis_index_groups=groups)
            rows = arrived.shape[0] // strands
            for s, held in enumerate(self.pieces):
                held.append(arrived[s * rows : (s + 1) * rows])
                self.on_way.append(ring.pass_on(held[0]))
        else:
            held = self.pieces[(self.step - self.adds - 1) % strands]
            held.append(arrived)
            if len(held) < INNER:
                self.on_way.append(ring.pass_on(arrived))
        return arrived

    @property
    def done(self):
        return not self.on_way

    def result(self):
        return [piece for arrived in zip(*self.pieces) for piece in arrived]


class RingSum(Sum):
    adds = INNER - 1

    def __init__(self, ring, packed, strands):
        super().__init__(ring, strands)
        self.packed = packed
        self.on_way = [ring.pass_on(self.piece(0))]
        self.mine = self.piece(1)

    def piece(self, step):
        number = (self.ring.place - step * self.ring.way) % INNER
        return lax.dynamic_index_in_dim(self.packed, number, 0, keepdims=False)

    def next_add(self, arrived):
        arrived = rounded_sum(arrived, self.mine)
        self.on_way = [self.ring.pass_on(arrived)]
        self.mine = self.piece(self.step + 1)
        return arrived

    def numbers(self):
        steps = lax.iota(jnp.int32, INNER) + INNER - 1
        return (self.ring.place - steps * self.ring.way) % INNER


class HalvingSum(Sum):
    adds = 3

    def __init__(self, ring, kept, given, strands):
        super().__init__(ring, strands)
        self.mine, self.on_way = kept, [self.give(given)]

    def give(self, value):
        step = self.step
        return self.ring.send(value, lambda d, c: d ^ 1 << (step + c) % 3)

    def next_add(self, arrived):
        side = self.ring.side(self.step)
        given, kept = [
            rounded_sum(*[
                lax.dynamic_index_in_dim(part.reshape(2, -1, *part.shape[-2:]), half, 0, keepdims=False)
                for part in (arrived, self.mine)
            ])
            for half in (1 - side, side)
        ]
        self.mine, self.on_way = kept, [self.give(given)]
        return given

    def numbers(self):
        ring = self.ring
        places = (ring.place - lax.iota(jnp.int32, INNER) * ring.way) % INNER
        members = jnp.where(places < INNER // 2, 2 * places, 2 * INNER - 1 - 2 * places)
        return sum((members >> ((step + ring.core) % 3) & 1) << (2 - step) for step in range(3))


def pin(value, *before):
    return lax.optimization_barrier((value, *before))[0]


def per_device(
    dp, tokens, gain_attn, w_query, w_key, w_value, w_out, gain_mlp, w_gate, w_up, w_down, doc_lens, pad_mask, cotangent
):
    ring = Ring(dp)
    t = jnp.stack([lax.axis_index("tensor"), ring.member, ring.side(0)]).astype(jnp.int32)
    width, hidden = w_gate.shape
    cols = w_query.shape[1]
    gain_one = gain_attn.reshape(1, width)
    gain_two = gain_mlp.reshape(1, width)
    gate_t, up_t = w_gate.T, w_up.T

    half = w_out.shape[0] // 2
    few = half // INNER
    w_share = lax.dynamic_slice_in_dim(w_out, half + ring.member * few, few, 0)
    w_half = w_out[:half]
    keep_parts = spread(pin(pad_mask.reshape(1, -1), gain_one, gain_two, t, w_share, w_half))
    w_first, w_straight = swap(w_share, 2), swap(w_half, 2)
    x_far = pin(swap(tokens, 2), keep_parts[2])
    x_parts = tokens, swap(tokens, 1), x_far, swap(x_far, 1)
    dy_parts = spread(cotangent)

    xn, q, k, v, o, log_norm, o_near, o_away = attend(t, doc_lens, gain_one, keep_parts, x_parts, w_query, w_key, w_value)
    dy_parts = spread(cotangent)
    near, away = spread(pin(o_near, dy_parts[2], w_first, w_straight)), spread(o_away)
    w_far = pin(w_first, o_near)
    for bit in (4, 2, 1):
        w_far = double(w_far, bit, dp)
    w_parts = w_out, swap(w_out, 1), w_straight, w_far, swap(w_straight, 1), swap(w_far, 1)

    weights = gain_two, gate_t, up_t, w_down
    f3, f2, b3_high, b2, b3_low, *far = mlp(
        t, (*away[:2], *near[2:]), w_parts, (x_parts[3], x_parts[2]), (dy_parts[3], dy_parts[2]), *weights, (3, 2)
    )
    passed = rounded_sum(b2, jnp.concatenate([swap(b3_high, 1), swap(b3_low, 1)], axis=0))
    f1, f0, b1_high, b0, b1_low, h_own, kept, given, gain_two_sum = mlp(
        t, (*near[:2], *away[2:]), w_parts, (x_parts[1], pin(x_parts[0], passed)), dy_parts[1::-1] + dy_parts[:1:-1], *weights, (1, 0), far
    )
    sum_mlp = HalvingSum(ring, kept, given, 2)
    sums = (b0, swap(b1_high, 1), swap(b1_low, 1), swap(passed, 2))
    dh, da, *do_parts = hidden_back(t, sums, h_own, cotangent, gain_two, w_parts)
    do_parts = [do_parts[0]] + [swap(do_parts[i], i) for i in range(1, 4)]
    ffn_passed = add(f2, swap(f3, 1))
    da_far = swap(pin(da, do_parts[2], do_parts[3], ffn_passed), 2)
    pairs = [attend_back(t, doc_lens, keep_parts, q, k, v, do_parts, o, log_norm, 0)]
    step = sum_mlp.advance(pairs[0][0])
    pairs.append(attend_back(t, doc_lens, keep_parts, pin(q, step), k, v, do_parts, o, log_norm, 1))
    da_far = pin(da_far, pairs[1][0])
    da_parts = da, swap(da, 1), da_far, swap(da_far, 1)
    head_parts = [pairs[p][m] for m in range(3) for p in range(2)]
    ffn_terms = f0, swap(f1, 1), swap(pin(ffn_passed, da_far), 2)
    packed = head_grads(t, gain_two_sum, xn, o, da_parts, head_parts, w_query, w_key, w_value)
    sum_head = RingSum(ring, packed, 1)
    step = sum_mlp.advance(packed)

    def back(step):
        out["dx"] = tokens_back(t, [pin(head_parts[0], step), *head_parts[1:]], w_query, w_key, w_value)
        out["across"] = swap(out["dx"][3], 1)
        return out["dx"][0]

    def pass_on(step):
        dx = out["dx"]
        passed = add(pin(dx[2], step), out["across"])
        out["dxn"] = dx[0], swap(dx[1], 1), swap(passed, 2)
        return passed

    def finish_output(step):
        out["y"] = add(h_own, *[pin(term, step) for term in ffn_terms])
        return out["y"]

    def finish_tokens(step):
        out["dx"] = tokens_end(gain_one, [pin(term, step) for term in out["dxn"]], dh, tokens)
        return out["dx"]

    out = {}
    tasks = [back, pass_on, finish_output, *[None] * 4, finish_tokens]
    while not (sum_mlp.done and sum_head.done):
        if not sum_head.done:
            step = sum_head.advance(step)
        for _ in range(2 if sum_head.step >= 4 and sum_head.step % 2 == 0 else 1):
            if not sum_mlp.done and sum_head.step != 1:
                step = sum_mlp.advance(step)
        if tasks:
            task = tasks.pop(0)
            step = task(step) if task else step
    gains = gain_rows(sum_head.numbers(), sum_head.result())
    first, *others = sum_mlp.result()
    grad_query, grad_key, grad_value, grad_out, grad_gate, grad_up, grad_down = unpack(
        sum_head.numbers(), sum_head.result(), ((width, cols),) * 3 + ((cols, width),),
        sum_mlp.numbers(), [pin(first, gains), *others], ((hidden, width),) * 3,
    )
    others = [pin(swap(gains, k), grad_gate) for k in range(1, 4)]
    gains = (gains + others[0]) + (others[1] + others[2])
    output, grad_tokens = out["y"], out["dx"]
    grad_gain_attn, grad_gain_mlp = gains[0] / gain_attn.astype(f32), gains[8] / gain_mlp.astype(f32)
    return (
        output, grad_tokens, grad_gain_attn, grad_query, grad_key, grad_value, grad_out, grad_gain_mlp,
        grad_gate.T, grad_up.T, grad_down,
    )


def solution(mesh):
    rows = P(("dp", "tensor"), None)
    columns = P(None, "tensor")
    shares = P("tensor", None)
    return jax.shard_map(
        functools.partial(per_device, mesh.shape["dp"]),
        mesh=mesh,
        in_specs=(
            rows, P(), columns, columns, columns, shares, P(), columns, columns, shares,
            P("dp", None), P(("dp", "tensor")), rows,
        ),
        out_specs=(rows, rows, P(), columns, columns, columns, shares, P(), columns, columns, shares),
        check_vma=False,
    )
```
